128 devices in a mesh: ta: 8 (over y, core), gx: 16 (over z, x).
Axes of the slice: x: 4, y: 4, z: 4, core: 2. Of those that a mesh axis runs over, the one named last changes fastest.
Arguments:
- gauge_links: float32 [4, 2, 3, 3, 16, 64, 256], P(None, None, None, None, 'ta', 'gx'), may hold values from -1 to 1, as said below
Outputs:
- rotated: float32 [4, 2, 3, 3, 16, 64, 256], P(None, None, None, None, 'ta', 'gx')
The draws below stay inside these ranges and needn't reach their ends.
Inputs may be any that keep to these rules, and one draw needn't show every extreme that they name: `gauge_links`: every link is a special unitary 3 x 3 matrix.
All inputs are finite; a program needn't handle non-finite values.
Results may differ from the reference program's by a relative error of at most 0.0003.
Values sent between devices are 32-bit elements; how exact they have to be, the bound alone decides.
A program may use at most 64 MiB of HBM per device.

```python
import math
import jax
import jax.numpy as jnp
from jax import lax

NY = 16
NZ = 16
NEWTON = 5
NT = 16
NX = 64


def embed_rotation(key, first, second, base_shape):
    key_alpha, key_beta, key_theta = jax.random.split(key, 3)
    alpha = jax.random.uniform(key_alpha, base_shape, jnp.float32, -math.pi, math.pi)
    beta = jax.random.uniform(key_beta, base_shape, jnp.float32, -math.pi, math.pi)
    theta = jax.random.uniform(key_theta, base_shape, jnp.float32, 0.0, 0.5 * math.pi)
    zeros = jnp.zeros(base_shape, jnp.float32)
    ones = jnp.ones(base_shape, jnp.float32)
    real_rows = [[ones if row == col else zeros for col in range(3)] for row in range(3)]
    imag_rows = [[zeros for col in range(3)] for row in range(3)]
    cos_t = jnp.cos(theta)
    sin_t = jnp.sin(theta)
    real_rows[first][first] = jnp.cos(alpha) * cos_t
    imag_rows[first][first] = jnp.sin(alpha) * cos_t
    real_rows[first][second] = jnp.cos(beta) * sin_t
    imag_rows[first][second] = jnp.sin(beta) * sin_t
    real_rows[second][first] = -jnp.cos(beta) * sin_t
    imag_rows[second][first] = jnp.sin(beta) * sin_t
    real_rows[second][second] = jnp.cos(alpha) * cos_t
    imag_rows[second][second] = -jnp.sin(alpha) * cos_t
    return (real_rows, imag_rows)


def multiply_lists(left_pair, right_pair):
    left_re, left_im = left_pair
    right_re, right_im = right_pair
    out_re = [[None] * 3 for row in range(3)]
    out_im = [[None] * 3 for row in range(3)]
    for row in range(3):
        for col in range(3):
            acc_re = left_re[row][0] * right_re[0][col] - left_im[row][0] * right_im[0][col]
            acc_im = left_re[row][0] * right_im[0][col] + left_im[row][0] * right_re[0][col]
            for inner in (1, 2):
                acc_re = acc_re + left_re[row][inner] * right_re[inner][col] - left_im[row][inner] * right_im[inner][col]
                acc_im = acc_im + left_re[row][inner] * right_im[inner][col] + left_im[row][inner] * right_re[inner][col]
            out_re[row][col] = acc_re
            out_im[row][col] = acc_im
    return (out_re, out_im)


def draw_gauge_links(key, part):
    base_shape = (4, NT, NX, NY * NZ)
    key_one, key_two, key_three = jax.random.split(jax.random.fold_in(key, 17), 3)
    first_rot = embed_rotation(key_one, 0, 1, base_shape)
    second_rot = embed_rotation(key_two, 1, 2, base_shape)
    third_rot = embed_rotation(key_three, 0, 2, base_shape)
    whole_re, whole_im = multiply_lists(multiply_lists(first_rot, second_rot), third_rot)
    real_all = jnp.stack([jnp.stack(whole_re[row], 1) for row in range(3)], 1)
    imag_all = jnp.stack([jnp.stack(whole_im[row], 1) for row in range(3)], 1)
    return jnp.stack([real_all, imag_all], axis=1)


def setup_inputs(seed: int = 0) -> dict:
    arg_keys = jax.random.split(jax.random.key(seed), 2)
    return {
        "gauge_links": draw_gauge_links(jax.random.fold_in(arg_keys[1], 71), 0),
    }


ape_weight = 0.4

def matmul_pair(left_mat, right_mat):
    real_part = left_mat[0][:, 0, None] * right_mat[0][None, 0] - left_mat[1][:, 0, None] * right_mat[1][None, 0]
    imag_part = left_mat[0][:, 0, None] * right_mat[1][None, 0] + left_mat[1][:, 0, None] * right_mat[0][None, 0]
    for column in (1, 2):
        real_part = real_part + left_mat[0][:, column, None] * right_mat[0][None, column] - left_mat[1][:, column, None] * right_mat[1][None, column]
        imag_part = imag_part + left_mat[0][:, column, None] * right_mat[1][None, column] + left_mat[1][:, column, None] * right_mat[0][None, column]
    return jnp.stack([real_part, imag_part])

def dagger_of(matrix):
    return jnp.stack([jnp.swapaxes(matrix[0], 0, 1), -jnp.swapaxes(matrix[1], 0, 1)])

def identity_like(template):
    tail = template.shape[3:]
    real_part = jnp.broadcast_to(jnp.eye(3, dtype=jnp.float32).reshape((3, 3) + (1,) * len(tail)), (3, 3) + tail)
    return jnp.stack([real_part, jnp.zeros_like(real_part)])

def yz_roll(source, shift_y, shift_z):
    if shift_y == 0 and shift_z == 0:
        return source
    dims_now = source.shape
    plane = source.reshape(dims_now[:-1] + (NY, NZ))
    plane = jnp.roll(plane, (-shift_y, -shift_z), axis=(-2, -1))
    return plane.reshape(dims_now)

def shifted(source, offset):
    moved_part = jnp.roll(source, (-offset[0], -offset[1]), axis=(-3, -2))
    return yz_roll(moved_part, offset[2], offset[3])

def unit_offset(direction):
    return tuple((1 if axis_pos == direction else 0 for axis_pos in range(4)))

def unitarise(blended):
    three_eye = 3.0 * identity_like(blended)
    frobenius = jnp.sqrt(lax.optimization_barrier(jnp.sum(blended * blended, axis=(0, 1, 2))))
    current = blended / jnp.maximum(frobenius, 1.0)
    for repeat in range(NEWTON):
        current = 0.5 * matmul_pair(current, three_eye - matmul_pair(dagger_of(current), current))
    return current

def smear(gauge_links, mover):
    result = []
    anchor = (0, 0, 0, 0)
    for direction in range(4):
        step_dir = unit_offset(direction)
        staple_sum = None
        for other in range(4):
            if other == direction:
                continue
            step_other = unit_offset(other)
            back_other = tuple((-value for value in step_other))
            diagonal_step = tuple((first - second for first, second in zip(step_dir, step_other)))
            upper_path = matmul_pair(matmul_pair(mover(gauge_links[other], anchor), mover(gauge_links[direction], step_other)), dagger_of(mover(gauge_links[other], step_dir)))
            lower_path = matmul_pair(matmul_pair(dagger_of(mover(gauge_links[other], back_other)), mover(gauge_links[direction], back_other)), mover(gauge_links[other], diagonal_step))
            if staple_sum is None:
                staple_sum = upper_path + lower_path
            else:
                staple_sum = staple_sum + upper_path + lower_path
        blended = (1.0 - ape_weight) * mover(gauge_links[direction], anchor) + ape_weight / 6.0 * staple_sum
        result.append(unitarise(blended))
    return jnp.stack(result)

def chain_step(carry_mat, link_now):
    return (matmul_pair(carry_mat, link_now), carry_mat)

def reference(gauge_links):
    current = gauge_links
    for repeat in range(2):
        current = smear(current, shifted)
    temporal = jnp.moveaxis(current[0], 3, 0)
    start = identity_like(temporal[0])
    final, before = lax.scan(chain_step, start, temporal)
    rotation = jnp.moveaxis(before, 0, 3)
    after_rot = jnp.moveaxis(jnp.concatenate([before[1:], final[None]], 0), 0, 3)
    neighbours = [after_rot, jnp.roll(rotation, -1, axis=-2), yz_roll(rotation, 1, 0), yz_roll(rotation, 0, 1)]
    result = []
    for direction in range(4):
        result.append(matmul_pair(matmul_pair(rotation, current[direction]), dagger_of(neighbours[direction])))
    return jnp.stack(result)
```

```python
import functools

import jax
import jax.numpy as jnp
from jax import lax
from jax.experimental import pallas as pl
from jax.experimental.pallas import tpu as pltpu
from jax.sharding import PartitionSpec as P

MESH = pl.DeviceIdType.MESH
NZ = 16
NEWTON = 5
ape_weight = 0.4
LANES = 128


def mm(a, b, da=False, db=False):
    def left(c):
        return tuple(q[c, :, None] if da else q[:, c, None] for q in a)

    def right(c):
        return tuple(q[None, :, c] if db else q[None, c] for q in b)

    re = im = None
    for c in range(3):
        lr, li = left(c)
        rr, ri = right(c)
        x, y = lr * rr, li * ri
        u, v = lr * ri, li * rr
        re = x if re is None else re + x
        re = re + y if da != db else re - y
        if im is None:
            if da and db:
                im = -u - v
            elif da:
                im = u - v
            elif db:
                im = v - u
            else:
                im = u + v
        else:
            im = im - u if db else im + u
            im = im - v if da else im + v
    return re, im


def lane_of(shape):
    return lax.broadcasted_iota(jnp.int32, shape, len(shape) - 1)


def each(f, pair):
    return tuple(f(q) for q in pair)


def sroll(v, shift):
    shift = shift % 8
    if shift == 0:
        return v
    flat = v.reshape((9, 8, LANES))
    return pltpu.roll(flat, shift, 1).reshape(v.shape)


def lroll(v, shift):
    return pltpu.roll(v.reshape((72, LANES)), shift % LANES, 1).reshape(v.shape)


def yz_shift(pair, m, sign):
    lane = lane_of((3, 3, 8, LANES))
    z = lax.rem(lane, NZ)
    if isinstance(m, int):
        if m == 2:

            def move(v):
                r = lroll(v, -NZ * sign)
                stay = lane < LANES - NZ if sign > 0 else lane >= NZ
                return jnp.where(stay, r, sroll(r, 4))

        else:

            def move(v):
                stay = z < NZ - 1 if sign > 0 else z >= 1
                return jnp.where(stay, lroll(v, -sign), lroll(v, sign * (NZ - 1)))

        return each(move, pair)
    raise NotImplementedError


def kernel(x_ref, o_ref, U, XH, CH, PK0, PK3, acc, Q, R1, R2, GH, OUT, hs, hr, cs, cr, ds, dr, io):
    ta = lax.axis_index("ta")
    gx = lax.axis_index("gx")
    nta = lax.axis_size("ta")
    ngx = lax.axis_size("gx")

    def dev(dt, dg):
        return {"ta": lax.rem(ta + dt + nta, nta), "gx": lax.rem(gx + dg + ngx, ngx)}

    edge = (ta == 0) | (ta == 4)

    barrier = pltpu.get_barrier_semaphore()
    greeted = [dev(0, 1), dev(0, -1), dev(-1, 1), dev(1, -1)] + [dev(k, 0) for k in range(1, 8)]
    for d in greeted:
        pl.semaphore_signal(barrier, inc=1, device_id=d, device_id_type=MESH)
    for row in (0, 4):
        d = {"ta": row, "gx": lax.rem(gx + 1, ngx)}
        pl.semaphore_signal(barrier, inc=1, device_id=d, device_id_type=MESH)

    loads = []
    for t in range(2):
        for h in range(2):
            c = pltpu.make_async_copy(
                x_ref.at[:, :, :, :, t, :, pl.ds(h * LANES, LANES)],
                U.at[0, 1 + t, :, :, :, :, pl.ds(4 * h, 4), :],
                io.at[2 * t + h],
            )
            c.start()
            loads.append(c)

    def ld(ref, *at):
        v = ref[at]
        return v[0], v[1]

    def add(m, s, pair):
        acc[m, s, 0] = acc[m, s, 0] + pair[0]
        acc[m, s, 1] = acc[m, s, 1] + pair[1]

    row4 = lax.rem(lax.broadcasted_iota(jnp.int32, (3, 3, 8, LANES), 2), 4)

    def pack(w, m):
        parts = [U[w, 1, m, 0], U[w, 2, m, 0], U[w, 1, m, 1], U[w, 2, m, 1]]
        for col, out in ((0, PK0), (3, PK3)):
            moved = [sroll(v, q - col) for q, v in enumerate(parts)]
            out[w, m] = jnp.where(
                row4 < 2,
                jnp.where(row4 == 0, moved[0], moved[1]),
                jnp.where(row4 == 2, moved[2], moved[3]),
            )

    def x_next(pair, halo, t):
        return tuple(
            jnp.where(row4 == 3, sroll(halo, 3 - t - 2 * q), sroll(v, -1))
            for q, v in enumerate(pair)
        )

    def x_prev(pair, column, t):
        return tuple(
            jnp.where(row4 == 0, sroll(c, -t), sroll(v, 1)) for v, c in zip(pair, column)
        )

    def unpacked(v):
        return v, sroll(v, -2)

    def copy(w, slot, src, dst, d):
        return pltpu.make_async_remote_copy(
            src_ref=src,
            dst_ref=dst,
            send_sem=hs.at[w, slot],
            recv_sem=hr.at[w, slot],
            device_id=d,
            device_id_type=MESH,
        )

    def down(w, m):
        return copy(w, m, U.at[w, 1, m], U.at[w, 3, m], dev(-1, 0))

    def up(w, m):
        return copy(w, 4 + m, U.at[w, 2, m], U.at[w, 0, m], dev(1, 0))

    def left(w, m):
        return copy(w, 8 + m, PK0.at[w, m], XH.at[w, m], dev(0, -1))

    def right(w, m):
        return copy(w, 12 + m, PK3.at[w, m], CH.at[w, m], dev(0, 1))

    def corner_up(w):
        return copy(w, 16, PK0.at[w, 0], XH.at[w, 1], dev(1, -1))

    def corner_down(w):
        return copy(w, 17, PK3.at[w, 1], CH.at[w, 4], dev(-1, 1))

    for c in loads:
        c.wait()

    @pl.loop(0, 4)
    def _(m):
        pack(0, m)
        for s in range(2):
            acc[m, s] = 9.0 * U[0, 1 + s, m]

    pl.semaphore_wait(barrier, 11 + jnp.where(edge, 8, 0))
    corner_up(0).start()
    corner_down(0).start()
    for m in range(4):
        right(0, m).start()
        if m != 1:
            left(0, m).start()
    for m in range(4):
        up(0, m).start()
        if m != 0:
            down(0, m).start()

    def plane_yz(w):
        for s in (1, 2):
            uy, uz = ld(U, w, s, 2), ld(U, w, s, 3)
            uyz, uzy = yz_shift(uy, 3, 1), yz_shift(uz, 2, 1)
            p1, p2 = mm(uy, uzy), mm(uz, uyz)
            add(2, s - 1, mm(p2, uzy, db=True))
            add(3, s - 1, mm(p1, uyz, db=True))
            add(2, s - 1, yz_shift(mm(uz, p1, da=True), 3, -1))
            add(3, s - 1, yz_shift(mm(uy, p2, da=True), 2, -1))

    def plane_t(w, m, s):
        ut, um, umt = ld(U, w, s, 0), ld(U, w, s, m), ld(U, w, s + 1, m)
        utm = yz_shift(ut, m, 1)
        p1, p2 = mm(ut, umt), mm(um, utm)
        add(0, s - 1, mm(p2, umt, db=True))
        add(m, s - 1, mm(p1, utm, db=True))
        add(0, s - 1, yz_shift(mm(um, p1, da=True), m, -1))
        if s == 1:
            add(m, 1, mm(ut, p2, da=True))

    def plane_t_before(w, m):
        ut, um = ld(U, w, 0, 0), ld(U, w, 0, m)
        p2 = mm(um, yz_shift(ut, m, 1))
        add(m, 0, mm(ut, p2, da=True))

    def plane_tx(w):
        cx_re, cx_im = unpacked(CH[w, 1])
        far_re, far_im = unpacked(CH[w, 4])
        cx = (cx_re, cx_im)
        cxt = tuple(
            jnp.where(row4 == 0, sroll(v, -1), sroll(f, 1)) for v, f in ((cx_re, far_re), (cx_im, far_im))
        )
        ct = unpacked(CH[w, 0])
        lower_c = mm(cx, mm(ct, cxt), da=True)
        for s in (0, 1, 2):
            ut, ux = ld(U, w, s, 0), ld(U, w, s, 1)
            if s == 0:
                utx = x_next(ut, XH[w, 1], 1)
            else:
                utx = x_next(ut, XH[w, 0], s - 1)
            p2 = mm(ux, utx)
            if s < 2:
                add(1, s, mm(ut, p2, da=True))
            if s > 0:
                uxt = ld(U, w, s + 1, 1)
                p1 = mm(ut, uxt)
                add(0, s - 1, mm(p2, uxt, db=True))
                add(1, s - 1, mm(p1, utx, db=True))
                add(0, s - 1, x_prev(mm(ux, p1, da=True), lower_c, s - 1))

    def plane_x(w, m):
        cx, cm = unpacked(CH[w, 1]), unpacked(CH[w, m])
        lower_c = mm(cx, mm(cm, yz_shift(cx, m, 1)), da=True)
        for s in (1, 2):
            ux, um = ld(U, w, s, 1), ld(U, w, s, m)
            umx = x_next(um, XH[w, m], s - 1)
            uxm = yz_shift(ux, m, 1)
            p1, p2 = mm(ux, umx), mm(um, uxm)
            add(1, s - 1, mm(p2, umx, db=True))
            add(m, s - 1, mm(p1, uxm, db=True))
            add(1, s - 1, yz_shift(mm(um, p1, da=True), m, -1))
            add(m, s - 1, x_prev(mm(ux, p2, da=True), lower_c, s - 1))

    def unitarise(w, m):
        scale = ape_weight / 6.0
        for s in range(2):
            re = [[acc[m, s, 0, i, j] for j in range(3)] for i in range(3)]
            im = [[acc[m, s, 1, i, j] for j in range(3)] for i in range(3)]

            def diag(j):
                t = None
                for i in range(3):
                    q = re[i][j] * re[i][j] + im[i][j] * im[i][j]
                    t = q if t is None else t + q
                return t

            def off(j, k):
                a = b = None
                for i in range(3):
                    x = re[i][j] * re[i][k] + im[i][j] * im[i][k]
                    y = re[i][j] * im[i][k] - im[i][j] * re[i][k]
                    a = x if a is None else a + x
                    b = y if b is None else b + y
                return a, b

            k1, k2, k3 = diag(0), diag(1), diag(2)
            inverse = jnp.minimum(lax.rsqrt((scale * scale) * (k1 + k2 + k3)), 1.0)
            r = scale * inverse
            g = r * r
            a1, a2, a3 = g * k1, g * k2, g * k3
            b12 = tuple(g * v for v in off(0, 1))
            b13 = tuple(g * v for v in off(0, 2))
            b23 = tuple(g * v for v in off(1, 2))

            def norm(v):
                return v[0] * v[0] + v[1] * v[1]

            def times(a, b):
                return a[0] * b[0] - a[1] * b[1], a[0] * b[1] + a[1] * b[0]

            def ctimes(a, b):
                return a[0] * b[0] + a[1] * b[1], a[1] * b[0] - a[0] * b[1]

            j1 = a2 * a3 - norm(b23)
            j2 = a1 * a3 - norm(b13)
            j3 = a1 * a2 - norm(b12)
            q = ctimes(b13, b23)
            j12 = (q[0] - a3 * b12[0], q[1] - a3 * b12[1])
            q = times(b12, b23)
            j13 = (q[0] - a2 * b13[0], q[1] - a2 * b13[1])
            q = ctimes(b13, b12)
            j23 = (q[0] - a1 * b23[0], q[1] - a1 * b23[1])
            e1 = a1 + a2 + a3
            e2 = j1 + j2 + j3
            e3 = (
                a1 * j1
                + (b12[0] * j12[0] + b12[1] * j12[1])
                + (b13[0] * j13[0] + b13[1] * j13[1])
            )

            def reduce(d0, d1, d2, d3, d4):
                d3 = d3 + e1 * d4
                d2 = d2 - e2 * d4 + e1 * d3
                d1 = d1 + e3 * d4 - e2 * d3
                return d0 + e3 * d3, d1, d2

            h = (0.25 * e3, 2.25 - 0.25 * e2, 0.25 * e1 - 1.5)
            p = None
            for k in range(1, NEWTON):
                y = (1.5 - 0.5 * h[0], -0.5 * h[1], -0.5 * h[2])
                if p is None:
                    d3 = -0.5 * y[2]
                    p = (
                        1.5 * y[0] + e3 * d3,
                        1.5 * y[1] - 0.5 * y[0] - e2 * d3,
                        1.5 * y[2] - 0.5 * y[1] + e1 * d3,
                    )
                else:
                    p = reduce(
                        p[0] * y[0],
                        p[0] * y[1] + p[1] * y[0],
                        p[0] * y[2] + p[1] * y[1] + p[2] * y[0],
                        p[1] * y[2] + p[2] * y[1],
                        p[2] * y[2],
                    )
                if k < NEWTON - 1:
                    twice = p[0] + p[0]
                    f = reduce(
                        p[0] * p[0],
                        twice * p[1],
                        twice * p[2] + p[1] * p[1],
                        (p[1] + p[1]) * p[2],
                        p[2] * p[2],
                    )
                    h = (e3 * f[2], f[0] - e2 * f[2], f[1] + e1 * f[2])

            c2 = r * p[2]
            c1 = r * p[1] + e1 * c2
            c0 = r * p[0] - e2 * c2

            def entry(b, j):
                return c1 * b[0] + c2 * j[0], c1 * b[1] + c2 * j[1]

            m12, m13, m23 = entry(b12, j12), entry(b13, j13), entry(b23, j23)
            dg = [c0 + c1 * a + c2 * j for a, j in ((a1, j1), (a2, j2), (a3, j3))]
            table = {(0, 1): m12, (0, 2): m13, (1, 2): m23}
            for i in range(3):
                for j in range(3):
                    x = re[i][j] * dg[j]
                    y = im[i][j] * dg[j]
                    for k in range(3):
                        if k == j:
                            continue
                        vr, vi = table[(min(k, j), max(k, j))]
                        ur, ui = re[i][k], im[i][k]
                        if k < j:
                            x = x + ur * vr - ui * vi
                            y = y + ur * vi + ui * vr
                        else:
                            x = x + ur * vr + ui * vi
                            y = y - ur * vi + ui * vr
                    U[w + 1, 1 + s, m, 0, i, j] = x
                    U[w + 1, 1 + s, m, 1, i, j] = y
        for s in range(2):
            acc[m, s] = 9.0 * U[w + 1, 1 + s, m]

    def scatter(stage, src, dst, k):
        return pltpu.make_async_remote_copy(
            src_ref=src.at[:, :, :, pl.ds(k, 1), :],
            dst_ref=dst.at[:, :, :, pl.ds(8 - k, 1), :],
            send_sem=cs.at[stage, k],
            recv_sem=cr.at[stage, 8 - k],
            device_id=dev(k, 0),
            device_id_type=MESH,
        )

    def gathered(stage, src, dst, k):
        return pltpu.make_async_remote_copy(
            src_ref=src.at[:, :, :, pl.ds(8 - k, 1), :],
            dst_ref=dst.at[:, :, :, pl.ds(k, 1), :],
            send_sem=cs.at[stage, 8 - k],
            recv_sem=cr.at[stage, k],
            device_id=dev(8 - k, 0),
            device_id_type=MESH,
        )

    def turn(v, shift):
        flat = v.reshape((9, 8, LANES))
        return pltpu.roll(flat, shift, 1).reshape(v.shape)

    back = lax.rem(8 - ta, 8)

    def chain_start():
        q = mm(ld(U, 2, 1, 0), ld(U, 2, 2, 0))
        for c in range(2):
            Q[0, c] = turn(q[c], back)
        for k in range(1, 8):
            scatter(0, Q.at[0], R1, k).start()

    @pl.loop(0, 2)
    def _(w):
        plane_yz(w)
        for m in (2, 3):
            plane_t(w, m, 1)
        for m in (1, 2, 3):
            down(w, m).wait_recv()
        for m in range(4):
            up(w, m).wait_recv()
        for m in (2, 3):
            plane_t(w, m, 2)
            plane_t_before(w, m)
        for m in range(4):
            if m != 1:
                left(w, m).wait_recv()
            right(w, m).wait_recv()
        corner_up(w).wait_recv()
        corner_down(w).wait_recv()
        plane_tx(w)
        unitarise(w, 0)
        pack(w + 1, 0)
        left(w + 1, 0).start()

        @pl.when(w == 0)
        def _():
            corner_up(1).start()
            right(1, 0).start()
            up(1, 0).start()

        @pl.when(w == 1)
        def _():
            chain_start()

        for m in (2, 3):
            plane_x(w, m)

        @pl.loop(1, 4)
        def _(m):
            unitarise(w, m)

            @pl.when(w == 0)
            def _():
                pack(1, m)
                right(1, m).start()

                @pl.when(m != 1)
                def _():
                    left(1, m).start()

                @pl.when(m == 1)
                def _():
                    corner_down(1).start()

                up(1, m).start()
                down(1, m).start()

    for k in range(1, 8):
        gathered(0, Q.at[0], R1, k).wait_recv()
    sub = lax.broadcasted_iota(jnp.int32, (3, 3, 8, LANES), 2)
    eye = (
        lax.broadcasted_iota(jnp.int32, (3, 3, 8, LANES), 0)
        == lax.broadcasted_iota(jnp.int32, (3, 3, 8, LANES), 1)
    ).astype(jnp.float32)
    run = tuple(turn(jnp.where(sub == 0, Q[0, c], R1[c]), ta) for c in range(2))
    for step in (1, 2, 4):
        joined = mm(each(lambda v: sroll(v, step), run), run)
        run = tuple(jnp.where(sub >= step, j, v) for j, v in zip(joined, run))
    entering = (
        jnp.where(sub == 0, eye, sroll(run[0], 1)),
        jnp.where(sub == 0, 0.0, sroll(run[1], 1)),
    )
    for c in range(2):
        Q[1, c] = turn(entering[c], back)

    def column(k, h):
        return pltpu.make_async_remote_copy(
            src_ref=Q.at[1, :, :, :, pl.ds(k, 1), :],
            dst_ref=GH.at[:, :, :, pl.ds(4 * h + 3, 1), :],
            send_sem=ds.at[k],
            recv_sem=dr.at[h],
            device_id=dev(k, -1),
            device_id_type=MESH,
        )

    for h in range(2):

        @pl.when(ta == 4 * h)
        def _():
            for k in range(8):
                column(k, h).start()

    for k in range(1, 8):
        scatter(1, Q.at[1], R2, k).start()

    for k in range(1, 8):
        gathered(1, Q.at[1], R2, k).wait_recv()
    g1 = tuple(turn(jnp.where(sub == 0, Q[1, c], R2[c]), ta) for c in range(2))
    g2 = mm(g1, ld(U, 2, 1, 0))
    g3 = mm(g2, ld(U, 2, 2, 0))
    gs = (g1, g2)

    def store(m, s, pair):
        OUT[m, 0, :, :, s] = pair[0]
        OUT[m, 1, :, :, s] = pair[1]

    def save(m, t, h):
        return pltpu.make_async_copy(
            OUT.at[m, :, :, :, t, pl.ds(4 * h, 4), :],
            o_ref.at[m, :, :, :, t, :, pl.ds(h * LANES, LANES)],
            io.at[4 * m + 2 * t + h],
        )

    def save_all(m):
        for t in range(2):
            for h in range(2):
                save(m, t, h).start()

    store(0, 0, mm(g2, g2, db=True))
    store(0, 1, mm(g3, g3, db=True))
    save_all(0)
    for m in (2, 3):
        for s in range(2):
            store(m, s, mm(mm(gs[s], ld(U, 2, 1 + s, m)), yz_shift(gs[s], m, 1), db=True))
        save_all(m)
    left(2, 0).wait_recv()
    for h in range(2):
        pltpu.make_async_remote_copy(
            src_ref=Q.at[1, :, :, :, pl.ds(0, 1), :],
            dst_ref=GH.at[:, :, :, pl.ds(4 * h + 3, 1), :],
            send_sem=ds.at[0],
            recv_sem=dr.at[h],
            device_id=dev(0, -1),
            device_id_type=MESH,
        ).wait_recv()
    halo = XH[2, 0]
    gh1 = (GH[0], GH[1])
    gh2 = mm(gh1, tuple(sroll(halo, 3 - 2 * q) for q in range(2)))
    for s, gh in ((0, gh1), (1, gh2)):
        gx_next = tuple(jnp.where(row4 == 3, a, sroll(b, -1)) for a, b in zip(gh, gs[s]))
        store(1, s, mm(mm(gs[s], ld(U, 2, 1 + s, 1)), gx_next, db=True))
    save_all(1)

    for w in range(2):
        for m in range(4):
            if m != 0:
                down(w, m).wait_send()
            up(w, m).wait_send()
            if m != 1:
                left(w, m).wait_send()
            right(w, m).wait_send()
        corner_up(w).wait_send()
        corner_down(w).wait_send()
    left(2, 0).wait_send()
    for k in range(1, 8):
        scatter(0, Q.at[0], R1, k).wait_send()
        scatter(1, Q.at[1], R2, k).wait_send()
    for h in range(2):

        @pl.when(ta == 4 * h)
        def _():
            for k in range(8):
                column(k, h).wait_send()

    for m in range(4):
        for t in range(2):
            for h in range(2):
                save(m, t, h).wait()


def body(gauge_links):
    field = (2, 3, 3, 8, LANES)
    f32 = jnp.float32
    return pl.pallas_call(
        kernel,
        out_shape=jax.ShapeDtypeStruct(gauge_links.shape, f32),
        in_specs=[pl.BlockSpec(memory_space=pl.ANY)],
        out_specs=pl.BlockSpec(memory_space=pl.ANY),
        scratch_shapes=[
            pltpu.VMEM((3, 4, 4) + field, f32),
            pltpu.VMEM((3, 4) + field[1:], f32),
            pltpu.VMEM((2, 5) + field[1:], f32),
            pltpu.VMEM((3, 4) + field[1:], f32),
            pltpu.VMEM((3, 4) + field[1:], f32),
            pltpu.VMEM((4, 2) + field, f32),
            pltpu.VMEM((2,) + field, f32),
            pltpu.VMEM(field, f32),
            pltpu.VMEM(field, f32),
            pltpu.VMEM(field, f32),
            pltpu.VMEM((4, 2, 3, 3, 2, 8, LANES), f32),
            pltpu.SemaphoreType.DMA((3, 18)),
            pltpu.SemaphoreType.DMA((3, 18)),
            pltpu.SemaphoreType.DMA((2, 8)),
            pltpu.SemaphoreType.DMA((2, 8)),
            pltpu.SemaphoreType.DMA((8,)),
            pltpu.SemaphoreType.DMA((2,)),
            pltpu.SemaphoreType.DMA((16,)),
        ],
        compiler_params=pltpu.CompilerParams(
            collective_id=0, has_side_effects=True, vmem_limit_bytes=32 * 2**20
        ),
    )(gauge_links)


def solution(mesh):
    spec = P(None, None, None, None, "ta", "gx", None)
    return jax.shard_map(body, mesh=mesh, in_specs=(spec,), out_specs=spec, check_vma=False)
```

```python
import functools

import jax
import jax.numpy as jnp
from jax import lax
from jax.experimental import pallas as pl
from jax.experimental.pallas import tpu as pltpu
from jax.sharding import PartitionSpec as P

MESH = pl.DeviceIdType.MESH
NZ = 16
NEWTON = 5
ape_weight = 0.4
LANES = 128


def mm(a, b, da=False, db=False):
    def left(c):
        return tuple(q[c, :, None] if da else q[:, c, None] for q in a)

    def right(c):
        return tuple(q[None, :, c] if db else q[None, c] for q in b)

    re = im = None
    for c in range(3):
        lr, li = left(c)
        rr, ri = right(c)
        x, y = lr * rr, li * ri
        u, v = lr * ri, li * rr
        re = x if re is None else re + x
        re = re + y if da != db else re - y
        if im is None:
            if da and db:
                im = -u - v
            elif da:
                im = u - v
            elif db:
                im = v - u
            else:
                im = u + v
        else:
            im = im - u if db else im + u
            im = im - v if da else im + v
    return re, im


def lane_of(shape):
    return lax.broadcasted_iota(jnp.int32, shape, len(shape) - 1)


def each(f, pair):
    return tuple(f(q) for q in pair)


def sroll(v, shift):
    shift = shift % 8
    if shift == 0:
        return v
    flat = v.reshape((9, 8, LANES))
    return pltpu.roll(flat, shift, 1).reshape(v.shape)


def lroll(v, shift):
    return pltpu.roll(v.reshape((72, LANES)), shift % LANES, 1).reshape(v.shape)


def yz_shift(pair, m, sign):
    lane = lane_of((3, 3, 8, LANES))
    z = lax.rem(lane, NZ)
    if isinstance(m, int):
        if m == 2:

            def move(v):
                r = lroll(v, -NZ * sign)
                stay = lane < LANES - NZ if sign > 0 else lane >= NZ
                return jnp.where(stay, r, sroll(r, 4))

        else:

            def move(v):
                stay = z < NZ - 1 if sign > 0 else z >= 1
                return jnp.where(stay, lroll(v, -sign), lroll(v, sign * (NZ - 1)))

        return each(move, pair)
    raise NotImplementedError


def kernel(x_ref, o_ref, U, XH, CH, PK0, PK3, acc, Q, R1, R2, GH, OUT, hs, hr, cs, cr, ds, dr, io):
    ta = lax.axis_index("ta")
    gx = lax.axis_index("gx")
    nta = lax.axis_size("ta")
    ngx = lax.axis_size("gx")

    def dev(dt, dg):
        return {"ta": lax.rem(ta + dt + nta, nta), "gx": lax.rem(gx + dg + ngx, ngx)}

    barrier = pltpu.get_barrier_semaphore()
    greeted = [dev(0, 1), dev(0, -1), dev(-1, 1), dev(1, -1)] + [dev(k, 0) for k in range(1, 8)]
    for d in greeted:
        pl.semaphore_signal(barrier, inc=1, device_id=d, device_id_type=MESH)

    loads = []
    for t in range(2):
        for h in range(2):
            c = pltpu.make_async_copy(
                x_ref.at[:, :, :, :, t, :, pl.ds(h * LANES, LANES)],
                U.at[0, 1 + t, :, :, :, :, pl.ds(4 * h, 4), :],
                io.at[2 * t + h],
            )
            c.start()
            loads.append(c)

    def ld(ref, *at):
        v = ref[at]
        return v[0], v[1]

    def add(m, s, pair):
        acc[m, s, 0] = acc[m, s, 0] + pair[0]
        acc[m, s, 1] = acc[m, s, 1] + pair[1]

    row4 = lax.rem(lax.broadcasted_iota(jnp.int32, (3, 3, 8, LANES), 2), 4)

    def pack(w, m):
        parts = [U[w, 1, m, 0], U[w, 2, m, 0], U[w, 1, m, 1], U[w, 2, m, 1]]
        for col, out in ((0, PK0), (3, PK3)):
            moved = [sroll(v, q - col) for q, v in enumerate(parts)]
            out[w, m] = jnp.where(
                row4 < 2,
                jnp.where(row4 == 0, moved[0], moved[1]),
                jnp.where(row4 == 2, moved[2], moved[3]),
            )

    def x_next(pair, halo, t):
        return tuple(
            jnp.where(row4 == 3, sroll(halo, 3 - t - 2 * q), sroll(v, -1))
            for q, v in enumerate(pair)
        )

    def x_prev(pair, column, t):
        return tuple(
            jnp.where(row4 == 0, sroll(c, -t), sroll(v, 1)) for v, c in zip(pair, column)
        )

    def unpacked(v):
        return v, sroll(v, -2)

    def copy(w, slot, src, dst, d):
        return pltpu.make_async_remote_copy(
            src_ref=src,
            dst_ref=dst,
            send_sem=hs.at[w, slot],
            recv_sem=hr.at[w, slot],
            device_id=d,
            device_id_type=MESH,
        )

    def down(w, m):
        return copy(w, m, U.at[w, 1, m], U.at[w, 3, m], dev(-1, 0))

    def up(w, m):
        return copy(w, 4 + m, U.at[w, 2, m], U.at[w, 0, m], dev(1, 0))

    def left(w, m):
        return copy(w, 8 + m, PK0.at[w, m], XH.at[w, m], dev(0, -1))

    def right(w, m):
        return copy(w, 12 + m, PK3.at[w, m], CH.at[w, m], dev(0, 1))

    def corner_up(w):
        return copy(w, 16, PK0.at[w, 0], XH.at[w, 1], dev(1, -1))

    def corner_down(w):
        return copy(w, 17, PK3.at[w, 1], CH.at[w, 4], dev(-1, 1))

    for c in loads:
        c.wait()

    @pl.loop(0, 4)
    def _(m):
        pack(0, m)
        for s in range(2):
            acc[m, s] = 9.0 * U[0, 1 + s, m]

    pl.semaphore_wait(barrier, 11)
    corner_up(0).start()
    corner_down(0).start()
    for m in range(4):
        right(0, m).start()
        if m != 1:
            left(0, m).start()
    for m in range(4):
        up(0, m).start()
        if m != 0:
            down(0, m).start()

    def plane_yz(w):
        for s in (1, 2):
            uy, uz = ld(U, w, s, 2), ld(U, w, s, 3)
            uyz, uzy = yz_shift(uy, 3, 1), yz_shift(uz, 2, 1)
            p1, p2 = mm(uy, uzy), mm(uz, uyz)
            add(2, s - 1, mm(p2, uzy, db=True))
            add(3, s - 1, mm(p1, uyz, db=True))
            add(2, s - 1, yz_shift(mm(uz, p1, da=True), 3, -1))
            add(3, s - 1, yz_shift(mm(uy, p2, da=True), 2, -1))

    def plane_t(w, m, s):
        ut, um, umt = ld(U, w, s, 0), ld(U, w, s, m), ld(U, w, s + 1, m)
        utm = yz_shift(ut, m, 1)
        p1, p2 = mm(ut, umt), mm(um, utm)
        add(0, s - 1, mm(p2, umt, db=True))
        add(m, s - 1, mm(p1, utm, db=True))
        add(0, s - 1, yz_shift(mm(um, p1, da=True), m, -1))
        if s == 1:
            add(m, 1, mm(ut, p2, da=True))

    def plane_t_before(w, m):
        ut, um = ld(U, w, 0, 0), ld(U, w, 0, m)
        p2 = mm(um, yz_shift(ut, m, 1))
        add(m, 0, mm(ut, p2, da=True))

    def plane_tx(w):
        cx_re, cx_im = unpacked(CH[w, 1])
        far_re, far_im = unpacked(CH[w, 4])
        cx = (cx_re, cx_im)
        cxt = tuple(
            jnp.where(row4 == 0, sroll(v, -1), sroll(f, 1)) for v, f in ((cx_re, far_re), (cx_im, far_im))
        )
        ct = unpacked(CH[w, 0])
        lower_c = mm(cx, mm(ct, cxt), da=True)
        for s in (0, 1, 2):
            ut, ux = ld(U, w, s, 0), ld(U, w, s, 1)
            if s == 0:
                utx = x_next(ut, XH[w, 1], 1)
            else:
                utx = x_next(ut, XH[w, 0], s - 1)
            p2 = mm(ux, utx)
            if s < 2:
                add(1, s, mm(ut, p2, da=True))
            if s > 0:
                uxt = ld(U, w, s + 1, 1)
                p1 = mm(ut, uxt)
                add(0, s - 1, mm(p2, uxt, db=True))
                add(1, s - 1, mm(p1, utx, db=True))
                add(0, s - 1, x_prev(mm(ux, p1, da=True), lower_c, s - 1))

    def plane_x(w, m):
        cx, cm = unpacked(CH[w, 1]), unpacked(CH[w, m])
        lower_c = mm(cx, mm(cm, yz_shift(cx, m, 1)), da=True)
        for s in (1, 2):
            ux, um = ld(U, w, s, 1), ld(U, w, s, m)
            umx = x_next(um, XH[w, m], s - 1)
            uxm = yz_shift(ux, m, 1)
            p1, p2 = mm(ux, umx), mm(um, uxm)
            add(1, s - 1, mm(p2, umx, db=True))
            add(m, s - 1, mm(p1, uxm, db=True))
            add(1, s - 1, yz_shift(mm(um, p1, da=True), m, -1))
            add(m, s - 1, x_prev(mm(ux, p2, da=True), lower_c, s - 1))

    def unitarise(w, m):
        scale = ape_weight / 6.0
        for s in range(2):
            re = [[acc[m, s, 0, i, j] for j in range(3)] for i in range(3)]
            im = [[acc[m, s, 1, i, j] for j in range(3)] for i in range(3)]

            def diag(j):
                t = None
                for i in range(3):
                    q = re[i][j] * re[i][j] + im[i][j] * im[i][j]
                    t = q if t is None else t + q
                return t

            def off(j, k):
                a = b = None
                for i in range(3):
                    x = re[i][j] * re[i][k] + im[i][j] * im[i][k]
                    y = re[i][j] * im[i][k] - im[i][j] * re[i][k]
                    a = x if a is None else a + x
                    b = y if b is None else b + y
                return a, b

            k1, k2, k3 = diag(0), diag(1), diag(2)
            inverse = jnp.minimum(lax.rsqrt((scale * scale) * (k1 + k2 + k3)), 1.0)
            r = scale * inverse
            g = r * r
            a1, a2, a3 = g * k1, g * k2, g * k3
            b12 = tuple(g * v for v in off(0, 1))
            b13 = tuple(g * v for v in off(0, 2))
            b23 = tuple(g * v for v in off(1, 2))

            def norm(v):
                return v[0] * v[0] + v[1] * v[1]

            def times(a, b):
                return a[0] * b[0] - a[1] * b[1], a[0] * b[1] + a[1] * b[0]

            def ctimes(a, b):
                return a[0] * b[0] + a[1] * b[1], a[1] * b[0] - a[0] * b[1]

            j1 = a2 * a3 - norm(b23)
            j2 = a1 * a3 - norm(b13)
            j3 = a1 * a2 - norm(b12)
            q = ctimes(b13, b23)
            j12 = (q[0] - a3 * b12[0], q[1] - a3 * b12[1])
            q = times(b12, b23)
            j13 = (q[0] - a2 * b13[0], q[1] - a2 * b13[1])
            q = ctimes(b13, b12)
            j23 = (q[0] - a1 * b23[0], q[1] - a1 * b23[1])
            e1 = a1 + a2 + a3
            e2 = j1 + j2 + j3
            e3 = (
                a1 * j1
                + (b12[0] * j12[0] + b12[1] * j12[1])
                + (b13[0] * j13[0] + b13[1] * j13[1])
            )

            def reduce(d0, d1, d2, d3, d4):
                d3 = d3 + e1 * d4
                d2 = d2 - e2 * d4 + e1 * d3
                d1 = d1 + e3 * d4 - e2 * d3
                return d0 + e3 * d3, d1, d2

            h = (0.25 * e3, 2.25 - 0.25 * e2, 0.25 * e1 - 1.5)
            p = None
            for k in range(1, NEWTON):
                y = (1.5 - 0.5 * h[0], -0.5 * h[1], -0.5 * h[2])
                if p is None:
                    d3 = -0.5 * y[2]
                    p = (
                        1.5 * y[0] + e3 * d3,
                        1.5 * y[1] - 0.5 * y[0] - e2 * d3,
                        1.5 * y[2] - 0.5 * y[1] + e1 * d3,
                    )
                else:
                    p = reduce(
                        p[0] * y[0],
                        p[0] * y[1] + p[1] * y[0],
                        p[0] * y[2] + p[1] * y[1] + p[2] * y[0],
                        p[1] * y[2] + p[2] * y[1],
                        p[2] * y[2],
                    )
                if k < NEWTON - 1:
                    twice = p[0] + p[0]
                    f = reduce(
                        p[0] * p[0],
                        twice * p[1],
                        twice * p[2] + p[1] * p[1],
                        (p[1] + p[1]) * p[2],
                        p[2] * p[2],
                    )
                    h = (e3 * f[2], f[0] - e2 * f[2], f[1] + e1 * f[2])

            c2 = r * p[2]
            c1 = r * p[1] + e1 * c2
            c0 = r * p[0] - e2 * c2

            def entry(b, j):
                return c1 * b[0] + c2 * j[0], c1 * b[1] + c2 * j[1]

            m12, m13, m23 = entry(b12, j12), entry(b13, j13), entry(b23, j23)
            dg = [c0 + c1 * a + c2 * j for a, j in ((a1, j1), (a2, j2), (a3, j3))]
            table = {(0, 1): m12, (0, 2): m13, (1, 2): m23}
            for i in range(3):
                for j in range(3):
                    x = re[i][j] * dg[j]
                    y = im[i][j] * dg[j]
                    for k in range(3):
                        if k == j:
                            continue
                        vr, vi = table[(min(k, j), max(k, j))]
                        ur, ui = re[i][k], im[i][k]
                        if k < j:
                            x = x + ur * vr - ui * vi
                            y = y + ur * vi + ui * vr
                        else:
                            x = x + ur * vr + ui * vi
                            y = y - ur * vi + ui * vr
                    U[w + 1, 1 + s, m, 0, i, j] = x
                    U[w + 1, 1 + s, m, 1, i, j] = y
        for s in range(2):
            acc[m, s] = 9.0 * U[w + 1, 1 + s, m]

    def scatter(stage, src, dst, k):
        return pltpu.make_async_remote_copy(
            src_ref=src.at[:, :, :, pl.ds(k, 1), :],
            dst_ref=dst.at[:, :, :, pl.ds(8 - k, 1), :],
            send_sem=cs.at[stage, k],
            recv_sem=cr.at[stage, 8 - k],
            device_id=dev(k, 0),
            device_id_type=MESH,
        )

    def gathered(stage, src, dst, k):
        return pltpu.make_async_remote_copy(
            src_ref=src.at[:, :, :, pl.ds(8 - k, 1), :],
            dst_ref=dst.at[:, :, :, pl.ds(k, 1), :],
            send_sem=cs.at[stage, 8 - k],
            recv_sem=cr.at[stage, k],
            device_id=dev(8 - k, 0),
            device_id_type=MESH,
        )

    def turn(v, shift):
        flat = v.reshape((9, 8, LANES))
        return pltpu.roll(flat, shift, 1).reshape(v.shape)

    back = lax.rem(8 - ta, 8)

    def chain_start():
        q = mm(ld(U, 2, 1, 0), ld(U, 2, 2, 0))
        for c in range(2):
            Q[0, c] = turn(q[c], back)
        for k in range(1, 8):
            scatter(0, Q.at[0], R1, k).start()

    @pl.loop(0, 2)
    def _(w):
        plane_yz(w)
        for m in (2, 3):
            plane_t(w, m, 1)
        for m in (1, 2, 3):
            down(w, m).wait_recv()
        for m in range(4):
            up(w, m).wait_recv()
        for m in (2, 3):
            plane_t(w, m, 2)
            plane_t_before(w, m)
        for m in range(4):
            if m != 1:
                left(w, m).wait_recv()
            right(w, m).wait_recv()
        corner_up(w).wait_recv()
        corner_down(w).wait_recv()
        plane_tx(w)
        unitarise(w, 0)
        pack(w + 1, 0)
        left(w + 1, 0).start()

        @pl.when(w == 0)
        def _():
            corner_up(1).start()
            right(1, 0).start()
            up(1, 0).start()

        @pl.when(w == 1)
        def _():
            chain_start()

        for m in (2, 3):
            plane_x(w, m)

        @pl.loop(1, 4)
        def _(m):
            unitarise(w, m)

            @pl.when(w == 0)
            def _():
                pack(1, m)
                right(1, m).start()

                @pl.when(m != 1)
                def _():
                    left(1, m).start()

                @pl.when(m == 1)
                def _():
                    corner_down(1).start()

                up(1, m).start()
                down(1, m).start()

    for k in range(1, 8):
        gathered(0, Q.at[0], R1, k).wait_recv()
    sub = lax.broadcasted_iota(jnp.int32, (3, 3, 8, LANES), 2)
    eye = (
        lax.broadcasted_iota(jnp.int32, (3, 3, 8, LANES), 0)
        == lax.broadcasted_iota(jnp.int32, (3, 3, 8, LANES), 1)
    ).astype(jnp.float32)
    run = tuple(turn(jnp.where(sub == 0, Q[0, c], R1[c]), ta) for c in range(2))
    for step in (1, 2, 4):
        joined = mm(each(lambda v: sroll(v, step), run), run)
        run = tuple(jnp.where(sub >= step, j, v) for j, v in zip(joined, run))
    entering = (
        jnp.where(sub == 0, eye, sroll(run[0], 1)),
        jnp.where(sub == 0, 0.0, sroll(run[1], 1)),
    )
    for c in range(2):
        Q[1, c] = turn(entering[c], back)

    def column(k, h):
        return pltpu.make_async_remote_copy(
            src_ref=Q.at[1, :, :, :, pl.ds(k, 1), :],
            dst_ref=GH.at[:, :, :, pl.ds(4 * h + 3, 1), :],
            send_sem=ds.at[k],
            recv_sem=dr.at[h],
            device_id=dev(k, -1),
            device_id_type=MESH,
        )

    for h in range(2):

        @pl.when(ta == 4 * h)
        def _():
            for k in range(8):
                column(k, h).start()

    for k in range(1, 8):
        scatter(1, Q.at[1], R2, k).start()

    for k in range(1, 8):
        gathered(1, Q.at[1], R2, k).wait_recv()
    g1 = tuple(turn(jnp.where(sub == 0, Q[1, c], R2[c]), ta) for c in range(2))
    g2 = mm(g1, ld(U, 2, 1, 0))
    g3 = mm(g2, ld(U, 2, 2, 0))
    gs = (g1, g2)

    def store(m, s, pair):
        OUT[m, 0, :, :, s] = pair[0]
        OUT[m, 1, :, :, s] = pair[1]

    def save(m, t, h):
        return pltpu.make_async_copy(
            OUT.at[m, :, :, :, t, pl.ds(4 * h, 4), :],
            o_ref.at[m, :, :, :, t, :, pl.ds(h * LANES, LANES)],
            io.at[4 * m + 2 * t + h],
        )

    def save_all(m):
        for t in range(2):
            for h in range(2):
                save(m, t, h).start()

    store(0, 0, mm(g2, g2, db=True))
    store(0, 1, mm(g3, g3, db=True))
    save_all(0)
    for m in (2, 3):
        for s in range(2):
            store(m, s, mm(mm(gs[s], ld(U, 2, 1 + s, m)), yz_shift(gs[s], m, 1), db=True))
        save_all(m)
    left(2, 0).wait_recv()
    for h in range(2):
        pltpu.make_async_remote_copy(
            src_ref=Q.at[1, :, :, :, pl.ds(0, 1), :],
            dst_ref=GH.at[:, :, :, pl.ds(4 * h + 3, 1), :],
            send_sem=ds.at[0],
            recv_sem=dr.at[h],
            device_id=dev(0, -1),
            device_id_type=MESH,
        ).wait_recv()
    halo = XH[2, 0]
    gh1 = (GH[0], GH[1])
    gh2 = mm(gh1, tuple(sroll(halo, 3 - 2 * q) for q in range(2)))
    for s, gh in ((0, gh1), (1, gh2)):
        gx_next = tuple(jnp.where(row4 == 3, a, sroll(b, -1)) for a, b in zip(gh, gs[s]))
        store(1, s, mm(mm(gs[s], ld(U, 2, 1 + s, 1)), gx_next, db=True))
    save_all(1)

    for w in range(2):
        for m in range(4):
            if m != 0:
                down(w, m).wait_send()
            up(w, m).wait_send()
            if m != 1:
                left(w, m).wait_send()
            right(w, m).wait_send()
        corner_up(w).wait_send()
        corner_down(w).wait_send()
    left(2, 0).wait_send()
    for k in range(1, 8):
        scatter(0, Q.at[0], R1, k).wait_send()
        scatter(1, Q.at[1], R2, k).wait_send()
    for h in range(2):

        @pl.when(ta == 4 * h)
        def _():
            for k in range(8):
                column(k, h).wait_send()

    for m in range(4):
        for t in range(2):
            for h in range(2):
                save(m, t, h).wait()


def body(gauge_links):
    field = (2, 3, 3, 8, LANES)
    f32 = jnp.float32
    return pl.pallas_call(
        kernel,
        out_shape=jax.ShapeDtypeStruct(gauge_links.shape, f32),
        in_specs=[pl.BlockSpec(memory_space=pltpu.HBM)],
        out_specs=pl.BlockSpec(memory_space=pl.ANY),
        scratch_shapes=[
            pltpu.VMEM((3, 4, 4) + field, f32),
            pltpu.VMEM((3, 4) + field[1:], f32),
            pltpu.VMEM((2, 5) + field[1:], f32),
            pltpu.VMEM((3, 4) + field[1:], f32),
            pltpu.VMEM((3, 4) + field[1:], f32),
            pltpu.VMEM((4, 2) + field, f32),
            pltpu.VMEM((2,) + field, f32),
            pltpu.VMEM(field, f32),
            pltpu.VMEM(field, f32),
            pltpu.VMEM(field, f32),
            pltpu.VMEM((4, 2, 3, 3, 2, 8, LANES), f32),
            pltpu.SemaphoreType.DMA((3, 18)),
            pltpu.SemaphoreType.DMA((3, 18)),
            pltpu.SemaphoreType.DMA((2, 8)),
            pltpu.SemaphoreType.DMA((2, 8)),
            pltpu.SemaphoreType.DMA((8,)),
            pltpu.SemaphoreType.DMA((2,)),
            pltpu.SemaphoreType.DMA((16,)),
        ],
        compiler_params=pltpu.CompilerParams(
            collective_id=0, has_side_effects=True, vmem_limit_bytes=32 * 2**20
        ),
    )(gauge_links)


def solution(mesh):
    spec = P(None, None, None, None, "ta", "gx", None)
    return jax.shard_map(body, mesh=mesh, in_specs=(spec,), out_specs=spec, check_vma=False)
```

```python
import functools

import jax
import jax.numpy as jnp
from jax import lax
from jax.experimental import pallas as pl
from jax.experimental.pallas import tpu as pltpu
from jax.sharding import PartitionSpec as P

MESH = pl.DeviceIdType.MESH
NZ = 16
NEWTON = 5
ape_weight = 0.4
LANES = 128


def mm(a, b, da=False, db=False):
    def left(c):
        return tuple(q[c, :, None] if da else q[:, c, None] for q in a)

    def right(c):
        return tuple(q[None, :, c] if db else q[None, c] for q in b)

    re = im = None
    for c in range(3):
        lr, li = left(c)
        rr, ri = right(c)
        x, y = lr * rr, li * ri
        u, v = lr * ri, li * rr
        re = x if re is None else re + x
        re = re + y if da != db else re - y
        if im is None:
            if da and db:
                im = -u - v
            elif da:
                im = u - v
            elif db:
                im = v - u
            else:
                im = u + v
        else:
            im = im - u if db else im + u
            im = im - v if da else im + v
    return re, im


def lane_of(shape):
    return lax.broadcasted_iota(jnp.int32, shape, len(shape) - 1)


def each(f, pair):
    return tuple(f(q) for q in pair)


def sroll(v, shift):
    shift = shift % 8
    if shift == 0:
        return v
    flat = v.reshape((9, 8, LANES))
    return pltpu.roll(flat, shift, 1).reshape(v.shape)


def lroll(v, shift):
    return pltpu.roll(v.reshape((72, LANES)), shift % LANES, 1).reshape(v.shape)


def yz_shift(pair, m, sign):
    lane = lane_of((3, 3, 8, LANES))
    z = lax.rem(lane, NZ)
    if isinstance(m, int):
        if m == 2:

            def move(v):
                r = lroll(v, -NZ * sign)
                stay = lane < LANES - NZ if sign > 0 else lane >= NZ
                return jnp.where(stay, r, sroll(r, 4))

        else:

            def move(v):
                stay = z < NZ - 1 if sign > 0 else z >= 1
                return jnp.where(stay, lroll(v, -sign), lroll(v, sign * (NZ - 1)))

        return each(move, pair)
    raise NotImplementedError


def kernel(
    x_ref, o_ref, U, XH, CH, PK0, PK3, RL, acc, Q, SQ, CQ, EH, XQ, OUT, hs, hr, cs, cr, io
):
    ta = lax.axis_index("ta")
    gx = lax.axis_index("gx")
    nta = lax.axis_size("ta")
    ngx = lax.axis_size("gx")
    core, chip = lax.rem(ta, 2), ta // 2

    def dev(dt, dg):
        return {"ta": lax.rem(ta + dt + nta, nta), "gx": lax.rem(gx + dg + ngx, ngx)}

    barrier = pltpu.get_barrier_semaphore()
    for d in (dev(0, 1), dev(0, -1), dev(4, 0), dev(1, 0), dev(-1, 0)):
        pl.semaphore_signal(barrier, inc=1, device_id=d, device_id_type=MESH)

    loads = []
    for t in range(2):
        for h in range(2):
            c = pltpu.make_async_copy(
                x_ref.at[:, :, :, :, t, :, pl.ds(h * LANES, LANES)],
                U.at[0, 1 + t, :, :, :, :, pl.ds(4 * h, 4), :],
                io.at[2 * t + h],
            )
            c.start()
            loads.append(c)

    def ld(ref, *at):
        v = ref[at]
        return v[0], v[1]

    def add(m, s, pair):
        acc[m, s, 0] = acc[m, s, 0] + pair[0]
        acc[m, s, 1] = acc[m, s, 1] + pair[1]

    row4 = lax.rem(lax.broadcasted_iota(jnp.int32, (3, 3, 8, LANES), 2), 4)

    def pack(w, m):
        parts = [U[w, 1, m, 0], U[w, 2, m, 0], U[w, 1, m, 1], U[w, 2, m, 1]]
        for col, out in ((0, PK0), (3, PK3)):
            moved = [sroll(v, q - col) for q, v in enumerate(parts)]
            out[w, m] = jnp.where(
                row4 < 2,
                jnp.where(row4 == 0, moved[0], moved[1]),
                jnp.where(row4 == 2, moved[2], moved[3]),
            )

    def x_next(pair, halo, t):
        return tuple(
            jnp.where(row4 == 3, sroll(halo, 3 - t - 2 * q), sroll(v, -1))
            for q, v in enumerate(pair)
        )

    def x_prev(pair, column, t):
        return tuple(
            jnp.where(row4 == 0, sroll(c, -t), sroll(v, 1)) for v, c in zip(pair, column)
        )

    def unpacked(v):
        return v, sroll(v, -2)

    def copy(w, slot, src, dst, d):
        return pltpu.make_async_remote_copy(
            src_ref=src,
            dst_ref=dst,
            send_sem=hs.at[w, slot],
            recv_sem=hr.at[w, slot],
            device_id=d,
            device_id_type=MESH,
        )

    def face(w, s, m):
        return U.at[w, s, m, :, pl.ds(0, 2)] if w == 0 else U.at[w, s, m]

    def cols(ref, w, m):
        return ref.at[w, m, pl.ds(0, 2)] if w == 0 else ref.at[w, m]

    def down(w, m):
        return copy(w, m, face(w, 1, m), face(w, 3, m), dev(-1, 0))

    def up(w, m):
        return copy(w, 4 + m, face(w, 2, m), face(w, 0, m), dev(1, 0))

    def left(w, m):
        return copy(w, 8 + m, cols(PK0, w, m), cols(XH, w, m), dev(0, -1))

    def right(w, m):
        return copy(w, 12 + m, cols(PK3, w, m), cols(CH, w, m), dev(0, 1))

    def corner_up(w):
        return copy(w, 16, cols(PK0, w, 0), cols(XH, w, 1), dev(1, -1))

    def corner_down(w):
        return copy(w, 17, cols(PK3, w, 1), cols(CH, w, 4), dev(-1, 1))

    def first_up():
        return copy(0, 18, cols(PK0, 0, 0), RL.at[0], dev(1, 0))

    def first_down():
        return copy(0, 19, cols(PK3, 0, 1), RL.at[1], dev(-1, 0))

    def then_left():
        return copy(0, 16, RL.at[0], cols(XH, 0, 1), dev(0, -1))

    def then_right():
        return copy(0, 17, RL.at[1], cols(CH, 0, 4), dev(0, 1))

    def cross(a, b):
        out = []
        for j in range(3):
            (pr, pi), (qr, qi) = a[(j + 1) % 3], b[(j + 2) % 3]
            (tr, ti), (ur, ui) = a[(j + 2) % 3], b[(j + 1) % 3]
            out.append((pr * qr - pi * qi - tr * ur + ti * ui, tr * ui + ti * ur - pr * qi - pi * qr))
        return out

    def third_face(s, m):
        rows = [[(U[0, s, m, 0, i, j], U[0, s, m, 1, i, j]) for j in range(3)] for i in range(2)]
        for j, (re, im) in enumerate(cross(*rows)):
            U[0, s, m, 0, 2, j] = re
            U[0, s, m, 1, 2, j] = im

    quad = lax.rem(lax.broadcasted_iota(jnp.int32, (8, LANES), 0), 4)

    def third_cols(ref, m):
        rows = [
            [(ref[0, m, i, j], pltpu.roll(ref[0, m, i, j], 6, 0)) for j in range(3)] for i in range(2)
        ]
        for j, (re, im) in enumerate(cross(*rows)):
            ref[0, m, 2, j] = jnp.where(quad < 2, re, pltpu.roll(im, 2, 0))

    for c in loads:
        c.wait()

    @pl.loop(0, 4)
    def _(m):
        pack(0, m)
        for s in range(2):
            acc[m, s] = 9.0 * U[0, 1 + s, m]

    pl.semaphore_wait(barrier, 5)
    first_down().start()
    first_up().start()
    for m in (1, 0, 2, 3):
        right(0, m).start()
        if m != 1:
            left(0, m).start()
    for m in range(4):
        up(0, m).start()
        if m != 0:
            down(0, m).start()

    def plane_yz(w):
        for s in (1, 2):
            uy, uz = ld(U, w, s, 2), ld(U, w, s, 3)
            uyz, uzy = yz_shift(uy, 3, 1), yz_shift(uz, 2, 1)
            p1, p2 = mm(uy, uzy), mm(uz, uyz)
            add(2, s - 1, mm(p2, uzy, db=True))
            add(3, s - 1, mm(p1, uyz, db=True))
            add(2, s - 1, yz_shift(mm(uz, p1, da=True), 3, -1))
            add(3, s - 1, yz_shift(mm(uy, p2, da=True), 2, -1))

    def plane_t(w, m, s):
        ut, um, umt = ld(U, w, s, 0), ld(U, w, s, m), ld(U, w, s + 1, m)
        utm = yz_shift(ut, m, 1)
        p1, p2 = mm(ut, umt), mm(um, utm)
        add(0, s - 1, mm(p2, umt, db=True))
        add(m, s - 1, mm(p1, utm, db=True))
        add(0, s - 1, yz_shift(mm(um, p1, da=True), m, -1))
        if s == 1:
            add(m, 1, mm(ut, p2, da=True))

    def plane_t_before(w, m):
        ut, um = ld(U, w, 0, 0), ld(U, w, 0, m)
        p2 = mm(um, yz_shift(ut, m, 1))
        add(m, 0, mm(ut, p2, da=True))

    def plane_tx(w):
        cx_re, cx_im = unpacked(CH[w, 1])
        far_re, far_im = unpacked(CH[w, 4])
        cx = (cx_re, cx_im)
        cxt = tuple(
            jnp.where(row4 == 0, sroll(v, -1), sroll(f, 1)) for v, f in ((cx_re, far_re), (cx_im, far_im))
        )
        ct = unpacked(CH[w, 0])
        lower_c = mm(cx, mm(ct, cxt), da=True)
        for s in (0, 1, 2):
            ut, ux = ld(U, w, s, 0), ld(U, w, s, 1)
            if s == 0:
                utx = x_next(ut, XH[w, 1], 1)
            else:
                utx = x_next(ut, XH[w, 0], s - 1)
            p2 = mm(ux, utx)
            if s < 2:
                add(1, s, mm(ut, p2, da=True))
            if s > 0:
                uxt = ld(U, w, s + 1, 1)
                p1 = mm(ut, uxt)
                add(0, s - 1, mm(p2, uxt, db=True))
                add(1, s - 1, mm(p1, utx, db=True))
                add(0, s - 1, x_prev(mm(ux, p1, da=True), lower_c, s - 1))

    def plane_x(w, m):
        cx, cm = unpacked(CH[w, 1]), unpacked(CH[w, m])
        lower_c = mm(cx, mm(cm, yz_shift(cx, m, 1)), da=True)
        for s in (1, 2):
            ux, um = ld(U, w, s, 1), ld(U, w, s, m)
            umx = x_next(um, XH[w, m], s - 1)
            uxm = yz_shift(ux, m, 1)
            p1, p2 = mm(ux, umx), mm(um, uxm)
            add(1, s - 1, mm(p2, umx, db=True))
            add(m, s - 1, mm(p1, uxm, db=True))
            add(1, s - 1, yz_shift(mm(um, p1, da=True), m, -1))
            add(m, s - 1, x_prev(mm(ux, p2, da=True), lower_c, s - 1))

    def unitarise(w, m):
        scale = ape_weight / 6.0
        for s in range(2):
            re = [[acc[m, s, 0, i, j] for j in range(3)] for i in range(3)]
            im = [[acc[m, s, 1, i, j] for j in range(3)] for i in range(3)]

            def diag(j):
                t = None
                for i in range(3):
                    q = re[i][j] * re[i][j] + im[i][j] * im[i][j]
                    t = q if t is None else t + q
                return t

            def off(j, k):
                a = b = None
                for i in range(3):
                    x = re[i][j] * re[i][k] + im[i][j] * im[i][k]
                    y = re[i][j] * im[i][k] - im[i][j] * re[i][k]
                    a = x if a is None else a + x
                    b = y if b is None else b + y
                return a, b

            k1, k2, k3 = diag(0), diag(1), diag(2)
            inverse = jnp.minimum(lax.rsqrt((scale * scale) * (k1 + k2 + k3)), 1.0)
            r = scale * inverse
            g = r * r
            a1, a2, a3 = g * k1, g * k2, g * k3
            b12 = tuple(g * v for v in off(0, 1))
            b13 = tuple(g * v for v in off(0, 2))
            b23 = tuple(g * v for v in off(1, 2))

            def norm(v):
                return v[0] * v[0] + v[1] * v[1]

            def times(a, b):
                return a[0] * b[0] - a[1] * b[1], a[0] * b[1] + a[1] * b[0]

            def ctimes(a, b):
                return a[0] * b[0] + a[1] * b[1], a[1] * b[0] - a[0] * b[1]

            j1 = a2 * a3 - norm(b23)
            j2 = a1 * a3 - norm(b13)
            j3 = a1 * a2 - norm(b12)
            q = ctimes(b13, b23)
            j12 = (q[0] - a3 * b12[0], q[1] - a3 * b12[1])
            q = times(b12, b23)
            j13 = (q[0] - a2 * b13[0], q[1] - a2 * b13[1])
            q = ctimes(b13, b12)
            j23 = (q[0] - a1 * b23[0], q[1] - a1 * b23[1])
            e1 = a1 + a2 + a3
            e2 = j1 + j2 + j3
            e3 = (
                a1 * j1
                + (b12[0] * j12[0] + b12[1] * j12[1])
                + (b13[0] * j13[0] + b13[1] * j13[1])
            )

            def reduce(d0, d1, d2, d3, d4):
                d3 = d3 + e1 * d4
                d2 = d2 - e2 * d4 + e1 * d3
                d1 = d1 + e3 * d4 - e2 * d3
                return d0 + e3 * d3, d1, d2

            h = (0.25 * e3, 2.25 - 0.25 * e2, 0.25 * e1 - 1.5)
            p = None
            for k in range(1, NEWTON):
                y = (1.5 - 0.5 * h[0], -0.5 * h[1], -0.5 * h[2])
                if p is None:
                    d3 = -0.5 * y[2]
                    p = (
                        1.5 * y[0] + e3 * d3,
                        1.5 * y[1] - 0.5 * y[0] - e2 * d3,
                        1.5 * y[2] - 0.5 * y[1] + e1 * d3,
                    )
                else:
                    p = reduce(
                        p[0] * y[0],
                        p[0] * y[1] + p[1] * y[0],
                        p[0] * y[2] + p[1] * y[1] + p[2] * y[0],
                        p[1] * y[2] + p[2] * y[1],
                        p[2] * y[2],
                    )
                if k < NEWTON - 1:
                    twice = p[0] + p[0]
                    f = reduce(
                        p[0] * p[0],
                        twice * p[1],
                        twice * p[2] + p[1] * p[1],
                        (p[1] + p[1]) * p[2],
                        p[2] * p[2],
                    )
                    h = (e3 * f[2], f[0] - e2 * f[2], f[1] + e1 * f[2])

            c2 = r * p[2]
            c1 = r * p[1] + e1 * c2
            c0 = r * p[0] - e2 * c2

            def entry(b, j):
                return c1 * b[0] + c2 * j[0], c1 * b[1] + c2 * j[1]

            m12, m13, m23 = entry(b12, j12), entry(b13, j13), entry(b23, j23)
            dg = [c0 + c1 * a + c2 * j for a, j in ((a1, j1), (a2, j2), (a3, j3))]
            table = {(0, 1): m12, (0, 2): m13, (1, 2): m23}
            for i in range(3):
                for j in range(3):
                    x = re[i][j] * dg[j]
                    y = im[i][j] * dg[j]
                    for k in range(3):
                        if k == j:
                            continue
                        vr, vi = table[(min(k, j), max(k, j))]
                        ur, ui = re[i][k], im[i][k]
                        if k < j:
                            x = x + ur * vr - ui * vi
                            y = y + ur * vi + ui * vr
                        else:
                            x = x + ur * vr + ui * vi
                            y = y - ur * vi + ui * vr
                    U[w + 1, 1 + s, m, 0, i, j] = x
                    U[w + 1, 1 + s, m, 1, i, j] = y
        for s in range(2):
            acc[m, s] = 9.0 * U[w + 1, 1 + s, m]

    sub = lax.broadcasted_iota(jnp.int32, (3, 3, 8, LANES), 2)
    eye = (
        lax.broadcasted_iota(jnp.int32, (3, 3, 8, LANES), 0)
        == lax.broadcasted_iota(jnp.int32, (3, 3, 8, LANES), 1)
    ).astype(jnp.float32)
    one = (eye, jnp.zeros_like(eye))
    lower = core == 0
    sibling = dev(1 - 2 * core, 0)

    def pick(cond, a, b):
        return tuple(jnp.where(cond, x, y) for x, y in zip(a, b))

    def chain_copy(slot, src, dst, d):
        return pltpu.make_async_remote_copy(
            src_ref=src,
            dst_ref=dst,
            send_sem=cs.at[slot],
            recv_sem=cr.at[slot],
            device_id=d,
            device_id_type=MESH,
        )

    def rows(ref, first, count):
        return ref.at[:, :, :, pl.ds(first, count), :]

    def to_sibling():
        return chain_copy(0, Q.at[0], SQ, sibling)

    def half_to(k):
        return chain_copy(k, rows(Q.at[1], 0, 4), rows(CQ.at[k - 1], 0, 4), dev(2 * k, 0))

    def column_to(k, h):
        return chain_copy(
            2 + 2 * k + h, rows(Q.at[2], 4 * h, 1), rows(CQ.at[k - 1], 4 + h, 1), dev(2 * k, -1)
        )

    def column_own(h):
        return chain_copy(10 + h, rows(Q.at[0], 4 * h, 1), rows(XQ, 4 * h + 3, 1), dev(1, -1))

    def entering_to_sibling():
        return chain_copy(12, rows(Q.at[3], 0, 4), rows(EH, 4, 4), sibling)

    def chain_start():
        q = mm(ld(U, 2, 1, 0), ld(U, 2, 2, 0))
        Q[0, 0] = q[0]
        Q[0, 1] = q[1]
        to_sibling().start()

        @pl.when(lower)
        def _():
            for h in range(2):
                column_own(h).start()

    def chain_middle():
        to_sibling().wait_recv()
        mine, other = ld(Q, 0), (SQ[0], SQ[1])
        q = mm(pick(lower, mine, other), pick(lower, other, mine))
        for c in range(2):
            Q[2, c] = q[c]
            Q[1, c] = jnp.where(lower, q[c], sroll(q[c], 4))
        for k in (1, 3, 2):

            @pl.when(chip + k < 4)
            def _():
                half_to(k).start()
                for h in range(2):
                    column_to(k, h).start()

    def sweep_start(w):
        plane_yz(w)
        for m in (2, 3):
            plane_t(w, m, 1)

    def sweep_time(w):
        for m in (2, 3):
            plane_t(w, m, 2)
            plane_t_before(w, m)

    def wait_time(w):
        for m in range(4):
            up(w, m).wait_recv()
            if m != 0:
                down(w, m).wait_recv()

    def wait_x(w):
        for m in range(4):
            right(w, m).wait_recv()
            if m != 1:
                left(w, m).wait_recv()

    sweep_start(0)
    first_down().wait_recv()
    then_right().start()
    first_up().wait_recv()
    then_left().start()
    wait_time(0)
    for m in range(4):
        third_face(0, m)
        if m != 0:
            third_face(3, m)
    sweep_time(0)
    wait_x(0)
    for m in range(4):
        third_cols(CH, m)
        if m != 1:
            third_cols(XH, m)
    for m in (2, 3):
        plane_x(0, m)
    then_left().wait_recv()
    then_right().wait_recv()
    third_cols(XH, 1)
    third_cols(CH, 4)
    plane_tx(0)
    for m in range(4):
        unitarise(0, m)
        pack(1, m)
        if m == 0:
            corner_up(1).start()
        if m == 1:
            corner_down(1).start()
        right(1, m).start()
        if m != 1:
            left(1, m).start()
        up(1, m).start()
        if m != 0:
            down(1, m).start()

    sweep_start(1)
    wait_time(1)
    sweep_time(1)
    wait_x(1)
    corner_up(1).wait_recv()
    corner_down(1).wait_recv()
    plane_tx(1)
    unitarise(1, 0)
    chain_start()
    pack(2, 0)
    left(2, 0).start()
    for m in (2, 3):
        plane_x(1, m)
    chain_middle()
    for m in (1, 2, 3):
        unitarise(1, m)

    for k in (1, 2, 3):

        @pl.when(chip >= k)
        def _():
            half_to(k).wait_recv()
            for h in range(2):
                column_to(k, h).wait_recv()

    run = pick(chip >= 3, ld(CQ, 2), one)
    run = pick(chip >= 2, mm(run, ld(CQ, 1)), one)
    run = pick(chip >= 1, mm(run, ld(CQ, 0)), one)
    for c in range(2):
        Q[3, c] = run[c]
    entering_to_sibling().start()
    gh1 = tuple(jnp.where(sub < 4, sroll(v, -1), sroll(v, 2)) for v in run)

    @pl.when(core == 1)
    def _():
        for h in range(2):
            chain_copy(10 + h, rows(Q.at[0], 4 * h, 1), rows(XQ, 4 * h + 3, 1), dev(1, -1)).wait_recv()

    gh1 = pick(lower, gh1, mm(gh1, (XQ[0], XQ[1])))
    left(2, 0).wait_recv()
    halo = XH[2, 0]
    gh2 = mm(gh1, tuple(sroll(halo, 3 - 2 * q) for q in range(2)))
    entering_to_sibling().wait_recv()
    whole = tuple(jnp.where(sub < 4, v, EH[c]) for c, v in enumerate(run))
    whole = pick(lower, whole, each(lambda v: sroll(v, 4), whole))
    g1 = pick(lower, whole, mm(whole, (SQ[0], SQ[1])))
    g2 = mm(g1, ld(U, 2, 1, 0))
    g3 = mm(g2, ld(U, 2, 2, 0))
    gs = (g1, g2)

    def store(m, s, pair):
        OUT[m, 0, :, :, s] = pair[0]
        OUT[m, 1, :, :, s] = pair[1]

    def save(m, t, h):
        return pltpu.make_async_copy(
            OUT.at[m, :, :, :, t, pl.ds(4 * h, 4), :],
            o_ref.at[m, :, :, :, t, :, pl.ds(h * LANES, LANES)],
            io.at[4 * m + 2 * t + h],
        )

    def save_all(m):
        for t in range(2):
            for h in range(2):
                save(m, t, h).start()

    store(0, 0, mm(g2, g2, db=True))
    store(0, 1, mm(g3, g3, db=True))
    save_all(0)
    for m in (2, 3):
        for s in range(2):
            store(m, s, mm(mm(gs[s], ld(U, 2, 1 + s, m)), yz_shift(gs[s], m, 1), db=True))
        save_all(m)
    for s, gh in ((0, gh1), (1, gh2)):
        gx_next = tuple(jnp.where(row4 == 3, a, sroll(b, -1)) for a, b in zip(gh, gs[s]))
        store(1, s, mm(mm(gs[s], ld(U, 2, 1 + s, 1)), gx_next, db=True))
    save_all(1)

    for w in range(2):
        for m in range(4):
            if m != 0:
                down(w, m).wait_send()
            up(w, m).wait_send()
            if m != 1:
                left(w, m).wait_send()
            right(w, m).wait_send()
        if w == 1:
            corner_up(w).wait_send()
            corner_down(w).wait_send()
    first_up().wait_send()
    first_down().wait_send()
    then_left().wait_send()
    then_right().wait_send()
    left(2, 0).wait_send()
    to_sibling().wait_send()
    entering_to_sibling().wait_send()

    @pl.when(lower)
    def _():
        for h in range(2):
            column_own(h).wait_send()

    for k in (1, 2, 3):

        @pl.when(chip + k < 4)
        def _():
            half_to(k).wait_send()
            for h in range(2):
                column_to(k, h).wait_send()

    for m in range(4):
        for t in range(2):
            for h in range(2):
                save(m, t, h).wait()


def body(gauge_links):
    field = (2, 3, 3, 8, LANES)
    f32 = jnp.float32
    return pl.pallas_call(
        kernel,
        out_shape=jax.ShapeDtypeStruct(gauge_links.shape, f32),
        in_specs=[pl.BlockSpec(memory_space=pltpu.HBM)],
        out_specs=pl.BlockSpec(memory_space=pl.ANY),
        scratch_shapes=[
            pltpu.VMEM((3, 4, 4) + field, f32),
            pltpu.VMEM((3, 4) + field[1:], f32),
            pltpu.VMEM((2, 5) + field[1:], f32),
            pltpu.VMEM((3, 4) + field[1:], f32),
            pltpu.VMEM((3, 4) + field[1:], f32),
            pltpu.VMEM((2, 2) + field[2:], f32),
            pltpu.VMEM((4, 2) + field, f32),
            pltpu.VMEM((4,) + field, f32),
            pltpu.VMEM(field, f32),
            pltpu.VMEM((3,) + field, f32),
            pltpu.VMEM(field, f32),
            pltpu.VMEM(field, f32),
            pltpu.VMEM((4, 2, 3, 3, 2, 8, LANES), f32),
            pltpu.SemaphoreType.DMA((3, 20)),
            pltpu.SemaphoreType.DMA((3, 20)),
            pltpu.SemaphoreType.DMA((13,)),
            pltpu.SemaphoreType.DMA((13,)),
            pltpu.SemaphoreType.DMA((16,)),
        ],
        compiler_params=pltpu.CompilerParams(
            collective_id=0, has_side_effects=True, vmem_limit_bytes=32 * 2**20
        ),
    )(gauge_links)


def solution(mesh):
    spec = P(None, None, None, None, "ta", "gx", None)
    return jax.shard_map(body, mesh=mesh, in_specs=(spec,), out_specs=spec, check_vma=False)
```

```python
import functools

import jax
import jax.numpy as jnp
from jax import lax
from jax.experimental import pallas as pl
from jax.experimental.pallas import tpu as pltpu
from jax.sharding import PartitionSpec as P

MESH = pl.DeviceIdType.MESH
NZ = 16
NEWTON = 5
ape_weight = 0.4
LANES = 128


def mm(a, b, da=False, db=False):
    def left(c):
        return tuple(q[c, :, None] if da else q[:, c, None] for q in a)

    def right(c):
        return tuple(q[None, :, c] if db else q[None, c] for q in b)

    re = im = None
    for c in range(3):
        lr, li = left(c)
        rr, ri = right(c)
        x, y = lr * rr, li * ri
        u, v = lr * ri, li * rr
        re = x if re is None else re + x
        re = re + y if da != db else re - y
        if im is None:
            if da and db:
                im = -u - v
            elif da:
                im = u - v
            elif db:
                im = v - u
            else:
                im = u + v
        else:
            im = im - u if db else im + u
            im = im - v if da else im + v
    return re, im


def lane_of(shape):
    return lax.broadcasted_iota(jnp.int32, shape, len(shape) - 1)


def each(f, pair):
    return tuple(f(q) for q in pair)


def sroll(v, shift):
    shift = shift % 8
    if shift == 0:
        return v
    flat = v.reshape((9, 8, LANES))
    return pltpu.roll(flat, shift, 1).reshape(v.shape)


def lroll(v, shift):
    return pltpu.roll(v.reshape((72, LANES)), shift % LANES, 1).reshape(v.shape)


def yz_shift(pair, m, sign):
    lane = lane_of((3, 3, 8, LANES))
    z = lax.rem(lane, NZ)
    if isinstance(m, int):
        if m == 2:

            def move(v):
                r = lroll(v, -NZ * sign)
                stay = lane < LANES - NZ if sign > 0 else lane >= NZ
                return jnp.where(stay, r, sroll(r, 4))

        else:

            def move(v):
                stay = z < NZ - 1 if sign > 0 else z >= 1
                return jnp.where(stay, lroll(v, -sign), lroll(v, sign * (NZ - 1)))

        return each(move, pair)
    raise NotImplementedError


def kernel(
    x_ref, o_ref, U, XH, CH, PK0, PK3, RL, acc, KT, Q, SQ, CQ, EH, XQ, OUT, hs, hr, cs, cr, io
):
    ta = lax.axis_index("ta")
    gx = lax.axis_index("gx")
    nta = lax.axis_size("ta")
    ngx = lax.axis_size("gx")
    core, chip = lax.rem(ta, 2), ta // 2

    def dev(dt, dg):
        return {"ta": lax.rem(ta + dt + nta, nta), "gx": lax.rem(gx + dg + ngx, ngx)}

    barrier = pltpu.get_barrier_semaphore()
    for d in (dev(0, 1), dev(0, -1), dev(4, 0), dev(1, 0), dev(-1, 0)):
        pl.semaphore_signal(barrier, inc=1, device_id=d, device_id_type=MESH)

    loads = []
    for t in range(2):
        for h in range(2):
            c = pltpu.make_async_copy(
                x_ref.at[:, :, :, :, t, :, pl.ds(h * LANES, LANES)],
                U.at[0, 1 + t, :, :, :, :, pl.ds(4 * h, 4), :],
                io.at[2 * t + h],
            )
            c.start()
            loads.append(c)

    def ld(ref, *at):
        v = ref[at]
        return v[0], v[1]

    def add(m, s, pair):
        acc[m, s, 0] = acc[m, s, 0] + pair[0]
        acc[m, s, 1] = acc[m, s, 1] + pair[1]

    row4 = lax.rem(lax.broadcasted_iota(jnp.int32, (3, 3, 8, LANES), 2), 4)

    def pack(w, m):
        parts = [U[w, 1, m, 0], U[w, 2, m, 0], U[w, 1, m, 1], U[w, 2, m, 1]]
        for col, out in ((0, PK0), (3, PK3)):
            moved = [sroll(v, q - col) for q, v in enumerate(parts)]
            out[w, m] = jnp.where(
                row4 < 2,
                jnp.where(row4 == 0, moved[0], moved[1]),
                jnp.where(row4 == 2, moved[2], moved[3]),
            )

    def x_next(pair, halo, t):
        return tuple(
            jnp.where(row4 == 3, sroll(halo, 3 - t - 2 * q), sroll(v, -1))
            for q, v in enumerate(pair)
        )

    def x_prev(pair, column, t):
        return tuple(
            jnp.where(row4 == 0, sroll(c, -t), sroll(v, 1)) for v, c in zip(pair, column)
        )

    def unpacked(v):
        return v, sroll(v, -2)

    def copy(w, slot, src, dst, d):
        return pltpu.make_async_remote_copy(
            src_ref=src,
            dst_ref=dst,
            send_sem=hs.at[w, slot],
            recv_sem=hr.at[w, slot],
            device_id=d,
            device_id_type=MESH,
        )

    def face(w, s, m):
        return U.at[w, s, m, :, pl.ds(0, 2)] if w == 0 else U.at[w, s, m]

    def cols(ref, w, m):
        return ref.at[w, m, pl.ds(0, 2)] if w == 0 else ref.at[w, m]

    def down(w, m):
        return copy(w, m, face(w, 1, m), face(w, 3, m), dev(-1, 0))

    def up(w, m):
        return copy(w, 4 + m, face(w, 2, m), face(w, 0, m), dev(1, 0))

    def left(w, m):
        return copy(w, 8 + m, cols(PK0, w, m), cols(XH, w, m), dev(0, -1))

    def right(w, m):
        return copy(w, 12 + m, cols(PK3, w, m), cols(CH, w, m), dev(0, 1))

    def corner_up(w):
        return copy(w, 16, cols(PK0, w, 0), cols(XH, w, 1), dev(1, -1))

    def corner_down(w):
        return copy(w, 17, cols(PK3, w, 1), cols(CH, w, 4), dev(-1, 1))

    def first_up():
        return copy(0, 18, cols(PK0, 0, 0), RL.at[0], dev(1, 0))

    def first_down():
        return copy(0, 19, cols(PK3, 0, 1), RL.at[1], dev(-1, 0))

    def then_left():
        return copy(0, 16, RL.at[0], cols(XH, 0, 1), dev(0, -1))

    def then_right():
        return copy(0, 17, RL.at[1], cols(CH, 0, 4), dev(0, 1))

    def cross(a, b):
        out = []
        for j in range(3):
            (pr, pi), (qr, qi) = a[(j + 1) % 3], b[(j + 2) % 3]
            (tr, ti), (ur, ui) = a[(j + 2) % 3], b[(j + 1) % 3]
            out.append((pr * qr - pi * qi - tr * ur + ti * ui, tr * ui + ti * ur - pr * qi - pi * qr))
        return out

    def third_face(s, m):
        rows = [[(U[0, s, m, 0, i, j], U[0, s, m, 1, i, j]) for j in range(3)] for i in range(2)]
        for j, (re, im) in enumerate(cross(*rows)):
            U[0, s, m, 0, 2, j] = re
            U[0, s, m, 1, 2, j] = im

    quad = lax.rem(lax.broadcasted_iota(jnp.int32, (8, LANES), 0), 4)

    def third_cols(ref, m):
        rows = [
            [(ref[0, m, i, j], pltpu.roll(ref[0, m, i, j], 6, 0)) for j in range(3)] for i in range(2)
        ]
        for j, (re, im) in enumerate(cross(*rows)):
            ref[0, m, 2, j] = jnp.where(quad < 2, re, pltpu.roll(im, 2, 0))

    for c in loads:
        c.wait()

    @pl.loop(0, 4)
    def _(m):
        pack(0, m)
        for s in range(2):
            acc[m, s] = 9.0 * U[0, 1 + s, m]

    pl.semaphore_wait(barrier, 5)
    first_down().start()
    first_up().start()
    for m in (1, 0, 2, 3):
        right(0, m).start()
        if m != 1:
            left(0, m).start()
    for m in range(4):
        up(0, m).start()
        if m != 0:
            down(0, m).start()

    def plane_yz(w):
        for s in (1, 2):
            uy, uz = ld(U, w, s, 2), ld(U, w, s, 3)
            uyz, uzy = yz_shift(uy, 3, 1), yz_shift(uz, 2, 1)
            p1, p2 = mm(uy, uzy), mm(uz, uyz)
            add(2, s - 1, mm(p2, uzy, db=True))
            add(3, s - 1, mm(p1, uyz, db=True))
            add(2, s - 1, yz_shift(mm(uz, p1, da=True), 3, -1))
            add(3, s - 1, yz_shift(mm(uy, p2, da=True), 2, -1))

    def plane_t(w, m, s):
        ut, um, umt = ld(U, w, s, 0), ld(U, w, s, m), ld(U, w, s + 1, m)
        utm = yz_shift(ut, m, 1)
        p1, p2 = mm(ut, umt), mm(um, utm)
        add(0, s - 1, mm(p2, umt, db=True))
        add(m, s - 1, mm(p1, utm, db=True))
        add(0, s - 1, yz_shift(mm(um, p1, da=True), m, -1))
        if s == 1:
            add(m, 1, mm(ut, p2, da=True))

    def plane_t_before(w, m):
        ut, um = ld(U, w, 0, 0), ld(U, w, 0, m)
        p2 = mm(um, yz_shift(ut, m, 1))
        add(m, 0, mm(ut, p2, da=True))

    def keep(slot, pair):
        KT[slot, 0] = pair[0]
        KT[slot, 1] = pair[1]

    def tx_local(w):
        for s in (1, 2):
            ut, ux, uxt = ld(U, w, s, 0), ld(U, w, s, 1), ld(U, w, s + 1, 1)
            p1 = mm(ut, uxt)
            keep(s - 1, p1)
            keep(s + 1, mm(ux, p1, da=True))

    def tx_upper(w):
        for s in (1, 2):
            ux, uxt = ld(U, w, s, 1), ld(U, w, s + 1, 1)
            utx = x_next(ld(U, w, s, 0), XH[w, 0], s - 1)
            p2 = mm(ux, utx)
            keep(s + 3, utx)
            add(0, s - 1, mm(p2, uxt, db=True))
            if s == 1:
                keep(6, p2)

    def tx_lower(w):
        cx_re, cx_im = unpacked(CH[w, 1])
        far_re, far_im = unpacked(CH[w, 4])
        cx = (cx_re, cx_im)
        cxt = tuple(
            jnp.where(row4 == 0, sroll(v, -1), sroll(f, 1)) for v, f in ((cx_re, far_re), (cx_im, far_im))
        )
        ct = unpacked(CH[w, 0])
        lower_c = mm(cx, mm(ct, cxt), da=True)
        for s in range(2):
            add(0, s, x_prev(ld(KT, 2 + s), lower_c, s))

    def tx_side(w):
        for s in range(2):
            add(1, s, mm(ld(KT, s), ld(KT, 4 + s), db=True))
        add(1, 1, mm(ld(U, w, 1, 0), ld(KT, 6), da=True))

    def tx_before(w):
        ut = ld(U, w, 0, 0)
        p2 = mm(ld(U, w, 0, 1), x_next(ut, XH[w, 1], 1))
        add(1, 0, mm(ut, p2, da=True))

    def plane_x(w, m):
        cx, cm = unpacked(CH[w, 1]), unpacked(CH[w, m])
        lower_c = mm(cx, mm(cm, yz_shift(cx, m, 1)), da=True)
        for s in (1, 2):
            ux, um = ld(U, w, s, 1), ld(U, w, s, m)
            umx = x_next(um, XH[w, m], s - 1)
            uxm = yz_shift(ux, m, 1)
            p1, p2 = mm(ux, umx), mm(um, uxm)
            add(1, s - 1, mm(p2, umx, db=True))
            add(m, s - 1, mm(p1, uxm, db=True))
            add(1, s - 1, yz_shift(mm(um, p1, da=True), m, -1))
            add(m, s - 1, x_prev(mm(ux, p2, da=True), lower_c, s - 1))

    def unitarise(w, m):
        scale = ape_weight / 6.0
        for s in range(2):
            re = [[acc[m, s, 0, i, j] for j in range(3)] for i in range(3)]
            im = [[acc[m, s, 1, i, j] for j in range(3)] for i in range(3)]

            def diag(j):
                t = None
                for i in range(3):
                    q = re[i][j] * re[i][j] + im[i][j] * im[i][j]
                    t = q if t is None else t + q
                return t

            def off(j, k):
                a = b = None
                for i in range(3):
                    x = re[i][j] * re[i][k] + im[i][j] * im[i][k]
                    y = re[i][j] * im[i][k] - im[i][j] * re[i][k]
                    a = x if a is None else a + x
                    b = y if b is None else b + y
                return a, b

            k1, k2, k3 = diag(0), diag(1), diag(2)
            inverse = jnp.minimum(lax.rsqrt((scale * scale) * (k1 + k2 + k3)), 1.0)
            r = scale * inverse
            g = r * r
            a1, a2, a3 = g * k1, g * k2, g * k3
            b12 = tuple(g * v for v in off(0, 1))
            b13 = tuple(g * v for v in off(0, 2))
            b23 = tuple(g * v for v in off(1, 2))

            def norm(v):
                return v[0] * v[0] + v[1] * v[1]

            def times(a, b):
                return a[0] * b[0] - a[1] * b[1], a[0] * b[1] + a[1] * b[0]

            def ctimes(a, b):
                return a[0] * b[0] + a[1] * b[1], a[1] * b[0] - a[0] * b[1]

            j1 = a2 * a3 - norm(b23)
            j2 = a1 * a3 - norm(b13)
            j3 = a1 * a2 - norm(b12)
            q = ctimes(b13, b23)
            j12 = (q[0] - a3 * b12[0], q[1] - a3 * b12[1])
            q = times(b12, b23)
            j13 = (q[0] - a2 * b13[0], q[1] - a2 * b13[1])
            q = ctimes(b13, b12)
            j23 = (q[0] - a1 * b23[0], q[1] - a1 * b23[1])
            e1 = a1 + a2 + a3
            e2 = j1 + j2 + j3
            e3 = (
                a1 * j1
                + (b12[0] * j12[0] + b12[1] * j12[1])
                + (b13[0] * j13[0] + b13[1] * j13[1])
            )

            def reduce(d0, d1, d2, d3, d4):
                d3 = d3 + e1 * d4
                d2 = d2 - e2 * d4 + e1 * d3
                d1 = d1 + e3 * d4 - e2 * d3
                return d0 + e3 * d3, d1, d2

            h = (0.25 * e3, 2.25 - 0.25 * e2, 0.25 * e1 - 1.5)
            p = None
            for k in range(1, NEWTON):
                y = (1.5 - 0.5 * h[0], -0.5 * h[1], -0.5 * h[2])
                if p is None:
                    d3 = -0.5 * y[2]
                    p = (
                        1.5 * y[0] + e3 * d3,
                        1.5 * y[1] - 0.5 * y[0] - e2 * d3,
                        1.5 * y[2] - 0.5 * y[1] + e1 * d3,
                    )
                else:
                    p = reduce(
                        p[0] * y[0],
                        p[0] * y[1] + p[1] * y[0],
                        p[0] * y[2] + p[1] * y[1] + p[2] * y[0],
                        p[1] * y[2] + p[2] * y[1],
                        p[2] * y[2],
                    )
                if k < NEWTON - 1:
                    twice = p[0] + p[0]
                    f = reduce(
                        p[0] * p[0],
                        twice * p[1],
                        twice * p[2] + p[1] * p[1],
                        (p[1] + p[1]) * p[2],
                        p[2] * p[2],
                    )
                    h = (e3 * f[2], f[0] - e2 * f[2], f[1] + e1 * f[2])

            c2 = r * p[2]
            c1 = r * p[1] + e1 * c2
            c0 = r * p[0] - e2 * c2

            def entry(b, j):
                return c1 * b[0] + c2 * j[0], c1 * b[1] + c2 * j[1]

            m12, m13, m23 = entry(b12, j12), entry(b13, j13), entry(b23, j23)
            dg = [c0 + c1 * a + c2 * j for a, j in ((a1, j1), (a2, j2), (a3, j3))]
            table = {(0, 1): m12, (0, 2): m13, (1, 2): m23}
            for i in range(3):
                for j in range(3):
                    x = re[i][j] * dg[j]
                    y = im[i][j] * dg[j]
                    for k in range(3):
                        if k == j:
                            continue
                        vr, vi = table[(min(k, j), max(k, j))]
                        ur, ui = re[i][k], im[i][k]
                        if k < j:
                            x = x + ur * vr - ui * vi
                            y = y + ur * vi + ui * vr
                        else:
                            x = x + ur * vr + ui * vi
                            y = y - ur * vi + ui * vr
                    U[w + 1, 1 + s, m, 0, i, j] = x
                    U[w + 1, 1 + s, m, 1, i, j] = y
        for s in range(2):
            acc[m, s] = 9.0 * U[w + 1, 1 + s, m]

    sub = lax.broadcasted_iota(jnp.int32, (3, 3, 8, LANES), 2)
    eye = (
        lax.broadcasted_iota(jnp.int32, (3, 3, 8, LANES), 0)
        == lax.broadcasted_iota(jnp.int32, (3, 3, 8, LANES), 1)
    ).astype(jnp.float32)
    one = (eye, jnp.zeros_like(eye))
    lower = core == 0
    sibling = dev(1 - 2 * core, 0)

    def pick(cond, a, b):
        return tuple(jnp.where(cond, x, y) for x, y in zip(a, b))

    def chain_copy(slot, src, dst, d):
        return pltpu.make_async_remote_copy(
            src_ref=src,
            dst_ref=dst,
            send_sem=cs.at[slot],
            recv_sem=cr.at[slot],
            device_id=d,
            device_id_type=MESH,
        )

    def rows(ref, first, count):
        return ref.at[:, :, :, pl.ds(first, count), :]

    def to_sibling():
        return chain_copy(0, Q.at[0], SQ, sibling)

    def half_to(k):
        return chain_copy(k, rows(Q.at[1], 0, 4), rows(CQ.at[k - 1], 0, 4), dev(2 * k, 0))

    def column_to(k, h):
        return chain_copy(
            2 + 2 * k + h, rows(Q.at[2], 4 * h, 1), rows(CQ.at[k - 1], 4 + h, 1), dev(2 * k, -1)
        )

    def column_own(h):
        return chain_copy(10 + h, rows(Q.at[0], 4 * h, 1), rows(XQ, 4 * h + 3, 1), dev(1, -1))

    def entering_to_sibling():
        return chain_copy(12, rows(Q.at[3], 0, 4), rows(EH, 4, 4), sibling)

    def chain_start():
        q = mm(ld(U, 2, 1, 0), ld(U, 2, 2, 0))
        Q[0, 0] = q[0]
        Q[0, 1] = q[1]
        to_sibling().start()

        @pl.when(lower)
        def _():
            for h in range(2):
                column_own(h).start()

    def chain_middle():
        to_sibling().wait_recv()
        mine, other = ld(Q, 0), (SQ[0], SQ[1])
        q = mm(pick(lower, mine, other), pick(lower, other, mine))
        for c in range(2):
            Q[2, c] = q[c]
            Q[1, c] = jnp.where(lower, q[c], sroll(q[c], 4))
        for k in (2, 3, 1):

            @pl.when(chip + k < 4)
            def _():
                half_to(k).start()

        for k in (2, 3, 1):

            @pl.when(chip + k < 4)
            def _():
                for h in range(2):
                    column_to(k, h).start()

    def sweep_start(w):
        plane_yz(w)
        for m in (2, 3):
            plane_t(w, m, 1)

    def sweep_time(w):
        for m in (2, 3):
            plane_t(w, m, 2)
            plane_t_before(w, m)

    def wait_time(w):
        for m in range(4):
            up(w, m).wait_recv()
            if m != 0:
                down(w, m).wait_recv()

    def wait_x(w):
        for m in range(4):
            right(w, m).wait_recv()
            if m != 1:
                left(w, m).wait_recv()

    sweep_start(0)
    first_down().wait_recv()
    then_right().start()
    first_up().wait_recv()
    then_left().start()
    wait_time(0)
    for m in range(4):
        third_face(0, m)
        if m != 0:
            third_face(3, m)
    sweep_time(0)
    tx_local(0)
    wait_x(0)
    for m in range(4):
        third_cols(CH, m)
        if m != 1:
            third_cols(XH, m)
    for m in (2, 3):
        plane_x(0, m)

    def finish(m):
        unitarise(0, m)
        pack(1, m)
        if m == 1:
            corner_down(1).start()
        right(1, m).start()
        if m != 1:
            left(1, m).start()
        if m == 0:
            corner_up(1).start()
        up(1, m).start()
        if m != 0:
            down(1, m).start()

    finish(2)
    finish(3)
    tx_upper(0)
    tx_side(0)
    then_left().wait_recv()
    third_cols(XH, 1)
    tx_before(0)
    finish(1)
    then_right().wait_recv()
    third_cols(CH, 4)
    tx_lower(0)
    finish(0)

    sweep_start(1)
    wait_time(1)
    sweep_time(1)
    tx_local(1)
    wait_x(1)
    tx_upper(1)
    corner_down(1).wait_recv()
    tx_lower(1)
    unitarise(1, 0)
    chain_start()
    pack(2, 0)
    left(2, 0).start()
    tx_side(1)
    for m in (2, 3):
        plane_x(1, m)
    chain_middle()
    corner_up(1).wait_recv()
    tx_before(1)
    for m in (1, 2, 3):
        unitarise(1, m)

    for k in (1, 2, 3):

        @pl.when(chip >= k)
        def _():
            half_to(k).wait_recv()
            for h in range(2):
                column_to(k, h).wait_recv()

    run = pick(chip >= 3, ld(CQ, 2), one)
    run = pick(chip >= 2, mm(run, ld(CQ, 1)), one)
    run = pick(chip >= 1, mm(run, ld(CQ, 0)), one)
    for c in range(2):
        Q[3, c] = run[c]
    entering_to_sibling().start()
    gh1 = tuple(jnp.where(sub < 4, sroll(v, -1), sroll(v, 2)) for v in run)

    @pl.when(core == 1)
    def _():
        for h in range(2):
            chain_copy(10 + h, rows(Q.at[0], 4 * h, 1), rows(XQ, 4 * h + 3, 1), dev(1, -1)).wait_recv()

    gh1 = pick(lower, gh1, mm(gh1, (XQ[0], XQ[1])))
    left(2, 0).wait_recv()
    halo = XH[2, 0]
    gh2 = mm(gh1, tuple(sroll(halo, 3 - 2 * q) for q in range(2)))
    entering_to_sibling().wait_recv()
    whole = tuple(jnp.where(sub < 4, v, EH[c]) for c, v in enumerate(run))
    whole = pick(lower, whole, each(lambda v: sroll(v, 4), whole))
    g1 = pick(lower, whole, mm(whole, (SQ[0], SQ[1])))
    g2 = mm(g1, ld(U, 2, 1, 0))
    g3 = mm(g2, ld(U, 2, 2, 0))
    gs = (g1, g2)

    def store(m, s, pair):
        OUT[m, 0, :, :, s] = pair[0]
        OUT[m, 1, :, :, s] = pair[1]

    def save(m, t, h):
        return pltpu.make_async_copy(
            OUT.at[m, :, :, :, t, pl.ds(4 * h, 4), :],
            o_ref.at[m, :, :, :, t, :, pl.ds(h * LANES, LANES)],
            io.at[4 * m + 2 * t + h],
        )

    def save_all(m):
        for t in range(2):
            for h in range(2):
                save(m, t, h).start()

    store(0, 0, mm(g2, g2, db=True))
    store(0, 1, mm(g3, g3, db=True))
    save_all(0)
    for m in (2, 3):
        for s in range(2):
            store(m, s, mm(mm(gs[s], ld(U, 2, 1 + s, m)), yz_shift(gs[s], m, 1), db=True))
        save_all(m)
    for s, gh in ((0, gh1), (1, gh2)):
        gx_next = tuple(jnp.where(row4 == 3, a, sroll(b, -1)) for a, b in zip(gh, gs[s]))
        store(1, s, mm(mm(gs[s], ld(U, 2, 1 + s, 1)), gx_next, db=True))
    save_all(1)

    for w in range(2):
        for m in range(4):
            if m != 0:
                down(w, m).wait_send()
            up(w, m).wait_send()
            if m != 1:
                left(w, m).wait_send()
            right(w, m).wait_send()
        if w == 1:
            corner_up(w).wait_send()
            corner_down(w).wait_send()
    first_up().wait_send()
    first_down().wait_send()
    then_left().wait_send()
    then_right().wait_send()
    left(2, 0).wait_send()
    to_sibling().wait_send()
    entering_to_sibling().wait_send()

    @pl.when(lower)
    def _():
        for h in range(2):
            column_own(h).wait_send()

    for k in (1, 2, 3):

        @pl.when(chip + k < 4)
        def _():
            half_to(k).wait_send()
            for h in range(2):
                column_to(k, h).wait_send()

    for m in range(4):
        for t in range(2):
            for h in range(2):
                save(m, t, h).wait()


def body(gauge_links):
    field = (2, 3, 3, 8, LANES)
    f32 = jnp.float32
    return pl.pallas_call(
        kernel,
        out_shape=jax.ShapeDtypeStruct(gauge_links.shape, f32),
        in_specs=[pl.BlockSpec(memory_space=pltpu.HBM)],
        out_specs=pl.BlockSpec(memory_space=pl.ANY),
        scratch_shapes=[
            pltpu.VMEM((3, 4, 4) + field, f32),
            pltpu.VMEM((3, 4) + field[1:], f32),
            pltpu.VMEM((2, 5) + field[1:], f32),
            pltpu.VMEM((3, 4) + field[1:], f32),
            pltpu.VMEM((3, 4) + field[1:], f32),
            pltpu.VMEM((2, 2) + field[2:], f32),
            pltpu.VMEM((4, 2) + field, f32),
            pltpu.VMEM((7,) + field, f32),
            pltpu.VMEM((4,) + field, f32),
            pltpu.VMEM(field, f32),
            pltpu.VMEM((3,) + field, f32),
            pltpu.VMEM(field, f32),
            pltpu.VMEM(field, f32),
            pltpu.VMEM((4, 2, 3, 3, 2, 8, LANES), f32),
            pltpu.SemaphoreType.DMA((3, 20)),
            pltpu.SemaphoreType.DMA((3, 20)),
            pltpu.SemaphoreType.DMA((13,)),
            pltpu.SemaphoreType.DMA((13,)),
            pltpu.SemaphoreType.DMA((16,)),
        ],
        compiler_params=pltpu.CompilerParams(
            collective_id=0, has_side_effects=True, vmem_limit_bytes=32 * 2**20
        ),
    )(pltpu.with_memory_space_constraint(gauge_links, pltpu.HBM))


def solution(mesh):
    spec = P(None, None, None, None, "ta", "gx", None)
    return jax.shard_map(body, mesh=mesh, in_specs=(spec,), out_specs=spec, check_vma=False)
```

```python
import functools

import jax
import jax.numpy as jnp
from jax import lax
from jax.experimental import pallas as pl
from jax.experimental.pallas import tpu as pltpu
from jax.sharding import PartitionSpec as P

MESH = pl.DeviceIdType.MESH
NZ = 16
NEWTON = 5
ape_weight = 0.4
LANES = 128


def mm(a, b, da=False, db=False):
    def left(c):
        return tuple(q[c, :, None] if da else q[:, c, None] for q in a)

    def right(c):
        return tuple(q[None, :, c] if db else q[None, c] for q in b)

    re = im = None
    for c in range(3):
        lr, li = left(c)
        rr, ri = right(c)
        x, y = lr * rr, li * ri
        u, v = lr * ri, li * rr
        re = x if re is None else re + x
        re = re + y if da != db else re - y
        if im is None:
            if da and db:
                im = -u - v
            elif da:
                im = u - v
            elif db:
                im = v - u
            else:
                im = u + v
        else:
            im = im - u if db else im + u
            im = im - v if da else im + v
    return re, im


def lane_of(shape):
    return lax.broadcasted_iota(jnp.int32, shape, len(shape) - 1)


def each(f, pair):
    return tuple(f(q) for q in pair)


def sroll(v, shift):
    shift = shift % 8
    if shift == 0:
        return v
    flat = v.reshape((9, 8, LANES))
    return pltpu.roll(flat, shift, 1).reshape(v.shape)


def lroll(v, shift):
    return pltpu.roll(v.reshape((72, LANES)), shift % LANES, 1).reshape(v.shape)


def yz_shift(pair, m, sign):
    lane = lane_of((3, 3, 8, LANES))
    z = lax.rem(lane, NZ)
    if isinstance(m, int):
        if m == 2:

            def move(v):
                r = lroll(v, -NZ * sign)
                stay = lane < LANES - NZ if sign > 0 else lane >= NZ
                return jnp.where(stay, r, sroll(r, 4))

        else:

            def move(v):
                stay = z < NZ - 1 if sign > 0 else z >= 1
                return jnp.where(stay, lroll(v, -sign), lroll(v, sign * (NZ - 1)))

        return each(move, pair)
    raise NotImplementedError


def kernel(
    x_ref, o_ref, U, XH, CH, PK0, PK3, RL, acc, KT, Q, SQ, CQ, EH, XQ, OUT, hs, hr, cs, cr, io
):
    ta = lax.axis_index("ta")
    gx = lax.axis_index("gx")
    nta = lax.axis_size("ta")
    ngx = lax.axis_size("gx")
    core, chip = lax.rem(ta, 2), ta // 2

    def dev(dt, dg):
        return {"ta": lax.rem(ta + dt + nta, nta), "gx": lax.rem(gx + dg + ngx, ngx)}

    barrier = pltpu.get_barrier_semaphore()
    for d in (dev(0, 1), dev(0, -1), dev(4, 0), dev(1, 0), dev(-1, 0)):
        pl.semaphore_signal(barrier, inc=1, device_id=d, device_id_type=MESH)

    loads = []
    for t in range(2):
        for h in range(2):
            c = pltpu.make_async_copy(
                x_ref.at[:, :, :, :, t, :, pl.ds(h * LANES, LANES)],
                U.at[0, 1 + t, :, :, :, :, pl.ds(4 * h, 4), :],
                io.at[2 * t + h],
            )
            c.start()
            loads.append(c)

    def ld(ref, *at):
        v = ref[at]
        return v[0], v[1]

    def add(m, s, pair):
        acc[m, s, 0] = acc[m, s, 0] + pair[0]
        acc[m, s, 1] = acc[m, s, 1] + pair[1]

    row4 = lax.rem(lax.broadcasted_iota(jnp.int32, (3, 3, 8, LANES), 2), 4)

    def pack(w, m):
        parts = [U[w, 1, m, 0], U[w, 2, m, 0], U[w, 1, m, 1], U[w, 2, m, 1]]
        for col, out in ((0, PK0), (3, PK3)):
            moved = [sroll(v, q - col) for q, v in enumerate(parts)]
            out[w, m] = jnp.where(
                row4 < 2,
                jnp.where(row4 == 0, moved[0], moved[1]),
                jnp.where(row4 == 2, moved[2], moved[3]),
            )

    def x_next(pair, halo, t):
        return tuple(
            jnp.where(row4 == 3, sroll(halo, 3 - t - 2 * q), sroll(v, -1))
            for q, v in enumerate(pair)
        )

    def x_prev(pair, column, t):
        return tuple(
            jnp.where(row4 == 0, sroll(c, -t), sroll(v, 1)) for v, c in zip(pair, column)
        )

    def unpacked(v):
        return v, sroll(v, -2)

    def copy(w, slot, src, dst, d):
        return pltpu.make_async_remote_copy(
            src_ref=src,
            dst_ref=dst,
            send_sem=hs.at[w, slot],
            recv_sem=hr.at[w, slot],
            device_id=d,
            device_id_type=MESH,
        )

    def face(w, s, m):
        return U.at[w, s, m, :, pl.ds(0, 2)] if w == 0 else U.at[w, s, m]

    def cols(ref, w, m):
        return ref.at[w, m, pl.ds(0, 2)] if w == 0 else ref.at[w, m]

    def down(w, m):
        return copy(w, m, face(w, 1, m), face(w, 3, m), dev(-1, 0))

    def up(w, m):
        return copy(w, 4 + m, face(w, 2, m), face(w, 0, m), dev(1, 0))

    def left(w, m):
        return copy(w, 8 + m, cols(PK0, w, m), cols(XH, w, m), dev(0, -1))

    def right(w, m):
        return copy(w, 12 + m, cols(PK3, w, m), cols(CH, w, m), dev(0, 1))

    def corner_up(w):
        return copy(w, 16, cols(PK0, w, 0), cols(XH, w, 1), dev(1, -1))

    def corner_down(w):
        return copy(w, 17, cols(PK3, w, 1), cols(CH, w, 4), dev(-1, 1))

    def up_all():
        return copy(0, 4, U.at[0, 2, :, :, pl.ds(0, 2)], U.at[0, 0, :, :, pl.ds(0, 2)], dev(1, 0))

    def down_all():
        links = pl.ds(1, 3)
        return copy(
            0, 1, U.at[0, 1, links, :, pl.ds(0, 2)], U.at[0, 3, links, :, pl.ds(0, 2)], dev(-1, 0)
        )

    def left_yz():
        links = pl.ds(2, 2)
        return copy(0, 10, PK0.at[0, links, pl.ds(0, 2)], XH.at[0, links, pl.ds(0, 2)], dev(0, -1))

    def right_xyz():
        links = pl.ds(1, 3)
        return copy(0, 13, PK3.at[0, links, pl.ds(0, 2)], CH.at[0, links, pl.ds(0, 2)], dev(0, 1))

    def first_up():
        return copy(0, 18, cols(PK0, 0, 0), RL.at[0], dev(1, 0))

    def first_down():
        return copy(0, 19, cols(PK3, 0, 1), RL.at[1], dev(-1, 0))

    def then_left():
        return copy(0, 16, RL.at[0], cols(XH, 0, 1), dev(0, -1))

    def then_right():
        return copy(0, 17, RL.at[1], cols(CH, 0, 4), dev(0, 1))

    def cross(a, b):
        out = []
        for j in range(3):
            (pr, pi), (qr, qi) = a[(j + 1) % 3], b[(j + 2) % 3]
            (tr, ti), (ur, ui) = a[(j + 2) % 3], b[(j + 1) % 3]
            out.append((pr * qr - pi * qi - tr * ur + ti * ui, tr * ui + ti * ur - pr * qi - pi * qr))
        return out

    def third_face(s, m):
        rows = [[(U[0, s, m, 0, i, j], U[0, s, m, 1, i, j]) for j in range(3)] for i in range(2)]
        for j, (re, im) in enumerate(cross(*rows)):
            U[0, s, m, 0, 2, j] = re
            U[0, s, m, 1, 2, j] = im

    quad = lax.rem(lax.broadcasted_iota(jnp.int32, (8, LANES), 0), 4)

    def third_cols(ref, m):
        rows = [
            [(ref[0, m, i, j], pltpu.roll(ref[0, m, i, j], 6, 0)) for j in range(3)] for i in range(2)
        ]
        for j, (re, im) in enumerate(cross(*rows)):
            ref[0, m, 2, j] = jnp.where(quad < 2, re, pltpu.roll(im, 2, 0))

    for c in loads:
        c.wait()

    @pl.loop(0, 4)
    def _(m):
        pack(0, m)
        for s in range(2):
            acc[m, s] = 9.0 * U[0, 1 + s, m]

    pl.semaphore_wait(barrier, 5)
    first_down().start()
    first_up().start()
    right_xyz().start()
    left_yz().start()
    right(0, 0).start()
    left(0, 0).start()
    up_all().start()
    down_all().start()

    def plane_yz(w):
        for s in (1, 2):
            uy, uz = ld(U, w, s, 2), ld(U, w, s, 3)
            uyz, uzy = yz_shift(uy, 3, 1), yz_shift(uz, 2, 1)
            p1, p2 = mm(uy, uzy), mm(uz, uyz)
            add(2, s - 1, mm(p2, uzy, db=True))
            add(3, s - 1, mm(p1, uyz, db=True))
            add(2, s - 1, yz_shift(mm(uz, p1, da=True), 3, -1))
            add(3, s - 1, yz_shift(mm(uy, p2, da=True), 2, -1))

    def plane_t(w, m, s):
        ut, um, umt = ld(U, w, s, 0), ld(U, w, s, m), ld(U, w, s + 1, m)
        utm = yz_shift(ut, m, 1)
        p1, p2 = mm(ut, umt), mm(um, utm)
        add(0, s - 1, mm(p2, umt, db=True))
        add(m, s - 1, mm(p1, utm, db=True))
        add(0, s - 1, yz_shift(mm(um, p1, da=True), m, -1))
        if s == 1:
            add(m, 1, mm(ut, p2, da=True))

    def plane_t_before(w, m):
        ut, um = ld(U, w, 0, 0), ld(U, w, 0, m)
        p2 = mm(um, yz_shift(ut, m, 1))
        add(m, 0, mm(ut, p2, da=True))

    def keep(slot, pair):
        KT[slot, 0] = pair[0]
        KT[slot, 1] = pair[1]

    def tx_local(w):
        for s in (1, 2):
            ut, ux, uxt = ld(U, w, s, 0), ld(U, w, s, 1), ld(U, w, s + 1, 1)
            p1 = mm(ut, uxt)
            keep(s - 1, p1)
            keep(s + 1, mm(ux, p1, da=True))

    def tx_upper(w):
        for s in (1, 2):
            ux, uxt = ld(U, w, s, 1), ld(U, w, s + 1, 1)
            utx = x_next(ld(U, w, s, 0), XH[w, 0], s - 1)
            p2 = mm(ux, utx)
            keep(s + 3, utx)
            add(0, s - 1, mm(p2, uxt, db=True))
            if s == 1:
                keep(6, p2)

    def tx_lower(w):
        cx_re, cx_im = unpacked(CH[w, 1])
        far_re, far_im = unpacked(CH[w, 4])
        cx = (cx_re, cx_im)
        cxt = tuple(
            jnp.where(row4 == 0, sroll(v, -1), sroll(f, 1)) for v, f in ((cx_re, far_re), (cx_im, far_im))
        )
        ct = unpacked(CH[w, 0])
        lower_c = mm(cx, mm(ct, cxt), da=True)
        for s in range(2):
            add(0, s, x_prev(ld(KT, 2 + s), lower_c, s))

    def tx_side(w):
        for s in range(2):
            add(1, s, mm(ld(KT, s), ld(KT, 4 + s), db=True))
        add(1, 1, mm(ld(U, w, 1, 0), ld(KT, 6), da=True))

    def tx_before(w):
        ut = ld(U, w, 0, 0)
        p2 = mm(ld(U, w, 0, 1), x_next(ut, XH[w, 1], 1))
        add(1, 0, mm(ut, p2, da=True))

    def plane_x(w, m):
        cx, cm = unpacked(CH[w, 1]), unpacked(CH[w, m])
        lower_c = mm(cx, mm(cm, yz_shift(cx, m, 1)), da=True)
        for s in (1, 2):
            ux, um = ld(U, w, s, 1), ld(U, w, s, m)
            umx = x_next(um, XH[w, m], s - 1)
            uxm = yz_shift(ux, m, 1)
            p1, p2 = mm(ux, umx), mm(um, uxm)
            add(1, s - 1, mm(p2, umx, db=True))
            add(m, s - 1, mm(p1, uxm, db=True))
            add(1, s - 1, yz_shift(mm(um, p1, da=True), m, -1))
            add(m, s - 1, x_prev(mm(ux, p2, da=True), lower_c, s - 1))

    def unitarise(w, m):
        scale = ape_weight / 6.0
        for s in range(2):
            re = [[acc[m, s, 0, i, j] for j in range(3)] for i in range(3)]
            im = [[acc[m, s, 1, i, j] for j in range(3)] for i in range(3)]

            def diag(j):
                t = None
                for i in range(3):
                    q = re[i][j] * re[i][j] + im[i][j] * im[i][j]
                    t = q if t is None else t + q
                return t

            def off(j, k):
                a = b = None
                for i in range(3):
                    x = re[i][j] * re[i][k] + im[i][j] * im[i][k]
                    y = re[i][j] * im[i][k] - im[i][j] * re[i][k]
                    a = x if a is None else a + x
                    b = y if b is None else b + y
                return a, b

            k1, k2, k3 = diag(0), diag(1), diag(2)
            inverse = jnp.minimum(lax.rsqrt((scale * scale) * (k1 + k2 + k3)), 1.0)
            r = scale * inverse
            g = r * r
            a1, a2, a3 = g * k1, g * k2, g * k3
            b12 = tuple(g * v for v in off(0, 1))
            b13 = tuple(g * v for v in off(0, 2))
            b23 = tuple(g * v for v in off(1, 2))

            def norm(v):
                return v[0] * v[0] + v[1] * v[1]

            def times(a, b):
                return a[0] * b[0] - a[1] * b[1], a[0] * b[1] + a[1] * b[0]

            def ctimes(a, b):
                return a[0] * b[0] + a[1] * b[1], a[1] * b[0] - a[0] * b[1]

            j1 = a2 * a3 - norm(b23)
            j2 = a1 * a3 - norm(b13)
            j3 = a1 * a2 - norm(b12)
            q = ctimes(b13, b23)
            j12 = (q[0] - a3 * b12[0], q[1] - a3 * b12[1])
            q = times(b12, b23)
            j13 = (q[0] - a2 * b13[0], q[1] - a2 * b13[1])
            q = ctimes(b13, b12)
            j23 = (q[0] - a1 * b23[0], q[1] - a1 * b23[1])
            e1 = a1 + a2 + a3
            e2 = j1 + j2 + j3
            e3 = (
                a1 * j1
                + (b12[0] * j12[0] + b12[1] * j12[1])
                + (b13[0] * j13[0] + b13[1] * j13[1])
            )

            def reduce(d0, d1, d2, d3, d4):
                d3 = d3 + e1 * d4
                d2 = d2 - e2 * d4 + e1 * d3
                d1 = d1 + e3 * d4 - e2 * d3
                return d0 + e3 * d3, d1, d2

            h = (0.25 * e3, 2.25 - 0.25 * e2, 0.25 * e1 - 1.5)
            p = None
            for k in range(1, NEWTON):
                y = (1.5 - 0.5 * h[0], -0.5 * h[1], -0.5 * h[2])
                if p is None:
                    d3 = -0.5 * y[2]
                    p = (
                        1.5 * y[0] + e3 * d3,
                        1.5 * y[1] - 0.5 * y[0] - e2 * d3,
                        1.5 * y[2] - 0.5 * y[1] + e1 * d3,
                    )
                else:
                    p = reduce(
                        p[0] * y[0],
                        p[0] * y[1] + p[1] * y[0],
                        p[0] * y[2] + p[1] * y[1] + p[2] * y[0],
                        p[1] * y[2] + p[2] * y[1],
                        p[2] * y[2],
                    )
                if k < NEWTON - 1:
                    twice = p[0] + p[0]
                    f = reduce(
                        p[0] * p[0],
                        twice * p[1],
                        twice * p[2] + p[1] * p[1],
                        (p[1] + p[1]) * p[2],
                        p[2] * p[2],
                    )
                    h = (e3 * f[2], f[0] - e2 * f[2], f[1] + e1 * f[2])

            c2 = r * p[2]
            c1 = r * p[1] + e1 * c2
            c0 = r * p[0] - e2 * c2

            def entry(b, j):
                return c1 * b[0] + c2 * j[0], c1 * b[1] + c2 * j[1]

            m12, m13, m23 = entry(b12, j12), entry(b13, j13), entry(b23, j23)
            dg = [c0 + c1 * a + c2 * j for a, j in ((a1, j1), (a2, j2), (a3, j3))]
            table = {(0, 1): m12, (0, 2): m13, (1, 2): m23}
            for i in range(3):
                for j in range(3):
                    x = re[i][j] * dg[j]
                    y = im[i][j] * dg[j]
                    for k in range(3):
                        if k == j:
                            continue
                        vr, vi = table[(min(k, j), max(k, j))]
                        ur, ui = re[i][k], im[i][k]
                        if k < j:
                            x = x + ur * vr - ui * vi
                            y = y + ur * vi + ui * vr
                        else:
                            x = x + ur * vr + ui * vi
                            y = y - ur * vi + ui * vr
                    U[w + 1, 1 + s, m, 0, i, j] = x
                    U[w + 1, 1 + s, m, 1, i, j] = y
        for s in range(2):
            acc[m, s] = 9.0 * U[w + 1, 1 + s, m]

    sub = lax.broadcasted_iota(jnp.int32, (3, 3, 8, LANES), 2)
    eye = (
        lax.broadcasted_iota(jnp.int32, (3, 3, 8, LANES), 0)
        == lax.broadcasted_iota(jnp.int32, (3, 3, 8, LANES), 1)
    ).astype(jnp.float32)
    one = (eye, jnp.zeros_like(eye))
    lower = core == 0
    sibling = dev(1 - 2 * core, 0)

    def pick(cond, a, b):
        return tuple(jnp.where(cond, x, y) for x, y in zip(a, b))

    def chain_copy(slot, src, dst, d):
        return pltpu.make_async_remote_copy(
            src_ref=src,
            dst_ref=dst,
            send_sem=cs.at[slot],
            recv_sem=cr.at[slot],
            device_id=d,
            device_id_type=MESH,
        )

    def rows(ref, first, count):
        return ref.at[:, :, :, pl.ds(first, count), :]

    def to_sibling():
        return chain_copy(0, Q.at[0], SQ, sibling)

    def half_to(k):
        return chain_copy(k, rows(Q.at[1], 0, 4), rows(CQ.at[k - 1], 0, 4), dev(2 * k, 0))

    def column_to(k, h):
        return chain_copy(
            2 + 2 * k + h, rows(Q.at[2], 4 * h, 1), rows(CQ.at[k - 1], 4 + h, 1), dev(2 * k, -1)
        )

    def column_own(h):
        return chain_copy(10 + h, rows(Q.at[0], 4 * h, 1), rows(XQ, 4 * h + 3, 1), dev(1, -1))

    def entering_to_sibling():
        return chain_copy(12, rows(Q.at[3], 0, 4), rows(EH, 4, 4), sibling)

    def chain_start():
        q = mm(ld(U, 2, 1, 0), ld(U, 2, 2, 0))
        Q[0, 0] = q[0]
        Q[0, 1] = q[1]
        to_sibling().start()

        @pl.when(lower)
        def _():
            for h in range(2):
                column_own(h).start()

    def chain_middle():
        to_sibling().wait_recv()
        mine, other = ld(Q, 0), (SQ[0], SQ[1])
        q = mm(pick(lower, mine, other), pick(lower, other, mine))
        for c in range(2):
            Q[2, c] = q[c]
            Q[1, c] = jnp.where(lower, q[c], sroll(q[c], 4))
        for k in (2, 3, 1):

            @pl.when(chip + k < 4)
            def _():
                half_to(k).start()

        for k in (2, 3, 1):

            @pl.when(chip + k < 4)
            def _():
                for h in range(2):
                    column_to(k, h).start()

    def sweep_start(w):
        plane_yz(w)
        for m in (2, 3):
            plane_t(w, m, 1)

    def sweep_time(w):
        for m in (2, 3):
            plane_t(w, m, 2)
            plane_t_before(w, m)

    def wait_time(w):
        for m in range(4):
            up(w, m).wait_recv()
            if m != 0:
                down(w, m).wait_recv()

    sweep_start(0)
    first_down().wait_recv()
    then_right().start()
    first_up().wait_recv()
    then_left().start()
    up_all().wait_recv()
    down_all().wait_recv()
    for m in range(4):
        third_face(0, m)
        if m != 0:
            third_face(3, m)
    sweep_time(0)
    tx_local(0)
    right_xyz().wait_recv()
    left_yz().wait_recv()
    third_cols(CH, 1)
    for m in (2, 3):
        third_cols(CH, m)
        third_cols(XH, m)
        plane_x(0, m)

    def arrived(m):
        right(1, m).wait_recv()
        if m != 1:
            left(1, m).wait_recv()

    def finish(m):
        unitarise(0, m)
        pack(1, m)
        if m == 1:
            corner_down(1).start()
        right(1, m).start()
        if m != 1:
            left(1, m).start()
        if m == 0:
            corner_up(1).start()
        up(1, m).start()
        if m != 0:
            down(1, m).start()

    finish(2)
    finish(3)
    right(0, 0).wait_recv()
    left(0, 0).wait_recv()
    third_cols(CH, 0)
    third_cols(XH, 0)
    tx_upper(0)
    tx_side(0)
    then_right().wait_recv()
    third_cols(CH, 4)
    tx_lower(0)
    finish(0)
    then_left().wait_recv()
    third_cols(XH, 1)
    tx_before(0)
    finish(1)

    sweep_start(1)
    wait_time(1)
    sweep_time(1)
    tx_local(1)
    arrived(0)
    arrived(1)
    tx_upper(1)
    corner_down(1).wait_recv()
    tx_lower(1)
    unitarise(1, 0)
    chain_start()
    pack(2, 0)
    left(2, 0).start()
    tx_side(1)
    for m in (2, 3):
        arrived(m)
        plane_x(1, m)
    chain_middle()
    corner_up(1).wait_recv()
    tx_before(1)
    for m in (1, 2, 3):
        unitarise(1, m)

    for c in (up_all, down_all, left_yz, right_xyz, first_up, first_down, then_left, then_right):
        c().wait_send()
    right(0, 0).wait_send()
    left(0, 0).wait_send()
    for m in range(4):
        if m != 0:
            down(1, m).wait_send()
        up(1, m).wait_send()
        if m != 1:
            left(1, m).wait_send()
        right(1, m).wait_send()
    corner_up(1).wait_send()
    corner_down(1).wait_send()
    left(2, 0).wait_send()

    for k in (1, 2, 3):

        @pl.when(chip >= k)
        def _():
            half_to(k).wait_recv()
            for h in range(2):
                column_to(k, h).wait_recv()

    run = pick(chip >= 3, ld(CQ, 2), one)
    run = pick(chip >= 2, mm(run, ld(CQ, 1)), one)
    run = pick(chip >= 1, mm(run, ld(CQ, 0)), one)
    for c in range(2):
        Q[3, c] = run[c]
    entering_to_sibling().start()
    gh1 = tuple(jnp.where(sub < 4, sroll(v, -1), sroll(v, 2)) for v in run)

    @pl.when(core == 1)
    def _():
        for h in range(2):
            chain_copy(10 + h, rows(Q.at[0], 4 * h, 1), rows(XQ, 4 * h + 3, 1), dev(1, -1)).wait_recv()

    gh1 = pick(lower, gh1, mm(gh1, (XQ[0], XQ[1])))
    left(2, 0).wait_recv()
    halo = XH[2, 0]
    gh2 = mm(gh1, tuple(sroll(halo, 3 - 2 * q) for q in range(2)))
    entering_to_sibling().wait_recv()
    whole = tuple(jnp.where(sub < 4, v, EH[c]) for c, v in enumerate(run))
    whole = pick(lower, whole, each(lambda v: sroll(v, 4), whole))
    g1 = pick(lower, whole, mm(whole, (SQ[0], SQ[1])))
    g2 = mm(g1, ld(U, 2, 1, 0))
    g3 = mm(g2, ld(U, 2, 2, 0))
    gs = (g1, g2)

    def store(m, s, pair):
        OUT[m, 0, :, :, s] = pair[0]
        OUT[m, 1, :, :, s] = pair[1]

    def save(m, h):
        return pltpu.make_async_copy(
            OUT.at[m, :, :, :, :, pl.ds(4 * h, 4), :],
            o_ref.at[m, :, :, :, :, :, pl.ds(h * LANES, LANES)],
            io.at[4 + 2 * m + h],
        )

    def save_all(m):
        for h in range(2):
            save(m, h).start()

    store(0, 0, mm(g2, g2, db=True))
    store(0, 1, mm(g3, g3, db=True))
    save_all(0)
    for m in (2, 3):
        for s in range(2):
            store(m, s, mm(mm(gs[s], ld(U, 2, 1 + s, m)), yz_shift(gs[s], m, 1), db=True))
        save_all(m)
    for s, gh in ((0, gh1), (1, gh2)):
        gx_next = tuple(jnp.where(row4 == 3, a, sroll(b, -1)) for a, b in zip(gh, gs[s]))
        store(1, s, mm(mm(gs[s], ld(U, 2, 1 + s, 1)), gx_next, db=True))
    save_all(1)

    to_sibling().wait_send()
    entering_to_sibling().wait_send()

    @pl.when(lower)
    def _():
        for h in range(2):
            column_own(h).wait_send()

    for k in (1, 2, 3):

        @pl.when(chip + k < 4)
        def _():
            half_to(k).wait_send()
            for h in range(2):
                column_to(k, h).wait_send()

    for m in range(4):
        for h in range(2):
            save(m, h).wait()


def body(gauge_links):
    field = (2, 3, 3, 8, LANES)
    f32 = jnp.float32
    return pl.pallas_call(
        kernel,
        out_shape=jax.ShapeDtypeStruct(gauge_links.shape, f32),
        in_specs=[pl.BlockSpec(memory_space=pltpu.HBM)],
        out_specs=pl.BlockSpec(memory_space=pl.ANY),
        scratch_shapes=[
            pltpu.VMEM((3, 4, 4) + field, f32),
            pltpu.VMEM((3, 4) + field[1:], f32),
            pltpu.VMEM((2, 5) + field[1:], f32),
            pltpu.VMEM((3, 4) + field[1:], f32),
            pltpu.VMEM((3, 4) + field[1:], f32),
            pltpu.VMEM((2, 2) + field[2:], f32),
            pltpu.VMEM((4, 2) + field, f32),
            pltpu.VMEM((7,) + field, f32),
            pltpu.VMEM((4,) + field, f32),
            pltpu.VMEM(field, f32),
            pltpu.VMEM((3,) + field, f32),
            pltpu.VMEM(field, f32),
            pltpu.VMEM(field, f32),
            pltpu.VMEM((4, 2, 3, 3, 2, 8, LANES), f32),
            pltpu.SemaphoreType.DMA((3, 20)),
            pltpu.SemaphoreType.DMA((3, 20)),
            pltpu.SemaphoreType.DMA((13,)),
            pltpu.SemaphoreType.DMA((13,)),
            pltpu.SemaphoreType.DMA((16,)),
        ],
        compiler_params=pltpu.CompilerParams(
            collective_id=0, has_side_effects=True, vmem_limit_bytes=32 * 2**20
        ),
    )(pltpu.with_memory_space_constraint(gauge_links, pltpu.HBM))


def solution(mesh):
    spec = P(None, None, None, None, "ta", "gx", None)
    return jax.shard_map(body, mesh=mesh, in_specs=(spec,), out_specs=spec, check_vma=False)
```

```python
import functools

import jax
import jax.numpy as jnp
from jax import lax
from jax.experimental import pallas as pl
from jax.experimental.pallas import tpu as pltpu
from jax.sharding import PartitionSpec as P

MESH = pl.DeviceIdType.MESH
NZ = 16
NEWTON = 5
ape_weight = 0.4
LANES = 128


def mm(a, b, da=False, db=False):
    def left(c):
        return tuple(q[c, :, None] if da else q[:, c, None] for q in a)

    def right(c):
        return tuple(q[None, :, c] if db else q[None, c] for q in b)

    re = im = None
    for c in range(3):
        lr, li = left(c)
        rr, ri = right(c)
        x, y = lr * rr, li * ri
        u, v = lr * ri, li * rr
        re = x if re is None else re + x
        re = re + y if da != db else re - y
        if im is None:
            if da and db:
                im = -u - v
            elif da:
                im = u - v
            elif db:
                im = v - u
            else:
                im = u + v
        else:
            im = im - u if db else im + u
            im = im - v if da else im + v
    return re, im


def lane_of(shape):
    return lax.broadcasted_iota(jnp.int32, shape, len(shape) - 1)


def each(f, pair):
    return tuple(f(q) for q in pair)


def sroll(v, shift):
    shift = shift % 8
    if shift == 0:
        return v
    flat = v.reshape((9, 8, LANES))
    return pltpu.roll(flat, shift, 1).reshape(v.shape)


def lroll(v, shift):
    return pltpu.roll(v.reshape((72, LANES)), shift % LANES, 1).reshape(v.shape)


def yz_shift(pair, m, sign):
    lane = lane_of((3, 3, 8, LANES))
    z = lax.rem(lane, NZ)
    if isinstance(m, int):
        if m == 2:

            def move(v):
                r = lroll(v, -NZ * sign)
                stay = lane < LANES - NZ if sign > 0 else lane >= NZ
                return jnp.where(stay, r, sroll(r, 4))

        else:

            def move(v):
                stay = z < NZ - 1 if sign > 0 else z >= 1
                return jnp.where(stay, lroll(v, -sign), lroll(v, sign * (NZ - 1)))

        return each(move, pair)
    raise NotImplementedError


def kernel(
    x_ref, o_ref, U, XH, CH, PK0, PK3, RL, acc, KT, Q, SQ, CQ, EH, XQ, OUT, hs, hr, cs, cr, io
):
    ta = lax.axis_index("ta")
    gx = lax.axis_index("gx")
    nta = lax.axis_size("ta")
    ngx = lax.axis_size("gx")
    core, chip = lax.rem(ta, 2), ta // 2

    def dev(dt, dg):
        return {"ta": lax.rem(ta + dt + nta, nta), "gx": lax.rem(gx + dg + ngx, ngx)}

    barrier = pltpu.get_barrier_semaphore()
    for d in (dev(0, 1), dev(0, -1), dev(4, 0), dev(1, 0), dev(-1, 0)):
        pl.semaphore_signal(barrier, inc=1, device_id=d, device_id_type=MESH)

    loads = []
    for t in range(2):
        for h in range(2):
            c = pltpu.make_async_copy(
                x_ref.at[:, :, :, :, t, :, pl.ds(h * LANES, LANES)],
                U.at[0, 1 + t, :, :, :, :, pl.ds(4 * h, 4), :],
                io.at[2 * t + h],
            )
            c.start()
            loads.append(c)

    def ld(ref, *at):
        v = ref[at]
        return v[0], v[1]

    def add(m, s, pair):
        acc[m, s, 0] = acc[m, s, 0] + pair[0]
        acc[m, s, 1] = acc[m, s, 1] + pair[1]

    row4 = lax.rem(lax.broadcasted_iota(jnp.int32, (3, 3, 8, LANES), 2), 4)

    def pack(w, m):
        parts = [U[w, 1, m, 0], U[w, 2, m, 0], U[w, 1, m, 1], U[w, 2, m, 1]]
        for col, out in ((0, PK0), (3, PK3)):
            moved = [sroll(v, q - col) for q, v in enumerate(parts)]
            out[w, m] = jnp.where(
                row4 < 2,
                jnp.where(row4 == 0, moved[0], moved[1]),
                jnp.where(row4 == 2, moved[2], moved[3]),
            )

    def x_next(pair, halo, t):
        return tuple(
            jnp.where(row4 == 3, sroll(halo, 3 - t - 2 * q), sroll(v, -1))
            for q, v in enumerate(pair)
        )

    def x_prev(pair, column, t):
        return tuple(
            jnp.where(row4 == 0, sroll(c, -t), sroll(v, 1)) for v, c in zip(pair, column)
        )

    def unpacked(v):
        return v, sroll(v, -2)

    def copy(w, slot, src, dst, d):
        return pltpu.make_async_remote_copy(
            src_ref=src,
            dst_ref=dst,
            send_sem=hs.at[w, slot],
            recv_sem=hr.at[w, slot],
            device_id=d,
            device_id_type=MESH,
        )

    def face(w, s, m):
        return U.at[w, s, m, :, pl.ds(0, 2)] if w == 0 else U.at[w, s, m]

    def cols(ref, w, m):
        return ref.at[w, m, pl.ds(0, 2)] if w == 0 else ref.at[w, m]

    def down(w, m):
        return copy(w, m, face(w, 1, m), face(w, 3, m), dev(-1, 0))

    def up(w, m):
        return copy(w, 4 + m, face(w, 2, m), face(w, 0, m), dev(1, 0))

    def left(w, m):
        return copy(w, 8 + m, cols(PK0, w, m), cols(XH, w, m), dev(0, -1))

    def right(w, m):
        return copy(w, 12 + m, cols(PK3, w, m), cols(CH, w, m), dev(0, 1))

    def corner_up(w):
        return copy(w, 16, cols(PK0, w, 0), cols(XH, w, 1), dev(1, -1))

    def corner_down(w):
        return copy(w, 17, cols(PK3, w, 1), cols(CH, w, 4), dev(-1, 1))

    def up_all():
        return copy(0, 4, U.at[0, 2, :, :, pl.ds(0, 2)], U.at[0, 0, :, :, pl.ds(0, 2)], dev(1, 0))

    def down_all():
        links = pl.ds(1, 3)
        return copy(
            0, 1, U.at[0, 1, links, :, pl.ds(0, 2)], U.at[0, 3, links, :, pl.ds(0, 2)], dev(-1, 0)
        )

    def left_yz():
        links = pl.ds(2, 2)
        return copy(0, 10, PK0.at[0, links, pl.ds(0, 2)], XH.at[0, links, pl.ds(0, 2)], dev(0, -1))

    def right_xyz():
        links = pl.ds(1, 3)
        return copy(0, 13, PK3.at[0, links, pl.ds(0, 2)], CH.at[0, links, pl.ds(0, 2)], dev(0, 1))

    def first_up():
        return copy(0, 18, cols(PK0, 0, 0), RL.at[0], dev(1, 0))

    def first_down():
        return copy(0, 19, cols(PK3, 0, 1), RL.at[1], dev(-1, 0))

    def then_left():
        return copy(0, 16, RL.at[0], cols(XH, 0, 1), dev(0, -1))

    def then_right():
        return copy(0, 17, RL.at[1], cols(CH, 0, 4), dev(0, 1))

    def cross(a, b):
        out = []
        for j in range(3):
            (pr, pi), (qr, qi) = a[(j + 1) % 3], b[(j + 2) % 3]
            (tr, ti), (ur, ui) = a[(j + 2) % 3], b[(j + 1) % 3]
            out.append((pr * qr - pi * qi - tr * ur + ti * ui, tr * ui + ti * ur - pr * qi - pi * qr))
        return out

    def third_face(s, m):
        rows = [[(U[0, s, m, 0, i, j], U[0, s, m, 1, i, j]) for j in range(3)] for i in range(2)]
        for j, (re, im) in enumerate(cross(*rows)):
            U[0, s, m, 0, 2, j] = re
            U[0, s, m, 1, 2, j] = im

    quad = lax.rem(lax.broadcasted_iota(jnp.int32, (8, LANES), 0), 4)

    def third_cols(ref, m):
        rows = [
            [(ref[0, m, i, j], pltpu.roll(ref[0, m, i, j], 6, 0)) for j in range(3)] for i in range(2)
        ]
        for j, (re, im) in enumerate(cross(*rows)):
            ref[0, m, 2, j] = jnp.where(quad < 2, re, pltpu.roll(im, 2, 0))

    for c in loads:
        c.wait()

    @pl.loop(0, 4)
    def _(m):
        pack(0, m)
        for s in range(2):
            acc[m, s] = 9.0 * U[0, 1 + s, m]

    pl.semaphore_wait(barrier, 5)
    first_down().start()
    first_up().start()
    right_xyz().start()
    left_yz().start()
    right(0, 0).start()
    left(0, 0).start()
    up_all().start()
    down_all().start()

    def plane_yz(w):
        for s in (1, 2):
            uy, uz = ld(U, w, s, 2), ld(U, w, s, 3)
            uyz, uzy = yz_shift(uy, 3, 1), yz_shift(uz, 2, 1)
            p1, p2 = mm(uy, uzy), mm(uz, uyz)
            add(2, s - 1, mm(p2, uzy, db=True))
            add(3, s - 1, mm(p1, uyz, db=True))
            add(2, s - 1, yz_shift(mm(uz, p1, da=True), 3, -1))
            add(3, s - 1, yz_shift(mm(uy, p2, da=True), 2, -1))

    def keep(slot, pair):
        KT[slot, 0] = pair[0]
        KT[slot, 1] = pair[1]

    def local_t(w, m):
        keep(5 + m, mm(ld(U, w, 2, m), yz_shift(ld(U, w, 2, 0), m, 1)))

    def local_x(w, m):
        for s in (1, 2):
            ux, um = ld(U, w, s, 1), ld(U, w, s, m)
            p2 = mm(um, yz_shift(ux, m, 1))
            keep(5 + 2 * m + s, p2)
            keep(9 + 2 * m + s, mm(ux, p2, da=True))

    def plane_t(w, m, s):
        ut, um, umt = ld(U, w, s, 0), ld(U, w, s, m), ld(U, w, s + 1, m)
        utm = yz_shift(ut, m, 1)
        p1 = mm(ut, umt)
        p2 = mm(um, utm) if s == 1 else ld(KT, 5 + m)
        add(0, s - 1, mm(p2, umt, db=True))
        add(m, s - 1, mm(p1, utm, db=True))
        add(0, s - 1, yz_shift(mm(um, p1, da=True), m, -1))
        if s == 1:
            add(m, 1, mm(ut, p2, da=True))

    def plane_t_before(w, m):
        ut, um = ld(U, w, 0, 0), ld(U, w, 0, m)
        p2 = mm(um, yz_shift(ut, m, 1))
        add(m, 0, mm(ut, p2, da=True))

    def tx_local(w, s):
        ut, ux, uxt = ld(U, w, s, 0), ld(U, w, s, 1), ld(U, w, s + 1, 1)
        p1 = mm(ut, uxt)
        keep(s - 1, p1)
        keep(s + 1, mm(ux, p1, da=True))

    def tx_upper(w):
        for s in (1, 2):
            ux, uxt = ld(U, w, s, 1), ld(U, w, s + 1, 1)
            utx = x_next(ld(U, w, s, 0), XH[w, 0], s - 1)
            p2 = mm(ux, utx)
            keep(s + 3, utx)
            add(0, s - 1, mm(p2, uxt, db=True))
            if s == 1:
                keep(6, p2)

    def tx_lower(w):
        cx_re, cx_im = unpacked(CH[w, 1])
        far_re, far_im = unpacked(CH[w, 4])
        cx = (cx_re, cx_im)
        cxt = tuple(
            jnp.where(row4 == 0, sroll(v, -1), sroll(f, 1)) for v, f in ((cx_re, far_re), (cx_im, far_im))
        )
        ct = unpacked(CH[w, 0])
        lower_c = mm(cx, mm(ct, cxt), da=True)
        for s in range(2):
            add(0, s, x_prev(ld(KT, 2 + s), lower_c, s))

    def tx_side(w):
        for s in range(2):
            add(1, s, mm(ld(KT, s), ld(KT, 4 + s), db=True))
        add(1, 1, mm(ld(U, w, 1, 0), ld(KT, 6), da=True))

    def tx_before(w):
        ut = ld(U, w, 0, 0)
        p2 = mm(ld(U, w, 0, 1), x_next(ut, XH[w, 1], 1))
        add(1, 0, mm(ut, p2, da=True))

    def plane_x(w, m):
        cx, cm = unpacked(CH[w, 1]), unpacked(CH[w, m])
        lower_c = mm(cx, mm(cm, yz_shift(cx, m, 1)), da=True)
        for s in (1, 2):
            ux, um = ld(U, w, s, 1), ld(U, w, s, m)
            umx = x_next(um, XH[w, m], s - 1)
            uxm = yz_shift(ux, m, 1)
            p1, p2 = mm(ux, umx), ld(KT, 5 + 2 * m + s)
            add(1, s - 1, mm(p2, umx, db=True))
            add(m, s - 1, mm(p1, uxm, db=True))
            add(1, s - 1, yz_shift(mm(um, p1, da=True), m, -1))
            add(m, s - 1, x_prev(ld(KT, 9 + 2 * m + s), lower_c, s - 1))

    def unitarise(w, m):
        scale = ape_weight / 6.0
        for s in range(2):
            re = [[acc[m, s, 0, i, j] for j in range(3)] for i in range(3)]
            im = [[acc[m, s, 1, i, j] for j in range(3)] for i in range(3)]

            def diag(j):
                t = None
                for i in range(3):
                    q = re[i][j] * re[i][j] + im[i][j] * im[i][j]
                    t = q if t is None else t + q
                return t

            def off(j, k):
                a = b = None
                for i in range(3):
                    x = re[i][j] * re[i][k] + im[i][j] * im[i][k]
                    y = re[i][j] * im[i][k] - im[i][j] * re[i][k]
                    a = x if a is None else a + x
                    b = y if b is None else b + y
                return a, b

            k1, k2, k3 = diag(0), diag(1), diag(2)
            inverse = jnp.minimum(lax.rsqrt((scale * scale) * (k1 + k2 + k3)), 1.0)
            r = scale * inverse
            g = r * r
            a1, a2, a3 = g * k1, g * k2, g * k3
            b12 = tuple(g * v for v in off(0, 1))
            b13 = tuple(g * v for v in off(0, 2))
            b23 = tuple(g * v for v in off(1, 2))

            def norm(v):
                return v[0] * v[0] + v[1] * v[1]

            def times(a, b):
                return a[0] * b[0] - a[1] * b[1], a[0] * b[1] + a[1] * b[0]

            def ctimes(a, b):
                return a[0] * b[0] + a[1] * b[1], a[1] * b[0] - a[0] * b[1]

            j1 = a2 * a3 - norm(b23)
            j2 = a1 * a3 - norm(b13)
            j3 = a1 * a2 - norm(b12)
            q = ctimes(b13, b23)
            j12 = (q[0] - a3 * b12[0], q[1] - a3 * b12[1])
            q = times(b12, b23)
            j13 = (q[0] - a2 * b13[0], q[1] - a2 * b13[1])
            q = ctimes(b13, b12)
            j23 = (q[0] - a1 * b23[0], q[1] - a1 * b23[1])
            e1 = a1 + a2 + a3
            e2 = j1 + j2 + j3
            e3 = (
                a1 * j1
                + (b12[0] * j12[0] + b12[1] * j12[1])
                + (b13[0] * j13[0] + b13[1] * j13[1])
            )

            def reduce(d0, d1, d2, d3, d4):
                d3 = d3 + e1 * d4
                d2 = d2 - e2 * d4 + e1 * d3
                d1 = d1 + e3 * d4 - e2 * d3
                return d0 + e3 * d3, d1, d2

            h = (0.25 * e3, 2.25 - 0.25 * e2, 0.25 * e1 - 1.5)
            p = None
            for k in range(1, NEWTON):
                y = (1.5 - 0.5 * h[0], -0.5 * h[1], -0.5 * h[2])
                if p is None:
                    d3 = -0.5 * y[2]
                    p = (
                        1.5 * y[0] + e3 * d3,
                        1.5 * y[1] - 0.5 * y[0] - e2 * d3,
                        1.5 * y[2] - 0.5 * y[1] + e1 * d3,
                    )
                else:
                    p = reduce(
                        p[0] * y[0],
                        p[0] * y[1] + p[1] * y[0],
                        p[0] * y[2] + p[1] * y[1] + p[2] * y[0],
                        p[1] * y[2] + p[2] * y[1],
                        p[2] * y[2],
                    )
                if k < NEWTON - 1:
                    twice = p[0] + p[0]
                    f = reduce(
                        p[0] * p[0],
                        twice * p[1],
                        twice * p[2] + p[1] * p[1],
                        (p[1] + p[1]) * p[2],
                        p[2] * p[2],
                    )
                    h = (e3 * f[2], f[0] - e2 * f[2], f[1] + e1 * f[2])

            c2 = r * p[2]
            c1 = r * p[1] + e1 * c2
            c0 = r * p[0] - e2 * c2

            def entry(b, j):
                return c1 * b[0] + c2 * j[0], c1 * b[1] + c2 * j[1]

            m12, m13, m23 = entry(b12, j12), entry(b13, j13), entry(b23, j23)
            dg = [c0 + c1 * a + c2 * j for a, j in ((a1, j1), (a2, j2), (a3, j3))]
            table = {(0, 1): m12, (0, 2): m13, (1, 2): m23}
            for i in range(3):
                for j in range(3):
                    x = re[i][j] * dg[j]
                    y = im[i][j] * dg[j]
                    for k in range(3):
                        if k == j:
                            continue
                        vr, vi = table[(min(k, j), max(k, j))]
                        ur, ui = re[i][k], im[i][k]
                        if k < j:
                            x = x + ur * vr - ui * vi
                            y = y + ur * vi + ui * vr
                        else:
                            x = x + ur * vr + ui * vi
                            y = y - ur * vi + ui * vr
                    U[w + 1, 1 + s, m, 0, i, j] = x
                    U[w + 1, 1 + s, m, 1, i, j] = y
        for s in range(2):
            acc[m, s] = 9.0 * U[w + 1, 1 + s, m]

    sub = lax.broadcasted_iota(jnp.int32, (3, 3, 8, LANES), 2)
    eye = (
        lax.broadcasted_iota(jnp.int32, (3, 3, 8, LANES), 0)
        == lax.broadcasted_iota(jnp.int32, (3, 3, 8, LANES), 1)
    ).astype(jnp.float32)
    one = (eye, jnp.zeros_like(eye))
    lower = core == 0
    sibling = dev(1 - 2 * core, 0)

    def pick(cond, a, b):
        return tuple(jnp.where(cond, x, y) for x, y in zip(a, b))

    def chain_copy(slot, src, dst, d):
        return pltpu.make_async_remote_copy(
            src_ref=src,
            dst_ref=dst,
            send_sem=cs.at[slot],
            recv_sem=cr.at[slot],
            device_id=d,
            device_id_type=MESH,
        )

    def rows(ref, first, count):
        return ref.at[:, :, :, pl.ds(first, count), :]

    def to_sibling():
        return chain_copy(0, Q.at[0], SQ, sibling)

    def half_to(k):
        return chain_copy(k, rows(Q.at[1], 0, 4), rows(CQ.at[k - 1], 0, 4), dev(2 * k, 0))

    def column_to(k, h):
        return chain_copy(
            2 + 2 * k + h, rows(Q.at[2], 4 * h, 1), rows(CQ.at[k - 1], 4 + h, 1), dev(2 * k, -1)
        )

    def column_own(h):
        return chain_copy(10 + h, rows(Q.at[0], 4 * h, 1), rows(XQ, 4 * h + 3, 1), dev(1, -1))

    def entering_to_sibling():
        return chain_copy(12, rows(Q.at[3], 0, 4), rows(EH, 4, 4), sibling)

    def chain_start():
        q = mm(ld(U, 2, 1, 0), ld(U, 2, 2, 0))
        Q[0, 0] = q[0]
        Q[0, 1] = q[1]
        to_sibling().start()

        @pl.when(lower)
        def _():
            for h in range(2):
                column_own(h).start()

    def chain_middle():
        to_sibling().wait_recv()
        mine, other = ld(Q, 0), (SQ[0], SQ[1])
        q = mm(pick(lower, mine, other), pick(lower, other, mine))
        for c in range(2):
            Q[2, c] = q[c]
            Q[1, c] = jnp.where(lower, q[c], sroll(q[c], 4))
        for k in (2, 3, 1):

            @pl.when(chip + k < 4)
            def _():
                half_to(k).start()

        for k in (2, 3, 1):

            @pl.when(chip + k < 4)
            def _():
                for h in range(2):
                    column_to(k, h).start()

    def sweep_start(w):
        plane_yz(w)
        for m in (2, 3):
            plane_t(w, m, 1)
            local_t(w, m)
        tx_local(w, 1)
        for m in (2, 3):
            local_x(w, m)

    def sweep_time(w):
        for m in (2, 3):
            plane_t(w, m, 2)
            plane_t_before(w, m)

    def wait_time(w):
        for m in range(4):
            up(w, m).wait_recv()
            if m != 0:
                down(w, m).wait_recv()

    sweep_start(0)
    first_down().wait_recv()
    then_right().start()
    first_up().wait_recv()
    then_left().start()
    up_all().wait_recv()
    down_all().wait_recv()
    for m in range(4):
        third_face(0, m)
        if m != 0:
            third_face(3, m)
    sweep_time(0)
    tx_local(0, 2)
    right_xyz().wait_recv()
    left_yz().wait_recv()
    third_cols(CH, 1)
    for m in (2, 3):
        third_cols(CH, m)
        third_cols(XH, m)
        plane_x(0, m)

    def arrived(m):
        right(1, m).wait_recv()
        if m != 1:
            left(1, m).wait_recv()

    def finish(m):
        unitarise(0, m)
        pack(1, m)
        if m == 1:
            corner_down(1).start()
        right(1, m).start()
        if m != 1:
            left(1, m).start()
        if m == 0:
            corner_up(1).start()
        up(1, m).start()
        if m != 0:
            down(1, m).start()

    finish(2)
    finish(3)
    right(0, 0).wait_recv()
    left(0, 0).wait_recv()
    third_cols(CH, 0)
    third_cols(XH, 0)
    tx_upper(0)
    tx_side(0)
    then_right().wait_recv()
    third_cols(CH, 4)
    tx_lower(0)
    finish(0)
    then_left().wait_recv()
    third_cols(XH, 1)
    tx_before(0)
    finish(1)

    sweep_start(1)
    wait_time(1)
    sweep_time(1)
    tx_local(1, 2)
    arrived(0)
    arrived(1)
    tx_upper(1)
    corner_down(1).wait_recv()
    tx_lower(1)
    unitarise(1, 0)
    chain_start()
    pack(2, 0)
    left(2, 0).start()
    tx_side(1)
    for m in (2, 3):
        arrived(m)
        plane_x(1, m)
    chain_middle()
    corner_up(1).wait_recv()
    tx_before(1)
    for m in (1, 2, 3):
        unitarise(1, m)

    for c in (up_all, down_all, left_yz, right_xyz, first_up, first_down, then_left, then_right):
        c().wait_send()
    right(0, 0).wait_send()
    left(0, 0).wait_send()
    for m in range(4):
        if m != 0:
            down(1, m).wait_send()
        up(1, m).wait_send()
        if m != 1:
            left(1, m).wait_send()
        right(1, m).wait_send()
    corner_up(1).wait_send()
    corner_down(1).wait_send()
    left(2, 0).wait_send()

    for k in (1, 2, 3):

        @pl.when(chip >= k)
        def _():
            half_to(k).wait_recv()
            for h in range(2):
                column_to(k, h).wait_recv()

    run = pick(chip >= 3, ld(CQ, 2), one)
    run = pick(chip >= 2, mm(run, ld(CQ, 1)), one)
    run = pick(chip >= 1, mm(run, ld(CQ, 0)), one)
    for c in range(2):
        Q[3, c] = run[c]
    entering_to_sibling().start()
    gh1 = tuple(jnp.where(sub < 4, sroll(v, -1), sroll(v, 2)) for v in run)

    @pl.when(core == 1)
    def _():
        for h in range(2):
            chain_copy(10 + h, rows(Q.at[0], 4 * h, 1), rows(XQ, 4 * h + 3, 1), dev(1, -1)).wait_recv()

    gh1 = pick(lower, gh1, mm(gh1, (XQ[0], XQ[1])))
    left(2, 0).wait_recv()
    halo = XH[2, 0]
    gh2 = mm(gh1, tuple(sroll(halo, 3 - 2 * q) for q in range(2)))
    entering_to_sibling().wait_recv()
    whole = tuple(jnp.where(sub < 4, v, EH[c]) for c, v in enumerate(run))
    whole = pick(lower, whole, each(lambda v: sroll(v, 4), whole))
    g1 = pick(lower, whole, mm(whole, (SQ[0], SQ[1])))
    g2 = mm(g1, ld(U, 2, 1, 0))
    g3 = mm(g2, ld(U, 2, 2, 0))
    gs = (g1, g2)

    def store(m, s, pair):
        OUT[m, 0, :, :, s] = pair[0]
        OUT[m, 1, :, :, s] = pair[1]

    def save(m, h):
        return pltpu.make_async_copy(
            OUT.at[m, :, :, :, :, pl.ds(4 * h, 4), :],
            o_ref.at[m, :, :, :, :, :, pl.ds(h * LANES, LANES)],
            io.at[4 + 2 * m + h],
        )

    def save_all(m):
        for h in range(2):
            save(m, h).start()

    store(0, 0, mm(g2, g2, db=True))
    store(0, 1, mm(g3, g3, db=True))
    save_all(0)
    for m in (2, 3):
        for s in range(2):
            store(m, s, mm(mm(gs[s], ld(U, 2, 1 + s, m)), yz_shift(gs[s], m, 1), db=True))
        save_all(m)
    for s, gh in ((0, gh1), (1, gh2)):
        gx_next = tuple(jnp.where(row4 == 3, a, sroll(b, -1)) for a, b in zip(gh, gs[s]))
        store(1, s, mm(mm(gs[s], ld(U, 2, 1 + s, 1)), gx_next, db=True))
    save_all(1)

    to_sibling().wait_send()
    entering_to_sibling().wait_send()

    @pl.when(lower)
    def _():
        for h in range(2):
            column_own(h).wait_send()

    for k in (1, 2, 3):

        @pl.when(chip + k < 4)
        def _():
            half_to(k).wait_send()
            for h in range(2):
                column_to(k, h).wait_send()

    for m in range(4):
        for h in range(2):
            save(m, h).wait()


def body(gauge_links):
    field = (2, 3, 3, 8, LANES)
    f32 = jnp.float32
    return pl.pallas_call(
        kernel,
        out_shape=jax.ShapeDtypeStruct(gauge_links.shape, f32),
        in_specs=[pl.BlockSpec(memory_space=pltpu.HBM)],
        out_specs=pl.BlockSpec(memory_space=pl.ANY),
        scratch_shapes=[
            pltpu.VMEM((3, 4, 4) + field, f32),
            pltpu.VMEM((3, 4) + field[1:], f32),
            pltpu.VMEM((2, 5) + field[1:], f32),
            pltpu.VMEM((3, 4) + field[1:], f32),
            pltpu.VMEM((3, 4) + field[1:], f32),
            pltpu.VMEM((2, 2) + field[2:], f32),
            pltpu.VMEM((4, 2) + field, f32),
            pltpu.VMEM((18,) + field, f32),
            pltpu.VMEM((4,) + field, f32),
            pltpu.VMEM(field, f32),
            pltpu.VMEM((3,) + field, f32),
            pltpu.VMEM(field, f32),
            pltpu.VMEM(field, f32),
            pltpu.VMEM((4, 2, 3, 3, 2, 8, LANES), f32),
            pltpu.SemaphoreType.DMA((3, 20)),
            pltpu.SemaphoreType.DMA((3, 20)),
            pltpu.SemaphoreType.DMA((13,)),
            pltpu.SemaphoreType.DMA((13,)),
            pltpu.SemaphoreType.DMA((16,)),
        ],
        compiler_params=pltpu.CompilerParams(
            collective_id=0, has_side_effects=True, vmem_limit_bytes=32 * 2**20
        ),
    )(pltpu.with_memory_space_constraint(gauge_links, pltpu.HBM))


def solution(mesh):
    spec = P(None, None, None, None, "ta", "gx", None)
    return jax.shard_map(body, mesh=mesh, in_specs=(spec,), out_specs=spec, check_vma=False)
```

```python
import functools

import jax
import jax.numpy as jnp
from jax import lax
from jax.experimental import pallas as pl
from jax.experimental.pallas import tpu as pltpu
from jax.sharding import PartitionSpec as P

MESH = pl.DeviceIdType.MESH
NZ = 16
NEWTON = 5
ape_weight = 0.4
LANES = 128


def mm(a, b, da=False, db=False):
    def left(c):
        return tuple(q[c, :, None] if da else q[:, c, None] for q in a)

    def right(c):
        return tuple(q[None, :, c] if db else q[None, c] for q in b)

    re = im = None
    for c in range(3):
        lr, li = left(c)
        rr, ri = right(c)
        x, y = lr * rr, li * ri
        u, v = lr * ri, li * rr
        re = x if re is None else re + x
        re = re + y if da != db else re - y
        if im is None:
            if da and db:
                im = -u - v
            elif da:
                im = u - v
            elif db:
                im = v - u
            else:
                im = u + v
        else:
            im = im - u if db else im + u
            im = im - v if da else im + v
    return re, im


def lane_of(shape):
    return lax.broadcasted_iota(jnp.int32, shape, len(shape) - 1)


def each(f, pair):
    return tuple(f(q) for q in pair)


def sroll(v, shift):
    shift = shift % 8
    if shift == 0:
        return v
    flat = v.reshape((9, 8, LANES))
    return pltpu.roll(flat, shift, 1).reshape(v.shape)


def lroll(v, shift):
    return pltpu.roll(v.reshape((72, LANES)), shift % LANES, 1).reshape(v.shape)


def yz_shift(pair, m, sign):
    lane = lane_of((3, 3, 8, LANES))
    z = lax.rem(lane, NZ)
    if isinstance(m, int):
        if m == 2:

            def move(v):
                r = lroll(v, -NZ * sign)
                stay = lane < LANES - NZ if sign > 0 else lane >= NZ
                return jnp.where(stay, r, sroll(r, 4))

        else:

            def move(v):
                stay = z < NZ - 1 if sign > 0 else z >= 1
                return jnp.where(stay, lroll(v, -sign), lroll(v, sign * (NZ - 1)))

        return each(move, pair)
    raise NotImplementedError


def kernel(
    x_ref, o_ref, U, XH, CH, PK0, PK3, RL, acc, KT, Q, SQ, CQ, EH, XQ, OUT, hs, hr, cs, cr, io
):
    ta = lax.axis_index("ta")
    gx = lax.axis_index("gx")
    nta = lax.axis_size("ta")
    ngx = lax.axis_size("gx")
    core, chip = lax.rem(ta, 2), ta // 2

    def dev(dt, dg):
        return {"ta": lax.rem(ta + dt + nta, nta), "gx": lax.rem(gx + dg + ngx, ngx)}

    barrier = pltpu.get_barrier_semaphore()
    for d in (dev(0, 1), dev(0, -1), dev(4, 0), dev(1, 0), dev(-1, 0)):
        pl.semaphore_signal(barrier, inc=1, device_id=d, device_id_type=MESH)

    loads = []
    for t in range(2):
        for h in range(2):
            c = pltpu.make_async_copy(
                x_ref.at[:, :, :, :, t, :, pl.ds(h * LANES, LANES)],
                U.at[0, 1 + t, :, :, :, :, pl.ds(4 * h, 4), :],
                io.at[2 * t + h],
            )
            c.start()
            loads.append(c)

    def ld(ref, *at):
        v = ref[at]
        return v[0], v[1]

    def add(m, s, pair):
        acc[m, s, 0] = acc[m, s, 0] + pair[0]
        acc[m, s, 1] = acc[m, s, 1] + pair[1]

    row4 = lax.rem(lax.broadcasted_iota(jnp.int32, (3, 3, 8, LANES), 2), 4)

    def pack(w, m):
        parts = [U[w, 1, m, 0], U[w, 2, m, 0], U[w, 1, m, 1], U[w, 2, m, 1]]
        for col, out in ((0, PK0), (3, PK3)):
            moved = [sroll(v, q - col) for q, v in enumerate(parts)]
            out[w, m] = jnp.where(
                row4 < 2,
                jnp.where(row4 == 0, moved[0], moved[1]),
                jnp.where(row4 == 2, moved[2], moved[3]),
            )

    def x_next(pair, halo, t):
        return tuple(
            jnp.where(row4 == 3, sroll(halo, 3 - t - 2 * q), sroll(v, -1))
            for q, v in enumerate(pair)
        )

    def x_prev(pair, column, t):
        return tuple(
            jnp.where(row4 == 0, sroll(c, -t), sroll(v, 1)) for v, c in zip(pair, column)
        )

    def unpacked(v):
        return v, sroll(v, -2)

    def copy(w, slot, src, dst, d):
        return pltpu.make_async_remote_copy(
            src_ref=src,
            dst_ref=dst,
            send_sem=hs.at[w, slot],
            recv_sem=hr.at[w, slot],
            device_id=d,
            device_id_type=MESH,
        )

    def face(w, s, m):
        return U.at[w, s, m, :, pl.ds(0, 2)] if w == 0 else U.at[w, s, m]

    def cols(ref, w, m):
        return ref.at[w, m, pl.ds(0, 2)] if w == 0 else ref.at[w, m]

    def down(w, m):
        return copy(w, m, face(w, 1, m), face(w, 3, m), dev(-1, 0))

    def up(w, m):
        return copy(w, 4 + m, face(w, 2, m), face(w, 0, m), dev(1, 0))

    def left(w, m):
        return copy(w, 8 + m, cols(PK0, w, m), cols(XH, w, m), dev(0, -1))

    def right(w, m):
        return copy(w, 12 + m, cols(PK3, w, m), cols(CH, w, m), dev(0, 1))

    def corner_up(w):
        return copy(w, 16, cols(PK0, w, 0), cols(XH, w, 1), dev(1, -1))

    def corner_down(w):
        return copy(w, 17, cols(PK3, w, 1), cols(CH, w, 4), dev(-1, 1))

    def up_all():
        return copy(0, 4, U.at[0, 2, :, :, pl.ds(0, 2)], U.at[0, 0, :, :, pl.ds(0, 2)], dev(1, 0))

    def down_all():
        links = pl.ds(1, 3)
        return copy(
            0, 1, U.at[0, 1, links, :, pl.ds(0, 2)], U.at[0, 3, links, :, pl.ds(0, 2)], dev(-1, 0)
        )

    def left_yz():
        links = pl.ds(2, 2)
        return copy(0, 10, PK0.at[0, links, pl.ds(0, 2)], XH.at[0, links, pl.ds(0, 2)], dev(0, -1))

    def right_xyz():
        links = pl.ds(1, 3)
        return copy(0, 13, PK3.at[0, links, pl.ds(0, 2)], CH.at[0, links, pl.ds(0, 2)], dev(0, 1))

    def first_up():
        return copy(0, 18, cols(PK0, 0, 0), RL.at[0], dev(1, 0))

    def first_down():
        return copy(0, 19, cols(PK3, 0, 1), RL.at[1], dev(-1, 0))

    def then_left():
        return copy(0, 16, RL.at[0], cols(XH, 0, 1), dev(0, -1))

    def then_right():
        return copy(0, 17, RL.at[1], cols(CH, 0, 4), dev(0, 1))

    def cross(a, b):
        out = []
        for j in range(3):
            (pr, pi), (qr, qi) = a[(j + 1) % 3], b[(j + 2) % 3]
            (tr, ti), (ur, ui) = a[(j + 2) % 3], b[(j + 1) % 3]
            out.append((pr * qr - pi * qi - tr * ur + ti * ui, tr * ui + ti * ur - pr * qi - pi * qr))
        return out

    def third_face(s, m):
        rows = [[(U[0, s, m, 0, i, j], U[0, s, m, 1, i, j]) for j in range(3)] for i in range(2)]
        for j, (re, im) in enumerate(cross(*rows)):
            U[0, s, m, 0, 2, j] = re
            U[0, s, m, 1, 2, j] = im

    quad = lax.rem(lax.broadcasted_iota(jnp.int32, (8, LANES), 0), 4)

    def third_cols(ref, m):
        rows = [
            [(ref[0, m, i, j], pltpu.roll(ref[0, m, i, j], 6, 0)) for j in range(3)] for i in range(2)
        ]
        for j, (re, im) in enumerate(cross(*rows)):
            ref[0, m, 2, j] = jnp.where(quad < 2, re, pltpu.roll(im, 2, 0))

    for c in loads:
        c.wait()

    @pl.loop(0, 4)
    def _(m):
        pack(0, m)
        for s in range(2):
            acc[m, s] = 9.0 * U[0, 1 + s, m]

    pl.semaphore_wait(barrier, 5)
    first_down().start()
    first_up().start()
    right_xyz().start()
    left_yz().start()
    right(0, 0).start()
    left(0, 0).start()
    up_all().start()
    down_all().start()

    def plane_yz(w):
        for s in (1, 2):
            uy, uz = ld(U, w, s, 2), ld(U, w, s, 3)
            uyz, uzy = yz_shift(uy, 3, 1), yz_shift(uz, 2, 1)
            p1, p2 = mm(uy, uzy), mm(uz, uyz)
            add(2, s - 1, mm(p2, uzy, db=True))
            add(3, s - 1, mm(p1, uyz, db=True))
            add(2, s - 1, yz_shift(mm(uz, p1, da=True), 3, -1))
            add(3, s - 1, yz_shift(mm(uy, p2, da=True), 2, -1))

    def keep(slot, pair):
        KT[slot, 0] = pair[0]
        KT[slot, 1] = pair[1]

    def local_t(w, m):
        keep(5 + m, mm(ld(U, w, 2, m), yz_shift(ld(U, w, 2, 0), m, 1)))

    def local_x(w, m):
        for s in (1, 2):
            ux, um = ld(U, w, s, 1), ld(U, w, s, m)
            p2 = mm(um, yz_shift(ux, m, 1))
            keep(5 + 2 * m + s, p2)
            keep(9 + 2 * m + s, mm(ux, p2, da=True))

    def plane_t(w, m, s):
        ut, um, umt = ld(U, w, s, 0), ld(U, w, s, m), ld(U, w, s + 1, m)
        utm = yz_shift(ut, m, 1)
        p1 = mm(ut, umt)
        p2 = mm(um, utm) if s == 1 else ld(KT, 5 + m)
        add(0, s - 1, mm(p2, umt, db=True))
        add(m, s - 1, mm(p1, utm, db=True))
        add(0, s - 1, yz_shift(mm(um, p1, da=True), m, -1))
        if s == 1:
            add(m, 1, mm(ut, p2, da=True))

    def plane_t_before(w, m):
        ut, um = ld(U, w, 0, 0), ld(U, w, 0, m)
        p2 = mm(um, yz_shift(ut, m, 1))
        add(m, 0, mm(ut, p2, da=True))

    def tx_local(w, s):
        ut, ux, uxt = ld(U, w, s, 0), ld(U, w, s, 1), ld(U, w, s + 1, 1)
        p1 = mm(ut, uxt)
        keep(s - 1, p1)
        keep(s + 1, mm(ux, p1, da=True))

    def tx_upper(w):
        for s in (1, 2):
            ux, uxt = ld(U, w, s, 1), ld(U, w, s + 1, 1)
            utx = x_next(ld(U, w, s, 0), XH[w, 0], s - 1)
            p2 = mm(ux, utx)
            keep(s + 3, utx)
            add(0, s - 1, mm(p2, uxt, db=True))
            if s == 1:
                keep(6, p2)

    def tx_lower(w):
        cx_re, cx_im = unpacked(CH[w, 1])
        far_re, far_im = unpacked(CH[w, 4])
        cx = (cx_re, cx_im)
        cxt = tuple(
            jnp.where(row4 == 0, sroll(v, -1), sroll(f, 1)) for v, f in ((cx_re, far_re), (cx_im, far_im))
        )
        ct = unpacked(CH[w, 0])
        lower_c = mm(cx, mm(ct, cxt), da=True)
        for s in range(2):
            add(0, s, x_prev(ld(KT, 2 + s), lower_c, s))

    def tx_side(w):
        for s in range(2):
            add(1, s, mm(ld(KT, s), ld(KT, 4 + s), db=True))
        add(1, 1, mm(ld(U, w, 1, 0), ld(KT, 6), da=True))

    def tx_before(w):
        ut = ld(U, w, 0, 0)
        p2 = mm(ld(U, w, 0, 1), x_next(ut, XH[w, 1], 1))
        add(1, 0, mm(ut, p2, da=True))

    def plane_x(w, m):
        cx, cm = unpacked(CH[w, 1]), unpacked(CH[w, m])
        lower_c = mm(cx, mm(cm, yz_shift(cx, m, 1)), da=True)
        for s in (1, 2):
            ux, um = ld(U, w, s, 1), ld(U, w, s, m)
            umx = x_next(um, XH[w, m], s - 1)
            uxm = yz_shift(ux, m, 1)
            p1, p2 = mm(ux, umx), ld(KT, 5 + 2 * m + s)
            add(1, s - 1, mm(p2, umx, db=True))
            add(m, s - 1, mm(p1, uxm, db=True))
            add(1, s - 1, yz_shift(mm(um, p1, da=True), m, -1))
            add(m, s - 1, x_prev(ld(KT, 9 + 2 * m + s), lower_c, s - 1))

    def unitarise(w, m):
        scale = ape_weight / 6.0
        for s in range(2):
            re = [[acc[m, s, 0, i, j] for j in range(3)] for i in range(3)]
            im = [[acc[m, s, 1, i, j] for j in range(3)] for i in range(3)]

            def diag(j):
                t = None
                for i in range(3):
                    q = re[i][j] * re[i][j] + im[i][j] * im[i][j]
                    t = q if t is None else t + q
                return t

            def off(j, k):
                a = b = None
                for i in range(3):
                    x = re[i][j] * re[i][k] + im[i][j] * im[i][k]
                    y = re[i][j] * im[i][k] - im[i][j] * re[i][k]
                    a = x if a is None else a + x
                    b = y if b is None else b + y
                return a, b

            k1, k2, k3 = diag(0), diag(1), diag(2)
            inverse = jnp.minimum(lax.rsqrt((scale * scale) * (k1 + k2 + k3)), 1.0)
            r = scale * inverse
            g = r * r
            a1, a2, a3 = g * k1, g * k2, g * k3
            b12 = tuple(g * v for v in off(0, 1))
            b13 = tuple(g * v for v in off(0, 2))
            b23 = tuple(g * v for v in off(1, 2))

            def norm(v):
                return v[0] * v[0] + v[1] * v[1]

            def times(a, b):
                return a[0] * b[0] - a[1] * b[1], a[0] * b[1] + a[1] * b[0]

            def ctimes(a, b):
                return a[0] * b[0] + a[1] * b[1], a[1] * b[0] - a[0] * b[1]

            j1 = a2 * a3 - norm(b23)
            j2 = a1 * a3 - norm(b13)
            j3 = a1 * a2 - norm(b12)
            q = ctimes(b13, b23)
            j12 = (q[0] - a3 * b12[0], q[1] - a3 * b12[1])
            q = times(b12, b23)
            j13 = (q[0] - a2 * b13[0], q[1] - a2 * b13[1])
            q = ctimes(b13, b12)
            j23 = (q[0] - a1 * b23[0], q[1] - a1 * b23[1])
            e1 = a1 + a2 + a3
            e2 = j1 + j2 + j3
            e3 = (
                a1 * j1
                + (b12[0] * j12[0] + b12[1] * j12[1])
                + (b13[0] * j13[0] + b13[1] * j13[1])
            )

            def reduce(d0, d1, d2, d3, d4):
                d3 = d3 + e1 * d4
                d2 = d2 - e2 * d4 + e1 * d3
                d1 = d1 + e3 * d4 - e2 * d3
                return d0 + e3 * d3, d1, d2

            h = (0.25 * e3, 2.25 - 0.25 * e2, 0.25 * e1 - 1.5)
            p = None
            for k in range(1, NEWTON):
                y = (1.5 - 0.5 * h[0], -0.5 * h[1], -0.5 * h[2])
                if p is None:
                    d3 = -0.5 * y[2]
                    p = (
                        1.5 * y[0] + e3 * d3,
                        1.5 * y[1] - 0.5 * y[0] - e2 * d3,
                        1.5 * y[2] - 0.5 * y[1] + e1 * d3,
                    )
                else:
                    p = reduce(
                        p[0] * y[0],
                        p[0] * y[1] + p[1] * y[0],
                        p[0] * y[2] + p[1] * y[1] + p[2] * y[0],
                        p[1] * y[2] + p[2] * y[1],
                        p[2] * y[2],
                    )
                if k < NEWTON - 1:
                    twice = p[0] + p[0]
                    f = reduce(
                        p[0] * p[0],
                        twice * p[1],
                        twice * p[2] + p[1] * p[1],
                        (p[1] + p[1]) * p[2],
                        p[2] * p[2],
                    )
                    h = (e3 * f[2], f[0] - e2 * f[2], f[1] + e1 * f[2])

            c2 = r * p[2]
            c1 = r * p[1] + e1 * c2
            c0 = r * p[0] - e2 * c2

            def entry(b, j):
                return c1 * b[0] + c2 * j[0], c1 * b[1] + c2 * j[1]

            m12, m13, m23 = entry(b12, j12), entry(b13, j13), entry(b23, j23)
            dg = [c0 + c1 * a + c2 * j for a, j in ((a1, j1), (a2, j2), (a3, j3))]
            table = {(0, 1): m12, (0, 2): m13, (1, 2): m23}
            for i in range(3):
                for j in range(3):
                    x = re[i][j] * dg[j]
                    y = im[i][j] * dg[j]
                    for k in range(3):
                        if k == j:
                            continue
                        vr, vi = table[(min(k, j), max(k, j))]
                        ur, ui = re[i][k], im[i][k]
                        if k < j:
                            x = x + ur * vr - ui * vi
                            y = y + ur * vi + ui * vr
                        else:
                            x = x + ur * vr + ui * vi
                            y = y - ur * vi + ui * vr
                    U[w + 1, 1 + s, m, 0, i, j] = x
                    U[w + 1, 1 + s, m, 1, i, j] = y
        for s in range(2):
            acc[m, s] = 9.0 * U[w + 1, 1 + s, m]

    sub = lax.broadcasted_iota(jnp.int32, (3, 3, 8, LANES), 2)
    eye = (
        lax.broadcasted_iota(jnp.int32, (3, 3, 8, LANES), 0)
        == lax.broadcasted_iota(jnp.int32, (3, 3, 8, LANES), 1)
    ).astype(jnp.float32)
    one = (eye, jnp.zeros_like(eye))
    lower = core == 0
    sibling = dev(1 - 2 * core, 0)

    def pick(cond, a, b):
        return tuple(jnp.where(cond, x, y) for x, y in zip(a, b))

    def chain_copy(slot, src, dst, d):
        return pltpu.make_async_remote_copy(
            src_ref=src,
            dst_ref=dst,
            send_sem=cs.at[slot],
            recv_sem=cr.at[slot],
            device_id=d,
            device_id_type=MESH,
        )

    def rows(ref, first, count):
        return ref.at[:, :, :, pl.ds(first, count), :]

    def to_sibling():
        return chain_copy(0, Q.at[0], SQ, sibling)

    def half_to(k):
        return chain_copy(k, rows(Q.at[1], 0, 4), rows(CQ.at[k - 1], 0, 4), dev(2 * k, 0))

    def column_to(k, h):
        return chain_copy(
            2 + 2 * k + h, rows(Q.at[2], 4 * h, 1), rows(CQ.at[k - 1], 4 + h, 1), dev(2 * k, -1)
        )

    def column_own(h):
        return chain_copy(10 + h, rows(Q.at[0], 4 * h, 1), rows(XQ, 4 * h + 3, 1), dev(1, -1))

    def entering_to_sibling():
        return chain_copy(12, rows(Q.at[3], 0, 4), rows(EH, 4, 4), sibling)

    def chain_start():
        q = mm(ld(U, 2, 1, 0), ld(U, 2, 2, 0))
        Q[0, 0] = q[0]
        Q[0, 1] = q[1]
        to_sibling().start()

        @pl.when(lower)
        def _():
            for h in range(2):
                column_own(h).start()

    def chain_middle():
        to_sibling().wait_recv()
        mine, other = ld(Q, 0), (SQ[0], SQ[1])
        q = mm(pick(lower, mine, other), pick(lower, other, mine))
        for c in range(2):
            Q[2, c] = q[c]
            Q[1, c] = jnp.where(lower, q[c], sroll(q[c], 4))
        for k in (2, 3, 1):

            @pl.when(chip + k < 4)
            def _():
                half_to(k).start()

        for k in (2, 3, 1):

            @pl.when(chip + k < 4)
            def _():
                for h in range(2):
                    column_to(k, h).start()

    def sweep_start(w):
        plane_yz(w)
        for m in (2, 3):
            plane_t(w, m, 1)
            local_t(w, m)
        tx_local(w, 1)
        for m in (2, 3):
            local_x(w, m)

    def sweep_time(w):
        for m in (2, 3):
            plane_t(w, m, 2)
            plane_t_before(w, m)

    def wait_time(w):
        for m in range(4):
            up(w, m).wait_recv()
            if m != 0:
                down(w, m).wait_recv()

    sweep_start(0)
    first_down().wait_recv()
    then_right().start()
    first_up().wait_recv()
    then_left().start()
    right_xyz().wait_recv()
    left_yz().wait_recv()
    third_cols(CH, 1)
    for m in (2, 3):
        third_cols(CH, m)
        third_cols(XH, m)
        plane_x(0, m)

    up_all().wait_recv()
    down_all().wait_recv()
    for m in range(4):
        third_face(0, m)
        if m != 0:
            third_face(3, m)
    sweep_time(0)
    tx_local(0, 2)
    def arrived(m):
        right(1, m).wait_recv()
        if m != 1:
            left(1, m).wait_recv()

    def finish(m):
        unitarise(0, m)
        pack(1, m)
        if m == 1:
            corner_down(1).start()
        right(1, m).start()
        if m != 1:
            left(1, m).start()
        if m == 0:
            corner_up(1).start()
        up(1, m).start()
        if m != 0:
            down(1, m).start()

    finish(2)
    finish(3)
    right(0, 0).wait_recv()
    left(0, 0).wait_recv()
    third_cols(CH, 0)
    third_cols(XH, 0)
    tx_upper(0)
    tx_side(0)
    then_right().wait_recv()
    third_cols(CH, 4)
    tx_lower(0)
    finish(0)
    then_left().wait_recv()
    third_cols(XH, 1)
    tx_before(0)
    finish(1)

    sweep_start(1)
    wait_time(1)
    sweep_time(1)
    tx_local(1, 2)
    arrived(0)
    arrived(1)
    tx_upper(1)
    corner_down(1).wait_recv()
    tx_lower(1)
    unitarise(1, 0)
    chain_start()
    pack(2, 0)
    left(2, 0).start()
    tx_side(1)
    for m in (2, 3):
        arrived(m)
        plane_x(1, m)
    chain_middle()
    corner_up(1).wait_recv()
    tx_before(1)
    for m in (1, 2, 3):
        unitarise(1, m)

    for c in (up_all, down_all, left_yz, right_xyz, first_up, first_down, then_left, then_right):
        c().wait_send()
    right(0, 0).wait_send()
    left(0, 0).wait_send()
    for m in range(4):
        if m != 0:
            down(1, m).wait_send()
        up(1, m).wait_send()
        if m != 1:
            left(1, m).wait_send()
        right(1, m).wait_send()
    corner_up(1).wait_send()
    corner_down(1).wait_send()
    left(2, 0).wait_send()

    for k in (1, 2, 3):

        @pl.when(chip >= k)
        def _():
            half_to(k).wait_recv()
            for h in range(2):
                column_to(k, h).wait_recv()

    run = pick(chip >= 3, ld(CQ, 2), one)
    run = pick(chip >= 2, mm(run, ld(CQ, 1)), one)
    run = pick(chip >= 1, mm(run, ld(CQ, 0)), one)
    for c in range(2):
        Q[3, c] = run[c]
    entering_to_sibling().start()
    gh1 = tuple(jnp.where(sub < 4, sroll(v, -1), sroll(v, 2)) for v in run)

    @pl.when(core == 1)
    def _():
        for h in range(2):
            chain_copy(10 + h, rows(Q.at[0], 4 * h, 1), rows(XQ, 4 * h + 3, 1), dev(1, -1)).wait_recv()

    gh1 = pick(lower, gh1, mm(gh1, (XQ[0], XQ[1])))
    left(2, 0).wait_recv()
    halo = XH[2, 0]
    gh2 = mm(gh1, tuple(sroll(halo, 3 - 2 * q) for q in range(2)))
    entering_to_sibling().wait_recv()
    whole = tuple(jnp.where(sub < 4, v, EH[c]) for c, v in enumerate(run))
    whole = pick(lower, whole, each(lambda v: sroll(v, 4), whole))
    g1 = pick(lower, whole, mm(whole, (SQ[0], SQ[1])))
    g2 = mm(g1, ld(U, 2, 1, 0))
    g3 = mm(g2, ld(U, 2, 2, 0))
    gs = (g1, g2)

    def store(m, s, pair):
        OUT[m, 0, :, :, s] = pair[0]
        OUT[m, 1, :, :, s] = pair[1]

    def save(m, h):
        return pltpu.make_async_copy(
            OUT.at[m, :, :, :, :, pl.ds(4 * h, 4), :],
            o_ref.at[m, :, :, :, :, :, pl.ds(h * LANES, LANES)],
            io.at[4 + 2 * m + h],
        )

    def save_all(m):
        for h in range(2):
            save(m, h).start()

    store(0, 0, mm(g2, g2, db=True))
    store(0, 1, mm(g3, g3, db=True))
    save_all(0)
    for m in (2, 3):
        for s in range(2):
            store(m, s, mm(mm(gs[s], ld(U, 2, 1 + s, m)), yz_shift(gs[s], m, 1), db=True))
        save_all(m)
    for s, gh in ((0, gh1), (1, gh2)):
        gx_next = tuple(jnp.where(row4 == 3, a, sroll(b, -1)) for a, b in zip(gh, gs[s]))
        store(1, s, mm(mm(gs[s], ld(U, 2, 1 + s, 1)), gx_next, db=True))
    save_all(1)

    to_sibling().wait_send()
    entering_to_sibling().wait_send()

    @pl.when(lower)
    def _():
        for h in range(2):
            column_own(h).wait_send()

    for k in (1, 2, 3):

        @pl.when(chip + k < 4)
        def _():
            half_to(k).wait_send()
            for h in range(2):
                column_to(k, h).wait_send()

    for m in range(4):
        for h in range(2):
            save(m, h).wait()


def body(gauge_links):
    field = (2, 3, 3, 8, LANES)
    f32 = jnp.float32
    return pl.pallas_call(
        kernel,
        out_shape=jax.ShapeDtypeStruct(gauge_links.shape, f32),
        in_specs=[pl.BlockSpec(memory_space=pltpu.HBM)],
        out_specs=pl.BlockSpec(memory_space=pl.ANY),
        scratch_shapes=[
            pltpu.VMEM((3, 4, 4) + field, f32),
            pltpu.VMEM((3, 4) + field[1:], f32),
            pltpu.VMEM((2, 5) + field[1:], f32),
            pltpu.VMEM((3, 4) + field[1:], f32),
            pltpu.VMEM((3, 4) + field[1:], f32),
            pltpu.VMEM((2, 2) + field[2:], f32),
            pltpu.VMEM((4, 2) + field, f32),
            pltpu.VMEM((18,) + field, f32),
            pltpu.VMEM((4,) + field, f32),
            pltpu.VMEM(field, f32),
            pltpu.VMEM((3,) + field, f32),
            pltpu.VMEM(field, f32),
            pltpu.VMEM(field, f32),
            pltpu.VMEM((4, 2, 3, 3, 2, 8, LANES), f32),
            pltpu.SemaphoreType.DMA((3, 20)),
            pltpu.SemaphoreType.DMA((3, 20)),
            pltpu.SemaphoreType.DMA((13,)),
            pltpu.SemaphoreType.DMA((13,)),
            pltpu.SemaphoreType.DMA((16,)),
        ],
        compiler_params=pltpu.CompilerParams(
            collective_id=0, has_side_effects=True, vmem_limit_bytes=32 * 2**20
        ),
    )(pltpu.with_memory_space_constraint(gauge_links, pltpu.HBM))


def solution(mesh):
    spec = P(None, None, None, None, "ta", "gx", None)
    return jax.shard_map(body, mesh=mesh, in_specs=(spec,), out_specs=spec, check_vma=False)
```

```python
import functools

import jax
import jax.numpy as jnp
from jax import lax
from jax.experimental import pallas as pl
from jax.experimental.pallas import tpu as pltpu
from jax.sharding import PartitionSpec as P

MESH = pl.DeviceIdType.MESH
NZ = 16
NEWTON = 5
ape_weight = 0.4
LANES = 128


def mm(a, b, da=False, db=False):
    def left(c):
        return tuple(q[c, :, None] if da else q[:, c, None] for q in a)

    def right(c):
        return tuple(q[None, :, c] if db else q[None, c] for q in b)

    re = im = None
    for c in range(3):
        lr, li = left(c)
        rr, ri = right(c)
        x, y = lr * rr, li * ri
        u, v = lr * ri, li * rr
        re = x if re is None else re + x
        re = re + y if da != db else re - y
        if im is None:
            if da and db:
                im = -u - v
            elif da:
                im = u - v
            elif db:
                im = v - u
            else:
                im = u + v
        else:
            im = im - u if db else im + u
            im = im - v if da else im + v
    return re, im


def lane_of(shape):
    return lax.broadcasted_iota(jnp.int32, shape, len(shape) - 1)


def each(f, pair):
    return tuple(f(q) for q in pair)


def sroll(v, shift):
    shift = shift % 8
    if shift == 0:
        return v
    flat = v.reshape((9, 8, LANES))
    return pltpu.roll(flat, shift, 1).reshape(v.shape)


def lroll(v, shift):
    return pltpu.roll(v.reshape((72, LANES)), shift % LANES, 1).reshape(v.shape)


def yz_shift(pair, m, sign):
    lane = lane_of((3, 3, 8, LANES))
    z = lax.rem(lane, NZ)
    if isinstance(m, int):
        if m == 2:

            def move(v):
                r = lroll(v, -NZ * sign)
                stay = lane < LANES - NZ if sign > 0 else lane >= NZ
                return jnp.where(stay, r, sroll(r, 4))

        else:

            def move(v):
                stay = z < NZ - 1 if sign > 0 else z >= 1
                return jnp.where(stay, lroll(v, -sign), lroll(v, sign * (NZ - 1)))

        return each(move, pair)
    raise NotImplementedError


def kernel(
    x_ref, o_ref, U, XH, CH, PK0, PK3, RL, acc, KT, Q, SQ, CQ, EH, XQ, OUT, hs, hr, cs, cr, io
):
    ta = lax.axis_index("ta")
    gx = lax.axis_index("gx")
    nta = lax.axis_size("ta")
    ngx = lax.axis_size("gx")
    core, chip = lax.rem(ta, 2), ta // 2

    def dev(dt, dg):
        return {"ta": lax.rem(ta + dt + nta, nta), "gx": lax.rem(gx + dg + ngx, ngx)}

    barrier = pltpu.get_barrier_semaphore()
    for d in (dev(0, 1), dev(0, -1), dev(4, 0), dev(1, 0), dev(-1, 0)):
        pl.semaphore_signal(barrier, inc=1, device_id=d, device_id_type=MESH)

    loads = []
    for t in range(2):
        for h in range(2):
            c = pltpu.make_async_copy(
                x_ref.at[:, :, :, :, t, :, pl.ds(h * LANES, LANES)],
                U.at[0, 1 + t, :, :, :, :, pl.ds(4 * h, 4), :],
                io.at[2 * t + h],
            )
            c.start()
            loads.append(c)

    def ld(ref, *at):
        v = ref[at]
        return v[0], v[1]

    def add(m, s, pair):
        acc[m, s, 0] = acc[m, s, 0] + pair[0]
        acc[m, s, 1] = acc[m, s, 1] + pair[1]

    row4 = lax.rem(lax.broadcasted_iota(jnp.int32, (3, 3, 8, LANES), 2), 4)

    def pack(w, m):
        parts = [U[w, 1, m, 0], U[w, 2, m, 0], U[w, 1, m, 1], U[w, 2, m, 1]]
        for col, out in ((0, PK0), (3, PK3)):
            moved = [sroll(v, q - col) for q, v in enumerate(parts)]
            out[w, m] = jnp.where(
                row4 < 2,
                jnp.where(row4 == 0, moved[0], moved[1]),
                jnp.where(row4 == 2, moved[2], moved[3]),
            )

    def x_next(pair, halo, t):
        return tuple(
            jnp.where(row4 == 3, sroll(halo, 3 - t - 2 * q), sroll(v, -1))
            for q, v in enumerate(pair)
        )

    def x_prev(pair, column, t):
        return tuple(
            jnp.where(row4 == 0, sroll(c, -t), sroll(v, 1)) for v, c in zip(pair, column)
        )

    def unpacked(v):
        return v, sroll(v, -2)

    def copy(w, slot, src, dst, d):
        return pltpu.make_async_remote_copy(
            src_ref=src,
            dst_ref=dst,
            send_sem=hs.at[w, slot],
            recv_sem=hr.at[w, slot],
            device_id=d,
            device_id_type=MESH,
        )

    def face(w, s, m):
        return U.at[w, s, m, :, pl.ds(0, 2)] if w == 0 else U.at[w, s, m]

    def cols(ref, w, m):
        return ref.at[w, m, pl.ds(0, 2)] if w == 0 else ref.at[w, m]

    def down(w, m):
        return copy(w, m, face(w, 1, m), face(w, 3, m), dev(-1, 0))

    def up(w, m):
        return copy(w, 4 + m, face(w, 2, m), face(w, 0, m), dev(1, 0))

    def left(w, m):
        return copy(w, 8 + m, cols(PK0, w, m), cols(XH, w, m), dev(0, -1))

    def right(w, m):
        return copy(w, 12 + m, cols(PK3, w, m), cols(CH, w, m), dev(0, 1))

    def corner_up(w):
        return copy(w, 16, cols(PK0, w, 0), cols(XH, w, 1), dev(1, -1))

    def corner_down(w):
        return copy(w, 17, cols(PK3, w, 1), cols(CH, w, 4), dev(-1, 1))

    def up_all():
        return copy(0, 4, U.at[0, 2, :, :, pl.ds(0, 2)], U.at[0, 0, :, :, pl.ds(0, 2)], dev(1, 0))

    def down_all():
        links = pl.ds(1, 3)
        return copy(
            0, 1, U.at[0, 1, links, :, pl.ds(0, 2)], U.at[0, 3, links, :, pl.ds(0, 2)], dev(-1, 0)
        )

    def left_yz():
        links = pl.ds(2, 2)
        return copy(0, 10, PK0.at[0, links, pl.ds(0, 2)], XH.at[0, links, pl.ds(0, 2)], dev(0, -1))

    def right_xyz():
        links = pl.ds(1, 3)
        return copy(0, 13, PK3.at[0, links, pl.ds(0, 2)], CH.at[0, links, pl.ds(0, 2)], dev(0, 1))

    def first_up():
        return copy(0, 18, cols(PK0, 0, 0), RL.at[0], dev(1, 0))

    def first_down():
        return copy(0, 19, cols(PK3, 0, 1), RL.at[1], dev(-1, 0))

    def then_left():
        return copy(0, 16, RL.at[0], cols(XH, 0, 1), dev(0, -1))

    def then_right():
        return copy(0, 17, RL.at[1], cols(CH, 0, 4), dev(0, 1))

    def cross(a, b):
        out = []
        for j in range(3):
            (pr, pi), (qr, qi) = a[(j + 1) % 3], b[(j + 2) % 3]
            (tr, ti), (ur, ui) = a[(j + 2) % 3], b[(j + 1) % 3]
            out.append((pr * qr - pi * qi - tr * ur + ti * ui, tr * ui + ti * ur - pr * qi - pi * qr))
        return out

    def third_face(s, m):
        rows = [[(U[0, s, m, 0, i, j], U[0, s, m, 1, i, j]) for j in range(3)] for i in range(2)]
        for j, (re, im) in enumerate(cross(*rows)):
            U[0, s, m, 0, 2, j] = re
            U[0, s, m, 1, 2, j] = im

    quad = lax.rem(lax.broadcasted_iota(jnp.int32, (8, LANES), 0), 4)

    def third_cols(ref, m):
        rows = [
            [(ref[0, m, i, j], pltpu.roll(ref[0, m, i, j], 6, 0)) for j in range(3)] for i in range(2)
        ]
        for j, (re, im) in enumerate(cross(*rows)):
            ref[0, m, 2, j] = jnp.where(quad < 2, re, pltpu.roll(im, 2, 0))

    for c in loads:
        c.wait()

    @pl.loop(0, 4)
    def _(m):
        pack(0, m)
        for s in range(2):
            acc[m, s] = 9.0 * U[0, 1 + s, m]

    pl.semaphore_wait(barrier, 5)
    first_down().start()
    first_up().start()
    right_xyz().start()
    left_yz().start()
    up_all().start()
    down_all().start()
    right(0, 0).start()
    left(0, 0).start()

    def plane_yz(w):
        for s in (1, 2):
            uy, uz = ld(U, w, s, 2), ld(U, w, s, 3)
            uyz, uzy = yz_shift(uy, 3, 1), yz_shift(uz, 2, 1)
            p1, p2 = mm(uy, uzy), mm(uz, uyz)
            add(2, s - 1, mm(p2, uzy, db=True))
            add(3, s - 1, mm(p1, uyz, db=True))
            add(2, s - 1, yz_shift(mm(uz, p1, da=True), 3, -1))
            add(3, s - 1, yz_shift(mm(uy, p2, da=True), 2, -1))

    def keep(slot, pair):
        KT[slot, 0] = pair[0]
        KT[slot, 1] = pair[1]

    def local_t(w, m):
        keep(5 + m, mm(ld(U, w, 2, m), yz_shift(ld(U, w, 2, 0), m, 1)))

    def local_x(w, m):
        for s in (1, 2):
            ux, um = ld(U, w, s, 1), ld(U, w, s, m)
            p2 = mm(um, yz_shift(ux, m, 1))
            keep(5 + 2 * m + s, p2)
            keep(9 + 2 * m + s, mm(ux, p2, da=True))

    def plane_t(w, m, s):
        ut, um, umt = ld(U, w, s, 0), ld(U, w, s, m), ld(U, w, s + 1, m)
        utm = yz_shift(ut, m, 1)
        p1 = mm(ut, umt)
        p2 = mm(um, utm) if s == 1 else ld(KT, 5 + m)
        add(0, s - 1, mm(p2, umt, db=True))
        add(m, s - 1, mm(p1, utm, db=True))
        add(0, s - 1, yz_shift(mm(um, p1, da=True), m, -1))
        if s == 1:
            add(m, 1, mm(ut, p2, da=True))

    def plane_t_before(w, m):
        ut, um = ld(U, w, 0, 0), ld(U, w, 0, m)
        p2 = mm(um, yz_shift(ut, m, 1))
        add(m, 0, mm(ut, p2, da=True))

    def tx_local(w, s):
        ut, ux, uxt = ld(U, w, s, 0), ld(U, w, s, 1), ld(U, w, s + 1, 1)
        p1 = mm(ut, uxt)
        keep(s - 1, p1)
        keep(s + 1, mm(ux, p1, da=True))

    def tx_upper(w):
        for s in (1, 2):
            ux, uxt = ld(U, w, s, 1), ld(U, w, s + 1, 1)
            utx = x_next(ld(U, w, s, 0), XH[w, 0], s - 1)
            p2 = mm(ux, utx)
            keep(s + 3, utx)
            add(0, s - 1, mm(p2, uxt, db=True))
            if s == 1:
                keep(6, p2)

    def tx_lower(w):
        cx_re, cx_im = unpacked(CH[w, 1])
        far_re, far_im = unpacked(CH[w, 4])
        cx = (cx_re, cx_im)
        cxt = tuple(
            jnp.where(row4 == 0, sroll(v, -1), sroll(f, 1)) for v, f in ((cx_re, far_re), (cx_im, far_im))
        )
        ct = unpacked(CH[w, 0])
        lower_c = mm(cx, mm(ct, cxt), da=True)
        for s in range(2):
            add(0, s, x_prev(ld(KT, 2 + s), lower_c, s))

    def tx_side(w):
        for s in range(2):
            add(1, s, mm(ld(KT, s), ld(KT, 4 + s), db=True))
        add(1, 1, mm(ld(U, w, 1, 0), ld(KT, 6), da=True))

    def tx_before(w):
        ut = ld(U, w, 0, 0)
        p2 = mm(ld(U, w, 0, 1), x_next(ut, XH[w, 1], 1))
        add(1, 0, mm(ut, p2, da=True))

    def plane_x(w, m):
        cx, cm = unpacked(CH[w, 1]), unpacked(CH[w, m])
        lower_c = mm(cx, mm(cm, yz_shift(cx, m, 1)), da=True)
        for s in (1, 2):
            ux, um = ld(U, w, s, 1), ld(U, w, s, m)
            umx = x_next(um, XH[w, m], s - 1)
            uxm = yz_shift(ux, m, 1)
            p1, p2 = mm(ux, umx), ld(KT, 5 + 2 * m + s)
            add(1, s - 1, mm(p2, umx, db=True))
            add(m, s - 1, mm(p1, uxm, db=True))
            add(1, s - 1, yz_shift(mm(um, p1, da=True), m, -1))
            add(m, s - 1, x_prev(ld(KT, 9 + 2 * m + s), lower_c, s - 1))

    def unitarise(w, m):
        scale = ape_weight / 6.0
        for s in range(2):
            re = [[acc[m, s, 0, i, j] for j in range(3)] for i in range(3)]
            im = [[acc[m, s, 1, i, j] for j in range(3)] for i in range(3)]

            def diag(j):
                t = None
                for i in range(3):
                    q = re[i][j] * re[i][j] + im[i][j] * im[i][j]
                    t = q if t is None else t + q
                return t

            def off(j, k):
                a = b = None
                for i in range(3):
                    x = re[i][j] * re[i][k] + im[i][j] * im[i][k]
                    y = re[i][j] * im[i][k] - im[i][j] * re[i][k]
                    a = x if a is None else a + x
                    b = y if b is None else b + y
                return a, b

            k1, k2, k3 = diag(0), diag(1), diag(2)
            inverse = jnp.minimum(lax.rsqrt((scale * scale) * (k1 + k2 + k3)), 1.0)
            r = scale * inverse
            g = r * r
            a1, a2, a3 = g * k1, g * k2, g * k3
            b12 = tuple(g * v for v in off(0, 1))
            b13 = tuple(g * v for v in off(0, 2))
            b23 = tuple(g * v for v in off(1, 2))

            def norm(v):
                return v[0] * v[0] + v[1] * v[1]

            def times(a, b):
                return a[0] * b[0] - a[1] * b[1], a[0] * b[1] + a[1] * b[0]

            def ctimes(a, b):
                return a[0] * b[0] + a[1] * b[1], a[1] * b[0] - a[0] * b[1]

            j1 = a2 * a3 - norm(b23)
            j2 = a1 * a3 - norm(b13)
            j3 = a1 * a2 - norm(b12)
            q = ctimes(b13, b23)
            j12 = (q[0] - a3 * b12[0], q[1] - a3 * b12[1])
            q = times(b12, b23)
            j13 = (q[0] - a2 * b13[0], q[1] - a2 * b13[1])
            q = ctimes(b13, b12)
            j23 = (q[0] - a1 * b23[0], q[1] - a1 * b23[1])
            e1 = a1 + a2 + a3
            e2 = j1 + j2 + j3
            e3 = (
                a1 * j1
                + (b12[0] * j12[0] + b12[1] * j12[1])
                + (b13[0] * j13[0] + b13[1] * j13[1])
            )

            def reduce(d0, d1, d2, d3, d4):
                d3 = d3 + e1 * d4
                d2 = d2 - e2 * d4 + e1 * d3
                d1 = d1 + e3 * d4 - e2 * d3
                return d0 + e3 * d3, d1, d2

            h = (0.25 * e3, 2.25 - 0.25 * e2, 0.25 * e1 - 1.5)
            p = None
            for k in range(1, NEWTON):
                y = (1.5 - 0.5 * h[0], -0.5 * h[1], -0.5 * h[2])
                if p is None:
                    d3 = -0.5 * y[2]
                    p = (
                        1.5 * y[0] + e3 * d3,
                        1.5 * y[1] - 0.5 * y[0] - e2 * d3,
                        1.5 * y[2] - 0.5 * y[1] + e1 * d3,
                    )
                else:
                    p = reduce(
                        p[0] * y[0],
                        p[0] * y[1] + p[1] * y[0],
                        p[0] * y[2] + p[1] * y[1] + p[2] * y[0],
                        p[1] * y[2] + p[2] * y[1],
                        p[2] * y[2],
                    )
                if k < NEWTON - 1:
                    twice = p[0] + p[0]
                    f = reduce(
                        p[0] * p[0],
                        twice * p[1],
                        twice * p[2] + p[1] * p[1],
                        (p[1] + p[1]) * p[2],
                        p[2] * p[2],
                    )
                    h = (e3 * f[2], f[0] - e2 * f[2], f[1] + e1 * f[2])

            c2 = r * p[2]
            c1 = r * p[1] + e1 * c2
            c0 = r * p[0] - e2 * c2

            def entry(b, j):
                return c1 * b[0] + c2 * j[0], c1 * b[1] + c2 * j[1]

            m12, m13, m23 = entry(b12, j12), entry(b13, j13), entry(b23, j23)
            dg = [c0 + c1 * a + c2 * j for a, j in ((a1, j1), (a2, j2), (a3, j3))]
            table = {(0, 1): m12, (0, 2): m13, (1, 2): m23}
            for i in range(3):
                for j in range(3):
                    x = re[i][j] * dg[j]
                    y = im[i][j] * dg[j]
                    for k in range(3):
                        if k == j:
                            continue
                        vr, vi = table[(min(k, j), max(k, j))]
                        ur, ui = re[i][k], im[i][k]
                        if k < j:
                            x = x + ur * vr - ui * vi
                            y = y + ur * vi + ui * vr
                        else:
                            x = x + ur * vr + ui * vi
                            y = y - ur * vi + ui * vr
                    U[w + 1, 1 + s, m, 0, i, j] = x
                    U[w + 1, 1 + s, m, 1, i, j] = y
        for s in range(2):
            acc[m, s] = 9.0 * U[w + 1, 1 + s, m]

    sub = lax.broadcasted_iota(jnp.int32, (3, 3, 8, LANES), 2)
    eye = (
        lax.broadcasted_iota(jnp.int32, (3, 3, 8, LANES), 0)
        == lax.broadcasted_iota(jnp.int32, (3, 3, 8, LANES), 1)
    ).astype(jnp.float32)
    one = (eye, jnp.zeros_like(eye))
    lower = core == 0
    sibling = dev(1 - 2 * core, 0)

    def pick(cond, a, b):
        return tuple(jnp.where(cond, x, y) for x, y in zip(a, b))

    def chain_copy(slot, src, dst, d):
        return pltpu.make_async_remote_copy(
            src_ref=src,
            dst_ref=dst,
            send_sem=cs.at[slot],
            recv_sem=cr.at[slot],
            device_id=d,
            device_id_type=MESH,
        )

    def rows(ref, first, count):
        return ref.at[:, :, :, pl.ds(first, count), :]

    def to_sibling():
        return chain_copy(0, Q.at[0], SQ, sibling)

    def half_to(k):
        return chain_copy(k, rows(Q.at[1], 0, 4), rows(CQ.at[k - 1], 0, 4), dev(2 * k, 0))

    def column_to(k, h):
        return chain_copy(
            2 + 2 * k + h, rows(Q.at[2], 4 * h, 1), rows(CQ.at[k - 1], 4 + h, 1), dev(2 * k, -1)
        )

    def column_own(h):
        return chain_copy(10 + h, rows(Q.at[0], 4 * h, 1), rows(XQ, 4 * h + 3, 1), dev(1, -1))

    def entering_to_sibling():
        return chain_copy(12, rows(Q.at[3], 0, 4), rows(EH, 4, 4), sibling)

    def chain_start():
        q = mm(ld(U, 2, 1, 0), ld(U, 2, 2, 0))
        Q[0, 0] = q[0]
        Q[0, 1] = q[1]
        to_sibling().start()

        @pl.when(lower)
        def _():
            for h in range(2):
                column_own(h).start()

    def chain_middle():
        to_sibling().wait_recv()
        mine, other = ld(Q, 0), (SQ[0], SQ[1])
        q = mm(pick(lower, mine, other), pick(lower, other, mine))
        for c in range(2):
            Q[2, c] = q[c]
            Q[1, c] = jnp.where(lower, q[c], sroll(q[c], 4))
        for k in (2, 3, 1):

            @pl.when(chip + k < 4)
            def _():
                half_to(k).start()

        for k in (2, 3, 1):

            @pl.when(chip + k < 4)
            def _():
                for h in range(2):
                    column_to(k, h).start()

    def sweep_start(w):
        plane_yz(w)
        for m in (2, 3):
            plane_t(w, m, 1)
            local_t(w, m)
        tx_local(w, 1)
        for m in (2, 3):
            local_x(w, m)

    def sweep_time(w):
        for m in (2, 3):
            plane_t(w, m, 2)
            plane_t_before(w, m)

    def wait_time(w):
        for m in range(4):
            up(w, m).wait_recv()
            if m != 0:
                down(w, m).wait_recv()

    sweep_start(0)
    first_down().wait_recv()
    then_right().start()
    first_up().wait_recv()
    then_left().start()
    right_xyz().wait_recv()
    left_yz().wait_recv()
    third_cols(CH, 1)
    for m in (2, 3):
        third_cols(CH, m)
        third_cols(XH, m)
        plane_x(0, m)

    up_all().wait_recv()
    down_all().wait_recv()
    for m in range(4):
        third_face(0, m)
        if m != 0:
            third_face(3, m)
    sweep_time(0)
    tx_local(0, 2)
    def arrived(m):
        right(1, m).wait_recv()
        if m != 1:
            left(1, m).wait_recv()

    def finish(m):
        unitarise(0, m)
        pack(1, m)
        if m == 1:
            corner_down(1).start()
        right(1, m).start()
        if m != 1:
            left(1, m).start()
        if m == 0:
            corner_up(1).start()
        up(1, m).start()
        if m != 0:
            down(1, m).start()

    finish(2)
    finish(3)
    right(0, 0).wait_recv()
    left(0, 0).wait_recv()
    third_cols(CH, 0)
    third_cols(XH, 0)
    tx_upper(0)
    tx_side(0)
    then_right().wait_recv()
    third_cols(CH, 4)
    tx_lower(0)
    finish(0)
    then_left().wait_recv()
    third_cols(XH, 1)
    tx_before(0)
    finish(1)

    sweep_start(1)
    wait_time(1)
    sweep_time(1)
    tx_local(1, 2)
    arrived(0)
    arrived(1)
    tx_upper(1)
    corner_down(1).wait_recv()
    tx_lower(1)
    unitarise(1, 0)
    chain_start()
    pack(2, 0)
    left(2, 0).start()
    tx_side(1)
    for m in (2, 3):
        arrived(m)
        plane_x(1, m)
    chain_middle()
    corner_up(1).wait_recv()
    tx_before(1)
    for m in (1, 2, 3):
        unitarise(1, m)

    for c in (up_all, down_all, left_yz, right_xyz, first_up, first_down, then_left, then_right):
        c().wait_send()
    right(0, 0).wait_send()
    left(0, 0).wait_send()
    for m in range(4):
        if m != 0:
            down(1, m).wait_send()
        up(1, m).wait_send()
        if m != 1:
            left(1, m).wait_send()
        right(1, m).wait_send()
    corner_up(1).wait_send()
    corner_down(1).wait_send()
    left(2, 0).wait_send()

    for k in (1, 2, 3):

        @pl.when(chip >= k)
        def _():
            half_to(k).wait_recv()
            for h in range(2):
                column_to(k, h).wait_recv()

    run = pick(chip >= 3, ld(CQ, 2), one)
    run = pick(chip >= 2, mm(run, ld(CQ, 1)), one)
    run = pick(chip >= 1, mm(run, ld(CQ, 0)), one)
    for c in range(2):
        Q[3, c] = run[c]
    entering_to_sibling().start()
    gh1 = tuple(jnp.where(sub < 4, sroll(v, -1), sroll(v, 2)) for v in run)

    @pl.when(core == 1)
    def _():
        for h in range(2):
            chain_copy(10 + h, rows(Q.at[0], 4 * h, 1), rows(XQ, 4 * h + 3, 1), dev(1, -1)).wait_recv()

    gh1 = pick(lower, gh1, mm(gh1, (XQ[0], XQ[1])))
    left(2, 0).wait_recv()
    halo = XH[2, 0]
    gh2 = mm(gh1, tuple(sroll(halo, 3 - 2 * q) for q in range(2)))
    entering_to_sibling().wait_recv()
    whole = tuple(jnp.where(sub < 4, v, EH[c]) for c, v in enumerate(run))
    whole = pick(lower, whole, each(lambda v: sroll(v, 4), whole))
    g1 = pick(lower, whole, mm(whole, (SQ[0], SQ[1])))
    g2 = mm(g1, ld(U, 2, 1, 0))
    g3 = mm(g2, ld(U, 2, 2, 0))
    gs = (g1, g2)

    def store(m, s, pair):
        OUT[m, 0, :, :, s] = pair[0]
        OUT[m, 1, :, :, s] = pair[1]

    def save(m, h):
        return pltpu.make_async_copy(
            OUT.at[m, :, :, :, :, pl.ds(4 * h, 4), :],
            o_ref.at[m, :, :, :, :, :, pl.ds(h * LANES, LANES)],
            io.at[4 + 2 * m + h],
        )

    def save_all(m):
        for h in range(2):
            save(m, h).start()

    store(0, 0, mm(g2, g2, db=True))
    store(0, 1, mm(g3, g3, db=True))
    save_all(0)
    for m in (2, 3):
        for s in range(2):
            store(m, s, mm(mm(gs[s], ld(U, 2, 1 + s, m)), yz_shift(gs[s], m, 1), db=True))
        save_all(m)
    for s, gh in ((0, gh1), (1, gh2)):
        gx_next = tuple(jnp.where(row4 == 3, a, sroll(b, -1)) for a, b in zip(gh, gs[s]))
        store(1, s, mm(mm(gs[s], ld(U, 2, 1 + s, 1)), gx_next, db=True))
    save_all(1)

    to_sibling().wait_send()
    entering_to_sibling().wait_send()

    @pl.when(lower)
    def _():
        for h in range(2):
            column_own(h).wait_send()

    for k in (1, 2, 3):

        @pl.when(chip + k < 4)
        def _():
            half_to(k).wait_send()
            for h in range(2):
                column_to(k, h).wait_send()

    for m in range(4):
        for h in range(2):
            save(m, h).wait()


def body(gauge_links):
    field = (2, 3, 3, 8, LANES)
    f32 = jnp.float32
    return pl.pallas_call(
        kernel,
        out_shape=jax.ShapeDtypeStruct(gauge_links.shape, f32),
        in_specs=[pl.BlockSpec(memory_space=pltpu.HBM)],
        out_specs=pl.BlockSpec(memory_space=pl.ANY),
        scratch_shapes=[
            pltpu.VMEM((3, 4, 4) + field, f32),
            pltpu.VMEM((3, 4) + field[1:], f32),
            pltpu.VMEM((2, 5) + field[1:], f32),
            pltpu.VMEM((3, 4) + field[1:], f32),
            pltpu.VMEM((3, 4) + field[1:], f32),
            pltpu.VMEM((2, 2) + field[2:], f32),
            pltpu.VMEM((4, 2) + field, f32),
            pltpu.VMEM((18,) + field, f32),
            pltpu.VMEM((4,) + field, f32),
            pltpu.VMEM(field, f32),
            pltpu.VMEM((3,) + field, f32),
            pltpu.VMEM(field, f32),
            pltpu.VMEM(field, f32),
            pltpu.VMEM((4, 2, 3, 3, 2, 8, LANES), f32),
            pltpu.SemaphoreType.DMA((3, 20)),
            pltpu.SemaphoreType.DMA((3, 20)),
            pltpu.SemaphoreType.DMA((13,)),
            pltpu.SemaphoreType.DMA((13,)),
            pltpu.SemaphoreType.DMA((16,)),
        ],
        compiler_params=pltpu.CompilerParams(
            collective_id=0, has_side_effects=True, vmem_limit_bytes=32 * 2**20
        ),
    )(pltpu.with_memory_space_constraint(gauge_links, pltpu.HBM))


def solution(mesh):
    spec = P(None, None, None, None, "ta", "gx", None)
    return jax.shard_map(body, mesh=mesh, in_specs=(spec,), out_specs=spec, check_vma=False)
```
